32 devices in a mesh: replica: 4 (over x, core), shard: 8 (over z, y).
Axes of the slice: x: 2, y: 2, z: 4, core: 2. Of those that a mesh axis runs over, the one named last changes fastest.
Arguments:
- inputs: bfloat16 [32768, 640], P(('replica', 'shard')), may hold values from -6 to 6
- segment_ids: int32 [32768], P(('replica', 'shard')), may hold values from -1 to 3, as said below
- out_grad: bfloat16 [32768, 640], P(('replica', 'shard')), may hold values from -6 to 6
- w_query: bfloat16 [640, 1024], P('shard'), may hold values from -0.25 to 0.25
- w_key: bfloat16 [640, 256], P('shard'), may hold values from -0.25 to 0.25
- w_value: bfloat16 [640, 256], P('shard'), may hold values from -0.25 to 0.25
- w_out: bfloat16 [1024, 640], P('shard'), may hold values from -0.1875 to 0.1875
- w_gate: bfloat16 [640, 2048], P('shard'), may hold values from -0.25 to 0.25
- w_up: bfloat16 [640, 2048], P('shard'), may hold values from -0.25 to 0.25
- w_down: bfloat16 [2048, 640], P('shard'), may hold values from -0.125 to 0.125
- scale_attn_in: bfloat16 [640], P('shard'), may hold values from 0.5 to 1.5
- scale_query: bfloat16 [256], P('shard'), may hold values from 0.5 to 1.5
- scale_key: bfloat16 [256], P('shard'), may hold values from 0.5 to 1.5
- scale_attn_out: bfloat16 [640], P('shard'), may hold values from 0.5 to 1.5
- scale_mlp_in: bfloat16 [640], P('shard'), may hold values from 0.5 to 1.5
- scale_mlp_out: bfloat16 [640], P('shard'), may hold values from 0.5 to 1.5
Outputs:
- output: bfloat16 [32768, 640], P(('replica', 'shard'))
- input_grad: float32 [32768, 640], P(('replica', 'shard'))
- grad_w_query: float32 [640, 1024], P('shard')
- grad_w_key: float32 [640, 256], P('shard')
- grad_w_value: float32 [640, 256], P('shard')
- grad_w_out: float32 [1024, 640], P('shard')
- grad_w_gate: float32 [640, 2048], P('shard')
- grad_w_up: float32 [640, 2048], P('shard')
- grad_w_down: float32 [2048, 640], P('shard')
- grad_scale_attn_in: float32 [640], P('shard')
- grad_scale_query: float32 [256], P('shard')
- grad_scale_key: float32 [256], P('shard')
- grad_scale_attn_out: float32 [640], P('shard')
- grad_scale_mlp_in: float32 [640], P('shard')
- grad_scale_mlp_out: float32 [640], P('shard')
The draws below stay inside these ranges and needn't reach their ends.
Inputs may be any that keep to these rules, and one draw needn't show every extreme that they name: `segment_ids`: each device's 1024 slots hold whole sequences numbered 0, 1, 2 and so on in order, then padding slots of id -1 to the end; on one device of every draw all 1024 slots are a single sequence, and on another the numbers reach the largest value.
All inputs are finite; a program needn't handle non-finite values.
Results may differ from the reference program's by a relative error of at most 0.019.
Values may be sent and summed in bfloat16 or wider, within the bound.
No kernel may reach another device: no remote copies, remote signals or barrier semaphores. Data moves between devices by JAX's collectives and lax.ppermute only.
A program may use at most 192 MiB of HBM per device.

```python
import jax
import jax.numpy as jnp
from jax import lax

D = 640
HQ = 4
HD = 256
FF = 2048
WINDOW = 512
TOK_DEV = 1024
BLOCK = 512
TOKENS = 32768


def draw_segment_ids(key, part):
    key = jax.random.fold_in(key, 11)
    key_live, key_full, key_cuts = jax.random.split(key, 3)
    rows = TOKENS // TOK_DEV
    most_id = 2 * TOK_DEV // WINDOW - 1
    even_len = TOK_DEV // (most_id + 1)
    live = jax.random.randint(key_live, (rows, 1), TOK_DEV // 4, TOK_DEV + 1)
    full_row = jax.random.randint(key_full, (), 0, rows)
    even_row = (full_row + 1) % rows
    row_index = jnp.arange(rows, dtype=jnp.int32)[:, None]
    live = jnp.where((row_index == full_row) | (row_index == even_row), TOK_DEV, live)
    slot = jnp.arange(TOK_DEV, dtype=jnp.int32)[None, :]
    cuts = jax.random.randint(key_cuts, (rows, TOK_DEV), 0, WINDOW) == 0
    cuts = cuts & (slot > 0) & (row_index != full_row)
    ids = jnp.minimum(jnp.cumsum(cuts.astype(jnp.int32), axis=1).astype(jnp.int32), most_id)
    even_ids = jnp.broadcast_to(slot // even_len, (rows, TOK_DEV)).astype(jnp.int32)
    ids = jnp.where(row_index == even_row, even_ids, ids)
    ids = jnp.where(slot < live, ids, -1)
    return ids.reshape(TOKENS).astype(jnp.int32)


def block_levels(own_key, dims, shards, smallest, high):
    def one(axis_at, parts):
        draws = jax.random.uniform(jax.random.fold_in(jax.random.fold_in(own_key, 6), axis_at), (parts,), jnp.float32, smallest / len(shards), high / len(shards))
        return jnp.repeat(jnp.exp(draws), dims[axis_at] // parts).reshape((-1,) + (1,) * (len(dims) - axis_at - 1))

    level = one(*shards[0])
    for cut in shards[1:]:
        level = level * one(*cut)
    return level


def scatter_about(rng, extent, scale, bound, cuts=(), held_as=jnp.bfloat16):
    array = jax.random.normal(rng, extent, jnp.float32) * scale
    if len(cuts) > 0:
        array = block_levels(rng, extent, cuts, -0.22, 0.18) * array
    return jnp.clip(array, min=-bound, max=bound).astype(held_as)


def setup_inputs(seed: int = 0) -> dict:
    splits = jax.random.split(jax.random.key(seed), 17)
    inputs = scatter_about(splits[0], (TOKENS, D), 1.0, 6.0, ((0, 32),))
    segment_ids = draw_segment_ids(jax.random.fold_in(splits[16], 71), 0)
    out_grad = scatter_about(splits[2], (TOKENS, D), 1.0, 6.0, ((0, 32),))
    w_query = scatter_about(splits[3], (D, HQ * HD), D ** -0.5, 0.25, ((0, 8),))
    w_key = scatter_about(splits[4], (D, HD), D ** -0.5, 0.25, ((0, 8),))
    w_value = scatter_about(splits[5], (D, HD), D ** -0.5, 0.25, ((0, 8),))
    w_out = scatter_about(splits[6], (HQ * HD, D), (HQ * HD) ** -0.5, 0.1875, ((0, 8),))
    w_gate = scatter_about(splits[7], (D, FF), D ** -0.5, 0.25, ((0, 8),))
    w_up = scatter_about(splits[8], (D, FF), D ** -0.5, 0.25, ((0, 8),))
    w_down = scatter_about(splits[9], (FF, D), FF ** -0.5, 0.125, ((0, 8),))
    scale_attn_in = jnp.clip(0.5 + 1.0 * jax.random.uniform(splits[10], (D,), jnp.float32) ** block_levels(splits[10], (D,), ((0, 8),), -0.2, 0.2), 0.5, 1.5).astype(jnp.bfloat16)
    scale_query = jnp.clip(0.5 + 1.0 * jax.random.uniform(splits[11], (HD,), jnp.float32) ** block_levels(splits[11], (HD,), ((0, 8),), -0.2, 0.2), 0.5, 1.5).astype(jnp.bfloat16)
    scale_key = jnp.clip(0.5 + 1.0 * jax.random.uniform(splits[12], (HD,), jnp.float32) ** block_levels(splits[12], (HD,), ((0, 8),), -0.2, 0.2), 0.5, 1.5).astype(jnp.bfloat16)
    scale_attn_out = jnp.clip(0.5 + 1.0 * jax.random.uniform(splits[13], (D,), jnp.float32) ** block_levels(splits[13], (D,), ((0, 8),), -0.2, 0.2), 0.5, 1.5).astype(jnp.bfloat16)
    scale_mlp_in = jnp.clip(0.5 + 1.0 * jax.random.uniform(splits[14], (D,), jnp.float32) ** block_levels(splits[14], (D,), ((0, 8),), -0.2, 0.2), 0.5, 1.5).astype(jnp.bfloat16)
    scale_mlp_out = jnp.clip(0.5 + 1.0 * jax.random.uniform(splits[15], (D,), jnp.float32) ** block_levels(splits[15], (D,), ((0, 8),), -0.2, 0.2), 0.5, 1.5).astype(jnp.bfloat16)
    return dict(inputs=inputs, segment_ids=segment_ids, out_grad=out_grad, w_query=w_query, w_key=w_key, w_value=w_value, w_out=w_out, w_gate=w_gate, w_up=w_up, w_down=w_down, scale_attn_in=scale_attn_in, scale_query=scale_query, scale_key=scale_key, scale_attn_out=scale_attn_out, scale_mlp_in=scale_mlp_in, scale_mlp_out=scale_mlp_out)


EPSILON = 1e-06
HIGHEST = lax.Precision.HIGHEST

@jax.custom_vjp
def low(v):
    return lax.optimization_barrier(v.astype(jnp.bfloat16)).astype(jnp.float32)

@jax.custom_vjp
def low_back(v):
    return v

def low_keep(v):
    return (low(v), None)

def low_pass(kept, grad):
    return (grad,)

def back_keep(v):
    return (v, None)

def back_low(kept, grad):
    return (low(grad),)
low.defvjp(low_keep, low_pass)
low_back.defvjp(back_keep, back_low)

def matmul(left, right):
    return jnp.dot(left, right, precision=HIGHEST, preferred_element_type=jnp.float32)

def rms_scale(value, gain):
    mean_sq = lax.optimization_barrier(jnp.mean(value * value, axis=-1, keepdims=True))
    return value * lax.rsqrt(mean_sq + EPSILON) * gain

def rotate(value, angles):
    half = value.shape[-1] // 2
    first_half, second_half = (value[..., :half], value[..., half:])
    cosine, sine = (jnp.cos(angles), jnp.sin(angles))
    return jnp.concatenate([first_half * cosine - second_half * sine, second_half * cosine + first_half * sine], axis=-1)

def positions(seg):
    length = seg.shape[0]
    index = jnp.arange(length, dtype=jnp.int32)
    previous = jnp.concatenate([jnp.full((1,), -3, jnp.int32), seg[:-1]])
    starts = jnp.where(seg != previous, index, jnp.zeros_like(index))
    return index - lax.cummax(starts, axis=0)

def rope_angles(position, head_dim):
    half = head_dim // 2
    freqs = 10000.0 ** (-2.0 * jnp.arange(half, dtype=jnp.float32) / head_dim)
    return position.astype(jnp.float32)[:, None] * freqs[None, :]

def allowed_pairs(seg_query, seg_keys, rows_query, rows_keys):
    same = (seg_query[:, None] == seg_keys[None, :]) & (seg_query[:, None] >= 0)
    offset = rows_query[:, None] - rows_keys[None, :]
    return same & (offset >= 0) & (offset < WINDOW) | (offset == 0)

def block_attend(item):
    query, keys, values, seg_query, seg_keys, start = item
    head_dim = keys.shape[-1]
    rows_query = start + jnp.arange(BLOCK, dtype=jnp.int32)
    rows_keys = start - BLOCK + jnp.arange(2 * BLOCK, dtype=jnp.int32)
    allowed = allowed_pairs(seg_query, seg_keys, rows_query, rows_keys)
    scores = jnp.einsum('qhd,kd->hqk', query, keys, precision=HIGHEST) * head_dim ** (-0.5)
    scores = low_back(scores)
    scores = jnp.where(allowed[None], scores, -1e+30)
    top = lax.optimization_barrier(jnp.max(scores, axis=-1, keepdims=True))
    expo = jnp.exp(scores - top)
    probs = low(expo / lax.optimization_barrier(jnp.sum(expo, axis=-1, keepdims=True)))
    return jnp.einsum('hqk,kd->qhd', probs, values, precision=HIGHEST)

def windows(blocks_arr, fill):
    previous = jnp.concatenate([jnp.full_like(blocks_arr[:1], fill), blocks_arr[:-1]], axis=0)
    return jnp.concatenate([previous, blocks_arr], axis=1)

def layer_row(params, stream, seg):
    w_query, w_key, w_value, w_out, w_gate, w_up, w_down, scale_attn_in, scale_query, scale_key, scale_attn_out, scale_mlp_in, scale_mlp_out = params
    length = stream.shape[0]
    head_dim = w_key.shape[1]
    heads = w_query.shape[1] // head_dim
    blocks = length // BLOCK
    angles = rope_angles(positions(seg), head_dim)
    normed = low(rms_scale(stream, scale_attn_in))
    query_raw = low_back(matmul(normed, w_query))
    key_raw = low_back(matmul(normed, w_key))
    values = low(low_back(matmul(normed, w_value)))
    queries = low(rotate(rms_scale(query_raw.reshape(length, heads, head_dim), scale_query), angles[:, None, :]))
    keys = low(rotate(rms_scale(key_raw, scale_key), angles))
    query_blocks = queries.reshape(blocks, BLOCK, heads, head_dim)
    key_windows = windows(keys.reshape(blocks, BLOCK, head_dim), 0.0)
    value_windows = windows(values.reshape(blocks, BLOCK, head_dim), 0.0)
    seg_blocks = seg.reshape(blocks, BLOCK)
    seg_windows = windows(seg_blocks, -2)
    starts = jnp.arange(blocks, dtype=jnp.int32) * BLOCK
    mixed = lax.map(jax.checkpoint(block_attend), (query_blocks, key_windows, value_windows, seg_blocks, seg_windows, starts))
    mixed = low(low_back(mixed.reshape(length, heads * head_dim)))
    branch = low_back(matmul(mixed, w_out))
    middle = stream + rms_scale(branch, scale_attn_out)
    inner = low(rms_scale(middle, scale_mlp_in))
    gate = low_back(matmul(inner, w_gate))
    up_proj = low_back(matmul(inner, w_up))
    hidden = low(jax.nn.gelu(gate, approximate=True) * up_proj)
    down = low_back(matmul(hidden, w_down))
    return middle + rms_scale(down, scale_mlp_out)

def reference(inputs, segment_ids, out_grad, w_query, w_key, w_value, w_out, w_gate, w_up, w_down, scale_attn_in, scale_query, scale_key, scale_attn_out, scale_mlp_in, scale_mlp_out):
    rows = TOKENS // TOK_DEV
    width = inputs.shape[1]
    stream_rows = inputs.astype(jnp.float32).reshape(rows, TOK_DEV, width)
    seg_rows = segment_ids.reshape(rows, TOK_DEV)
    params = tuple((p.astype(jnp.float32) for p in (w_query, w_key, w_value, w_out, w_gate, w_up, w_down, scale_attn_in, scale_query, scale_key, scale_attn_out, scale_mlp_in, scale_mlp_out)))

    def forward(stream_all, weights):

        def one_row(item):
            return layer_row(weights, item[0], item[1])
        return lax.map(jax.checkpoint(one_row), (stream_all, seg_rows))
    result, pullback = jax.vjp(forward, stream_rows, params)
    grad_stream, grads = pullback(out_grad.astype(jnp.float32).reshape(rows, TOK_DEV, width))
    return (result.reshape(TOKENS, width).astype(jnp.bfloat16), grad_stream.reshape(TOKENS, width), grads[0], grads[1], grads[2], grads[3], grads[4], grads[5], grads[6], grads[7], grads[8], grads[9], grads[10], grads[11], grads[12])
```

```python
import functools
import math

import jax
import jax.numpy as jnp
from jax import lax
from jax.experimental import pallas as pl
from jax.experimental.pallas import tpu as pltpu
from jax.sharding import PartitionSpec as P

WINDOW = 512
EPSILON = 1e-06
NEG = -1e30
QB = 256
RB = 512
CB = 512
AXES = ("replica", "shard")
F32 = jnp.float32
BF16 = jnp.bfloat16
GELU_C = math.sqrt(2.0 / math.pi)


def flip_pairs(reps, shards, axis, bit):
    pairs = []
    for rep in range(reps):
        for shard in range(shards):
            rep_to = rep ^ bit if axis == "replica" else rep
            shard_to = shard ^ bit if axis == "shard" else shard
            pairs.append((rep * shards + shard, rep_to * shards + shard_to))
    return pairs


class Net:
    def __init__(self, mesh):
        self.reps = mesh.shape["replica"]
        self.shards = mesh.shape["shard"]
        self.shard_bits = [1 << i for i in range(self.shards.bit_length() - 1)]
        self.rep_bits = [1 << i for i in range(self.reps.bit_length() - 1)]
        assert 1 << len(self.shard_bits) == self.shards
        assert self.reps == 4

    def swap(self, value, axis, bit):
        return lax.ppermute(value, AXES, flip_pairs(self.reps, self.shards, axis, bit))

    def gather(self, value, stages):
        for axis, bit in stages:
            value = jnp.concatenate([value, self.swap(value, axis, bit)], axis=0)
        return value

    def scatter(self, value, stages):
        for axis, bit in stages:
            half = value.shape[0] // 2
            got = self.swap(value[half:], axis, bit)
            value = (value[:half].astype(F32) + got.astype(F32)).astype(BF16)
        return value

    def total(self, value, axis, bit):
        return (value.astype(F32) + self.swap(value, axis, bit).astype(F32)).astype(BF16)

    def unflip(self, value, axis, bit, dim):
        got = self.swap(value, axis, bit)
        me = lax.axis_index(axis)
        first = (me & bit) == 0
        return jnp.concatenate(
            [jnp.where(first, value, got), jnp.where(first, got, value)], axis=dim
        )


def places(stages, parts):
    rep = lax.axis_index("replica")
    shard = lax.axis_index("shard")
    shards = 1
    for axis, bit in stages:
        shards *= 2 if axis == "shard" else 1
    count = 1 << len(parts)
    part = jnp.arange(count, dtype=jnp.int32)[:, None]
    block = jnp.arange(shards, dtype=jnp.int32)[None, :]
    part_rep = jnp.zeros_like(part)
    for i, bit in enumerate(parts):
        part_rep = part_rep + ((part >> (len(parts) - 1 - i)) & 1) * bit
    rep_diff = part_rep ^ rep
    shard_diff = block ^ shard
    where = jnp.zeros((count, shards), jnp.int32)
    for axis, bit in stages:
        diff = rep_diff if axis == "replica" else shard_diff
        where = where * 2 + jnp.where((diff & bit) != 0, 1, 0)
    return where.reshape(-1)


def dot(left, right):
    return jnp.dot(left, right, preferred_element_type=F32)


def dot_nt(left, right):
    return lax.dot_general(left, right, (((1,), (1,)), ((), ())), preferred_element_type=F32)


def dot_tn(left, right):
    return lax.dot_general(left, right, (((0,), (0,)), ((), ())), preferred_element_type=F32)


def inv_rms(value):
    return lax.rsqrt(jnp.mean(value * value, axis=-1, keepdims=True) + EPSILON)


def norm_back(grad, unit, inv, gain):
    scaled = grad * gain
    return inv * (scaled - unit * jnp.mean(scaled * unit, axis=-1, keepdims=True))


def rows_of(index, size):
    return pl.ds(pl.multiple_of(index * size, size), size)


def start_all(copies):
    for copy in copies:
        copy.start()


def wait_all(copies):
    for copy in copies:
        copy.wait()


def attn_fwd_kernel(
    cuts_qkv, cuts_out, heads,
    place_qkv, place_out, x_ref, cos_ref, sin_ref, segr_ref, segc_ref,
    gai_ref, gq_ref, gk_ref, gao_ref, gmi_ref, qkv_hbm, out_hbm,
    normed_ref, qraw_ref, kraw_ref, v_ref, q_ref, k_ref, probs_ref, mixed_ref, branch_ref,
    middle_ref, inner_ref,
    wqkv, wout, sem_qkv, sem_out,
):
    length = x_ref.shape[0]
    hd = k_ref.shape[1]
    half = hd // 2
    factor = hd ** (-0.5)
    in_qkv = block_copies(cuts_qkv, place_qkv, qkv_hbm, wqkv, sem_qkv, False)
    in_out = block_copies(cuts_out, place_out, out_hbm, wout, sem_out, False)
    start_all(in_qkv)
    start_all(in_out)
    gain = gai_ref[...]
    for i in range(length // QB):
        rows = slice(i * QB, (i + 1) * QB)
        x = x_ref[rows, :].astype(F32)
        normed_ref[rows, :] = (x * inv_rms(x) * gain).astype(BF16)
    wait_all(in_qkv)

    def turn(value, cos, sin):
        first, second = value[:, :half], value[:, half:]
        return jnp.concatenate([first * cos - second * sin, second * cos + first * sin], axis=1)

    def project(i, carry):
        rows = rows_of(i, QB)
        cos, sin = cos_ref[rows, :], sin_ref[rows, :]
        normed = normed_ref[rows, :]
        for h in range(heads):
            raw = dot(normed, wqkv[:, h * hd : (h + 1) * hd])
            qraw_ref[rows, h * hd : (h + 1) * hd] = raw.astype(BF16)
            turned = turn(raw * inv_rms(raw) * gq_ref[...], cos, sin)
            q_ref[h, rows, :] = (turned * factor).astype(BF16)
        raw = dot(normed, wqkv[:, heads * hd : (heads + 1) * hd])
        kraw_ref[rows, :] = raw.astype(BF16)
        k_ref[rows, :] = turn(raw * inv_rms(raw) * gk_ref[...], cos, sin).astype(BF16)
        v_ref[rows, :] = dot(normed, wqkv[:, (heads + 1) * hd :]).astype(BF16)
        return carry

    lax.fori_loop(0, length // QB, project, 0)

    for b in range(length // QB):
        low = max(0, b - WINDOW // QB) * QB
        high = (b + 1) * QB
        width = high - low
        rows = slice(b * QB, high)
        seg_q, seg_k = segr_ref[rows, :], segc_ref[:, low:high]
        offset = (
            lax.broadcasted_iota(jnp.int32, (QB, width), 0)
            - lax.broadcasted_iota(jnp.int32, (QB, width), 1)
            + (b * QB - low)
        )
        allowed = (seg_q == seg_k) & (seg_q >= 0) & (offset >= 0) & (offset < WINDOW)
        allowed = allowed | (offset == 0)
        keys, vals = k_ref[low:high, :], v_ref[low:high, :]
        for h in range(heads):
            scores = jnp.where(allowed, dot_nt(q_ref[h, rows, :], keys), NEG)
            expo = jnp.exp(scores - jnp.max(scores, axis=1, keepdims=True))
            probs = (expo * (1.0 / jnp.sum(expo, axis=1, keepdims=True))).astype(BF16)
            probs_ref[h, rows, 0:width] = probs
            mixed_ref[rows, h * hd : (h + 1) * hd] = dot(probs, vals).astype(BF16)

    wait_all(in_out)

    def finish(i, carry):
        rows = rows_of(i, QB)
        branch = dot(mixed_ref[rows, :], wout[...])
        branch_ref[rows, :] = branch.astype(BF16)
        middle = x_ref[rows, :].astype(F32) + branch * inv_rms(branch) * gao_ref[...]
        middle_ref[rows, :] = middle
        inner_ref[rows, :] = (middle * inv_rms(middle) * gmi_ref[...]).astype(BF16)
        return carry

    lax.fori_loop(0, length // QB, finish, 0)


def block_copies(cuts, place, hbm, mat, sem, outward):
    made = []
    for n, cut in enumerate(cuts):
        far, near = hbm.at[place[n]], mat.at[cut]
        src, dst = (near, far) if outward else (far, near)
        made.append(pltpu.make_async_copy(src, dst, sem.at[n]))
    return made


def mlp_fwd_kernel(
    cuts_gate, cuts_down, cuts_grad,
    place_gate, place_down, place_grad,
    inner_ref, middle_ref, top_ref, gmo_ref, gate_hbm, down_hbm,
    output_ref, act_ref, slope_ref, ddown_ref, ggain_ref, grad_hbm,
    wgu, wdown, hidden, grad, sem_gate, sem_down, sem_grad,
):
    length = inner_ref.shape[0]
    ff = wdown.shape[0]
    in_gate = block_copies(cuts_gate, place_gate, gate_hbm, wgu, sem_gate, False)
    in_down = block_copies(cuts_down, place_down, down_hbm, wdown, sem_down, False)
    start_all(in_gate)
    start_all(in_down)
    wait_all(in_gate)

    def forward(i, carry):
        rows = rows_of(i, RB)
        inner = inner_ref[rows, :]
        for c in range(ff // CB):
            cols = slice(c * CB, (c + 1) * CB)
            gate = dot(inner, wgu[:, cols])
            up = dot(inner, wgu[:, ff + c * CB : ff + (c + 1) * CB])
            square = gate * gate
            tanh = jnp.tanh(gate * (GELU_C + (GELU_C * 0.044715) * square))
            base = 0.5 + 0.5 * tanh
            act = gate * base
            slope = base + (0.5 * gate) * (1.0 - tanh * tanh) * (
                GELU_C + (3.0 * GELU_C * 0.044715) * square
            )
            hidden[rows, cols] = (act * up).astype(BF16)
            act_ref[rows, cols] = act.astype(BF16)
            slope_ref[rows, cols] = (slope * up).astype(BF16)
        return carry

    lax.fori_loop(0, length // RB, forward, 0)
    wait_all(in_down)
    ggain_ref[...] = jnp.zeros_like(ggain_ref)

    def finish(i, carry):
        rows = rows_of(i, QB)
        down = dot(hidden[rows, :], wdown[...])
        inv = inv_rms(down)
        unit = down * inv
        output_ref[rows, :] = (middle_ref[rows, :] + unit * gmo_ref[...]).astype(BF16)
        top = top_ref[rows, :].astype(F32)
        ddown_ref[rows, :] = norm_back(top, unit, inv, gmo_ref[...]).astype(BF16)
        ggain_ref[...] += jnp.sum(top * unit, axis=0, keepdims=True)
        return carry

    lax.fori_loop(0, length // QB, finish, 0)

    def weights(i, carry):
        cols = rows_of(i, CB)
        grad[cols, :] = dot_tn(hidden[:, cols], ddown_ref[...]).astype(BF16)
        return carry

    lax.fori_loop(0, ff // CB, weights, 0)
    out = block_copies(cuts_grad, place_grad, grad_hbm, grad, sem_grad, True)
    start_all(out)
    wait_all(out)


def mlp_bwd_kernel(
    cuts_gate, cuts_down, cuts_grad,
    place_gate, place_down, place_grad,
    ddown_ref, act_ref, slope_ref, inner_ref, middle_ref, branch_ref, top_ref, gmi_ref, gao_ref,
    gate_hbm, down_hbm,
    dmiddle_ref, dbranch_ref, ggain_ref, grad_hbm,
    wgu, wdown, dgu, grad, sem_gate, sem_down, sem_grad,
):
    length = inner_ref.shape[0]
    ff = wdown.shape[0]
    in_gate = block_copies(cuts_gate, place_gate, gate_hbm, wgu, sem_gate, False)
    in_down = block_copies(cuts_down, place_down, down_hbm, wdown, sem_down, False)
    start_all(in_down)
    start_all(in_gate)
    wait_all(in_down)

    def hidden(i, carry):
        rows = rows_of(i, RB)
        ddown = ddown_ref[rows, :]
        for c in range(ff // CB):
            cols = slice(c * CB, (c + 1) * CB)
            dhid = dot_nt(ddown, wdown[cols, :])
            dgu[rows, cols] = (dhid * slope_ref[rows, cols].astype(F32)).astype(BF16)
            dgu[rows, ff + c * CB : ff + (c + 1) * CB] = (
                dhid * act_ref[rows, cols].astype(F32)
            ).astype(BF16)
        return carry

    lax.fori_loop(0, length // RB, hidden, 0)

    def weights(i, carry):
        cols = rows_of(i, CB)
        grad[:, cols] = dot_tn(inner_ref[...], dgu[:, cols]).astype(BF16)
        return carry

    lax.fori_loop(0, 2 * ff // CB, weights, 0)
    out = block_copies(cuts_grad, place_grad, grad_hbm, grad, sem_grad, True)
    start_all(out)
    wait_all(in_gate)
    ggain_ref[...] = jnp.zeros_like(ggain_ref)

    def finish(i, carry):
        rows = rows_of(i, QB)
        dinner = dot_nt(dgu[rows, :], wgu[...])
        middle = middle_ref[rows, :]
        inv = inv_rms(middle)
        unit = middle * inv
        dmid = top_ref[rows, :].astype(F32) + norm_back(dinner, unit, inv, gmi_ref[...])
        dmiddle_ref[rows, :] = dmid
        ggain_ref[0:1, :] += jnp.sum(dinner * unit, axis=0, keepdims=True)
        branch = branch_ref[rows, :].astype(F32)
        inv = inv_rms(branch)
        unit = branch * inv
        dbranch_ref[rows, :] = norm_back(dmid, unit, inv, gao_ref[...]).astype(BF16)
        ggain_ref[1:2, :] += jnp.sum(dmid * unit, axis=0, keepdims=True)
        return carry

    lax.fori_loop(0, length // QB, finish, 0)
    wait_all(out)


def attn_bwd_kernel(
    cuts_qkv, cuts_out, cuts_gqkv, cuts_gout, heads,
    place_qkv, place_out, place_gqkv, place_gout,
    dbranch_ref, dmiddle_ref, mixed_ref, probs_ref, q_ref, k_ref, v_ref, qraw_ref, kraw_ref,
    normed_ref, x_ref, cos_ref, sin_ref, gai_ref, gq_ref, gk_ref, qkv_hbm, out_hbm,
    dx_ref, ggain_in_ref, ggain_qk_ref, gqkv_hbm, gout_hbm,
    wqkv, wout, dmixed, ds, dq, dk, dv, draw, gqkv, gout, sem_qkv, sem_out, sem_gqkv, sem_gout,
):
    length = x_ref.shape[0]
    hd = k_ref.shape[1]
    half = hd // 2
    factor = hd ** (-0.5)
    in_qkv = block_copies(cuts_qkv, place_qkv, qkv_hbm, wqkv, sem_qkv, False)
    in_out = block_copies(cuts_out, place_out, out_hbm, wout, sem_out, False)
    start_all(in_out)
    start_all(in_qkv)

    def weights_out(i, carry):
        cols = rows_of(i, QB)
        gout[cols, :] = dot_tn(mixed_ref[:, cols], dbranch_ref[...]).astype(BF16)
        return carry

    lax.fori_loop(0, heads * hd // QB, weights_out, 0)
    out_out = block_copies(cuts_gout, place_gout, gout_hbm, gout, sem_gout, True)
    start_all(out_out)
    wait_all(in_out)

    def mixed_back(i, carry):
        rows = rows_of(i, QB)
        for h in range(heads):
            cols = slice(h * hd, (h + 1) * hd)
            dmixed[h, rows, :] = dot_nt(dbranch_ref[rows, :], wout[cols, :]).astype(BF16)
        return carry

    lax.fori_loop(0, length // QB, mixed_back, 0)

    dk[...] = jnp.zeros_like(dk)
    dv[...] = jnp.zeros_like(dv)
    for b in range(length // QB):
        low = max(0, b - WINDOW // QB) * QB
        high = (b + 1) * QB
        width = high - low
        rows = slice(b * QB, high)
        keys, vals = k_ref[low:high, :], v_ref[low:high, :]
        for h in range(heads):
            probs = probs_ref[h, rows, 0:width].astype(F32)
            dprobs = dot_nt(dmixed[h, rows, :], vals)
            inner = jnp.sum(probs * dprobs, axis=1, keepdims=True)
            dscores = (probs * (dprobs - inner)).astype(BF16)
            ds[h, :, 0:width] = dscores
            dq[rows, h * hd : (h + 1) * hd] = dot(dscores, keys) * factor
        dk_add = jnp.zeros((width, hd), F32)
        dv_add = jnp.zeros((width, hd), F32)
        for h in range(heads):
            dk_add += dot_tn(ds[h, :, 0:width], q_ref[h, rows, :])
            dv_add += dot_tn(probs_ref[h, rows, 0:width], dmixed[h, rows, :])
        dk[low:high, :] += dk_add
        dv[low:high, :] += dv_add

    ggain_qk_ref[...] = jnp.zeros_like(ggain_qk_ref)

    def turn_back(value, cos, sin):
        first, second = value[:, :half], value[:, half:]
        return jnp.concatenate([first * cos + second * sin, second * cos - first * sin], axis=1)

    def raw_back(i, carry):
        rows = rows_of(i, QB)
        cos, sin = cos_ref[rows, :], sin_ref[rows, :]
        total = jnp.zeros((1, hd), F32)
        for h in range(heads):
            cols = slice(h * hd, (h + 1) * hd)
            grad = turn_back(dq[rows, cols], cos, sin)
            raw = qraw_ref[rows, cols].astype(F32)
            inv = inv_rms(raw)
            unit = raw * inv
            draw[rows, cols] = norm_back(grad, unit, inv, gq_ref[...]).astype(BF16)
            total += jnp.sum(grad * unit, axis=0, keepdims=True)
        ggain_qk_ref[0:1, :] += total
        grad = turn_back(dk[rows, :], cos, sin)
        raw = kraw_ref[rows, :].astype(F32)
        inv = inv_rms(raw)
        unit = raw * inv
        draw[rows, heads * hd : (heads + 1) * hd] = norm_back(
            grad, unit, inv, gk_ref[...]
        ).astype(BF16)
        ggain_qk_ref[1:2, :] += jnp.sum(grad * unit, axis=0, keepdims=True)
        draw[rows, (heads + 1) * hd :] = dv[rows, :].astype(BF16)
        return carry

    lax.fori_loop(0, length // QB, raw_back, 0)

    def weights(i, carry):
        cols = rows_of(i, QB)
        gqkv[:, cols] = dot_tn(normed_ref[...], draw[:, cols]).astype(BF16)
        return carry

    lax.fori_loop(0, (heads + 2) * hd // QB, weights, 0)
    out_qkv = block_copies(cuts_gqkv, place_gqkv, gqkv_hbm, gqkv, sem_gqkv, True)
    start_all(out_qkv)
    wait_all(in_qkv)
    ggain_in_ref[...] = jnp.zeros_like(ggain_in_ref)

    def finish(i, carry):
        rows = rows_of(i, QB)
        dnormed = dot_nt(draw[rows, :], wqkv[...])
        x = x_ref[rows, :].astype(F32)
        inv = inv_rms(x)
        unit = x * inv
        dx_ref[rows, :] = dmiddle_ref[rows, :] + norm_back(dnormed, unit, inv, gai_ref[...])
        ggain_in_ref[...] += jnp.sum(dnormed * unit, axis=0, keepdims=True)
        return carry

    lax.fori_loop(0, length // QB, finish, 0)
    wait_all(out_out)
    wait_all(out_qkv)


VMEM = pl.BlockSpec(memory_space=pltpu.VMEM)
SMEM = pl.BlockSpec(memory_space=pltpu.SMEM)
ANY = pl.BlockSpec(memory_space=pl.ANY)


def call(kernel, name, operands, outs, scratch, flops):
    total = 0
    for value, _ in list(operands) + list(outs):
        total += math.prod(value.shape) * value.dtype.itemsize
    return pl.pallas_call(
        kernel,
        name=name,
        out_shape=[value for value, _ in outs],
        in_specs=[spec for _, spec in operands],
        out_specs=[spec for _, spec in outs],
        scratch_shapes=scratch,
        compiler_params=pltpu.CompilerParams(vmem_limit_bytes=56 << 20),
        cost_estimate=pl.CostEstimate(
            flops=flops, bytes_accessed=total, transcendentals=0
        ),
    )(*[value for value, _ in operands])


def typed(shape, dtype):
    return jax.ShapeDtypeStruct(shape, dtype)


def positions(seg):
    length = seg.shape[0]
    index = jnp.arange(length, dtype=jnp.int32)
    previous = jnp.concatenate([jnp.full((1,), -3, jnp.int32), seg[:-1]])
    starts = jnp.where(seg != previous, index, jnp.zeros_like(index))
    return index - lax.cummax(starts, axis=0)


def rope_angles(position, head_dim):
    half = head_dim // 2
    freqs = 10000.0 ** (-2.0 * jnp.arange(half, dtype=F32) / head_dim)
    return position.astype(F32)[:, None] * freqs[None, :]


def layer(
    net,
    inputs,
    segment_ids,
    out_grad,
    w_query,
    w_key,
    w_value,
    w_out,
    w_gate,
    w_up,
    w_down,
    scale_attn_in,
    scale_query,
    scale_key,
    scale_attn_out,
    scale_mlp_in,
    scale_mlp_out,
):
    length, width = inputs.shape
    hd = w_key.shape[1]
    heads = w_query.shape[1] // hd
    qkv = (heads + 2) * hd
    ff = w_gate.shape[1]
    shards = net.shards
    rep = lax.axis_index("replica")
    core = rep & 1
    side = (rep >> 1) & 1

    along = [("shard", bit) for bit in reversed(net.shard_bits)]
    over_core, over_side = ("replica", 1), ("replica", 2)

    scales = (scale_attn_in, scale_attn_out, scale_mlp_in, scale_mlp_out, scale_query, scale_key)
    packed = net.gather(jnp.concatenate(scales)[None, None, :], along)[:, 0]
    packed = jnp.take(packed, places(along[::-1], []), axis=0)
    gains, at = [], 0
    for scale in scales:
        size = scale.shape[0]
        gains.append(packed[:, at : at + size].astype(F32).reshape(1, size * shards))
        at += size
    gai, gao, gmi, gmo, gq, gk = gains

    def half_rows(value, index, parts):
        size = value.shape[0] // parts
        return lax.dynamic_slice_in_dim(value, index * size, size, 0)

    def half_cols(value, index, parts):
        size = value.shape[1] // parts
        return lax.dynamic_slice_in_dim(value, index * size, size, 1)

    own_qkv = half_cols(jnp.concatenate([w_query, w_key, w_value], axis=1), core, 2)
    own_out = half_rows(w_out, core, 2)
    own_gate = half_cols(jnp.where(core == 0, w_gate, w_up), side, 2)
    own_down = half_rows(w_down, core, 2)
    path_2 = along + [over_core]
    path_4 = along + [over_side, over_core]
    all_qkv = net.gather(own_qkv[None], path_2)
    all_out = net.gather(own_out[None], path_2)
    all_gate = net.gather(own_gate[None], path_4)
    all_down = net.gather(own_down[None], path_2)
    at_2 = places(path_2[::-1], [1])
    at_4 = places(path_4[::-1], [1, 2])

    def cut_cols(rows, cols, parts):
        r, c = rows // shards, cols // parts
        return [
            (pl.ds(t * r, r), pl.ds(p * c, c)) for p in range(parts) for t in range(shards)
        ]

    def cut_rows(rows, parts):
        r = rows // shards // parts
        return [pl.ds((t * parts + p) * r, r) for p in range(parts) for t in range(shards)]

    def is_direct(rows):
        return rows % 16 == 0

    def weight(buf, place, cuts, by_cols, shape):
        if is_direct(buf.shape[1]):
            return place, buf, cuts
        parts = len(cuts) // shards
        laid = jnp.take(buf, place, axis=0).reshape((parts, shards) + buf.shape[1:])
        order = (1, 2, 0, 3) if by_cols else (1, 0, 2, 3)
        laid = laid.transpose(order).reshape((1,) + shape)
        return jnp.zeros((1,), jnp.int32), laid, [(slice(0, shape[0]), slice(0, shape[1]))]

    shape_qkv, shape_out = (width, qkv), (heads * hd, width)
    shape_gate, shape_down = (width, 2 * ff), (ff, width)
    wq_place, wq_buf, wq_cuts = weight(all_qkv, at_2, cut_cols(width, qkv, 2), True, shape_qkv)
    wo_place, wo_buf, wo_cuts = weight(all_out, at_2, cut_rows(heads * hd, 2), False, shape_out)
    wg_place, wg_buf, wg_cuts = weight(all_gate, at_4, cut_cols(width, 2 * ff, 4), True, shape_gate)
    wd_place, wd_buf, wd_cuts = weight(all_down, at_2, cut_rows(ff, 2), False, shape_down)

    class Grad:
        def __init__(self, stages, parts, cuts, by_cols, shape):
            self.stages, self.shape, self.by_cols = stages, shape, by_cols
            self.parts = len(parts)
            self.where = places(stages, parts)
            count = len(cuts)
            rows = shape[0] // shards if by_cols else shape[0] // count
            cols = shape[1] * shards // count if by_cols else shape[1]
            self.block = (rows, cols)
            self.direct = is_direct(rows)
            if self.direct:
                self.place, self.cuts, self.out = self.where, cuts, (count, rows, cols)
            else:
                self.place = jnp.zeros((1,), jnp.int32)
                self.cuts = [(slice(0, shape[0]), slice(0, shape[1]))]
                self.out = (1,) + shape

        def travel(self, buf):
            if not self.direct:
                count = 1 << self.parts
                if self.by_cols:
                    buf = buf.reshape(shards, self.block[0], count, self.block[1])
                    buf = buf.transpose(2, 0, 1, 3)
                else:
                    buf = buf.reshape(shards, count, self.block[0], self.block[1])
                    buf = buf.transpose(1, 0, 2, 3)
                buf = buf.reshape((count * shards,) + self.block)
                order = jnp.zeros_like(self.where).at[self.where].set(
                    jnp.arange(self.where.shape[0], dtype=jnp.int32)
                )
                buf = jnp.take(buf, order, axis=0)
            return net.scatter(buf, self.stages)[0]

    down_first = [over_core] + [("shard", bit) for bit in net.shard_bits]
    gate_first = [over_core, over_side] + [("shard", bit) for bit in net.shard_bits]
    grad_down = Grad(down_first, [1], cut_rows(ff, 2), False, shape_down)
    grad_gate = Grad(gate_first, [1, 2], cut_cols(width, 2 * ff, 4), True, shape_gate)
    grad_out = Grad(down_first, [1], cut_rows(heads * hd, 2), False, shape_out)
    grad_qkv = Grad(gate_first, [1, 2], cut_cols(width, qkv, 4), True, shape_qkv)

    angles = rope_angles(positions(segment_ids), hd)
    cos, sin = jnp.cos(angles), jnp.sin(angles)
    seg_rows = segment_ids.reshape(length, 1)
    seg_cols = segment_ids.reshape(1, length)
    reach = min(length, WINDOW + QB)
    in_v = lambda *values: [(value, VMEM) for value in values]
    out_v = lambda *types: [(typed(*one), VMEM) for one in types]
    dma = lambda cuts: pltpu.SemaphoreType.DMA((len(cuts),))

    (normed, qraw, kraw, values, queries, keys, probs, mixed, branch, middle, inner) = call(
        functools.partial(attn_fwd_kernel, wq_cuts, wo_cuts, heads),
        "attn_fwd",
        [(wq_place, SMEM), (wo_place, SMEM)]
        + in_v(inputs, cos, sin, seg_rows, seg_cols, gai, gq, gk, gao, gmi)
        + [(wq_buf, ANY), (wo_buf, ANY)],
        out_v(
            ((length, width), BF16),
            ((length, heads * hd), BF16),
            ((length, hd), BF16),
            ((length, hd), BF16),
            ((heads, length, hd), BF16),
            ((length, hd), BF16),
            ((heads, length, reach), BF16),
            ((length, heads * hd), BF16),
            ((length, width), BF16),
            ((length, width), F32),
            ((length, width), BF16),
        ),
        [pltpu.VMEM(shape_qkv, BF16), pltpu.VMEM(shape_out, BF16), dma(wq_cuts), dma(wo_cuts)],
        2 * length * (width * qkv + heads * hd * width + 2 * heads * hd * reach),
    )

    output, act, slope, ddown, ggain_mo, buf_down = call(
        functools.partial(mlp_fwd_kernel, wg_cuts, wd_cuts, grad_down.cuts),
        "mlp_fwd",
        [(wg_place, SMEM), (wd_place, SMEM), (grad_down.place, SMEM)]
        + in_v(inner, middle, out_grad, gmo)
        + [(wg_buf, ANY), (wd_buf, ANY)],
        out_v(
            ((length, width), BF16),
            ((length, ff), BF16),
            ((length, ff), BF16),
            ((length, width), BF16),
            ((1, width), F32),
        )
        + [(typed(grad_down.out, BF16), ANY)],
        [
            pltpu.VMEM(shape_gate, BF16),
            pltpu.VMEM(shape_down, BF16),
            pltpu.VMEM((length, ff), BF16),
            pltpu.VMEM(shape_down, BF16),
            dma(wg_cuts),
            dma(wd_cuts),
            dma(grad_down.cuts),
        ],
        2 * length * width * ff * 4,
    )
    share_down = net.total(grad_down.travel(buf_down), *over_side)

    dmiddle, dbranch, ggain_mid, buf_gate = call(
        functools.partial(mlp_bwd_kernel, wg_cuts, wd_cuts, grad_gate.cuts),
        "mlp_bwd",
        [(wg_place, SMEM), (wd_place, SMEM), (grad_gate.place, SMEM)]
        + in_v(ddown, act, slope, inner, middle, branch, out_grad, gmi, gao)
        + [(wg_buf, ANY), (wd_buf, ANY)],
        out_v(((length, width), F32), ((length, width), BF16), ((2, width), F32))
        + [(typed(grad_gate.out, BF16), ANY)],
        [
            pltpu.VMEM(shape_gate, BF16),
            pltpu.VMEM(shape_down, BF16),
            pltpu.VMEM((length, 2 * ff), BF16),
            pltpu.VMEM(shape_gate, BF16),
            dma(wg_cuts),
            dma(wd_cuts),
            dma(grad_gate.cuts),
        ],
        2 * length * width * ff * 5,
    )
    share_gate = net.unflip(grad_gate.travel(buf_gate), *over_side, 1)

    input_grad, ggain_in, ggain_qk, buf_qkv, buf_out = call(
        functools.partial(
            attn_bwd_kernel, wq_cuts, wo_cuts, grad_qkv.cuts, grad_out.cuts, heads
        ),
        "attn_bwd",
        [(wq_place, SMEM), (wo_place, SMEM), (grad_qkv.place, SMEM), (grad_out.place, SMEM)]
        + in_v(dbranch, dmiddle, mixed, probs, queries, keys, values, qraw, kraw)
        + in_v(normed, inputs, cos, sin, gai, gq, gk)
        + [(wq_buf, ANY), (wo_buf, ANY)],
        out_v(((length, width), F32), ((1, width), F32), ((2, hd), F32))
        + [(typed(grad_qkv.out, BF16), ANY), (typed(grad_out.out, BF16), ANY)],
        [
            pltpu.VMEM(shape_qkv, BF16),
            pltpu.VMEM(shape_out, BF16),
            pltpu.VMEM((heads, length, hd), BF16),
            pltpu.VMEM((heads, QB, reach), BF16),
            pltpu.VMEM((length, heads * hd), F32),
            pltpu.VMEM((length, hd), F32),
            pltpu.VMEM((length, hd), F32),
            pltpu.VMEM((length, qkv), BF16),
            pltpu.VMEM(shape_qkv, BF16),
            pltpu.VMEM(shape_out, BF16),
            dma(wq_cuts),
            dma(wo_cuts),
            dma(grad_qkv.cuts),
            dma(grad_out.cuts),
        ],
        2 * length * (2 * width * qkv + 2 * heads * hd * width + 4 * heads * hd * reach),
    )
    share_out = net.total(grad_out.travel(buf_out), *over_side)
    share_qkv = net.unflip(grad_qkv.travel(buf_qkv), *over_side, 1)

    full_qkv = net.unflip(share_qkv, *over_core, 1).astype(F32)
    full_out = net.unflip(share_out, *over_core, 0).astype(F32)
    full_down = net.unflip(share_down, *over_core, 0).astype(F32)
    other = net.swap(share_gate, *over_core)
    full_gate = jnp.where(core == 0, share_gate, other).astype(F32)
    full_up = jnp.where(core == 0, other, share_gate).astype(F32)

    sums = jnp.concatenate(
        [ggain_in, ggain_mid[1:2], ggain_mid[0:1], ggain_mo, ggain_qk[0:1], ggain_qk[1:2]], axis=1
    )
    sums = sums.reshape(-1, 128)
    for axis, bit in [over_core, over_side] + along:
        sums = sums + net.swap(sums, axis, bit)
    sums = sums.reshape(-1)
    shard = lax.axis_index("shard")
    grads, at = [], 0
    for scale in scales:
        size = scale.shape[0]
        grads.append(lax.dynamic_slice_in_dim(sums, at + shard * size, size, 0))
        at += size * shards
    return (
        output,
        input_grad,
        full_qkv[:, : heads * hd],
        full_qkv[:, heads * hd : (heads + 1) * hd],
        full_qkv[:, (heads + 1) * hd :],
        full_out,
        full_gate,
        full_up,
        full_down,
        grads[0],
        grads[4],
        grads[5],
        grads[1],
        grads[2],
        grads[3],
    )


def solution(mesh):
    rows, vector = P("shard", None), P("shard")
    tokens = P(AXES, None)
    return jax.shard_map(
        functools.partial(layer, Net(mesh)),
        mesh=mesh,
        in_specs=(tokens, P(AXES), tokens) + (rows,) * 7 + (vector,) * 6,
        out_specs=(tokens, tokens) + (rows,) * 7 + (vector,) * 6,
        check_vma=False,
    )
```

```python
import functools
import math

import jax
import jax.numpy as jnp
from jax import lax
from jax.experimental import pallas as pl
from jax.experimental.pallas import tpu as pltpu
from jax.sharding import PartitionSpec as P

WINDOW = 512
EPSILON = 1e-06
NEG = -1e30
QB = 256
RB = 512
CB = 512
AXES = ("replica", "shard")
F32 = jnp.float32
BF16 = jnp.bfloat16
GELU_C = math.sqrt(2.0 / math.pi)


def flip_pairs(reps, shards, axis, bit):
    pairs = []
    for rep in range(reps):
        for shard in range(shards):
            rep_to = rep ^ bit if axis == "replica" else rep
            shard_to = shard ^ bit if axis == "shard" else shard
            pairs.append((rep * shards + shard, rep_to * shards + shard_to))
    return pairs


class Net:
    def __init__(self, mesh):
        self.reps = mesh.shape["replica"]
        self.shards = mesh.shape["shard"]
        self.shard_bits = [1 << i for i in range(self.shards.bit_length() - 1)]
        self.rep_bits = [1 << i for i in range(self.reps.bit_length() - 1)]
        assert 1 << len(self.shard_bits) == self.shards
        assert self.reps == 4

    def swap(self, value, axis, bit):
        return lax.ppermute(value, AXES, flip_pairs(self.reps, self.shards, axis, bit))

    def beside(self, moves, work=None, args=()):
        values = [value for value, _ in moves]
        values, args = lax.optimization_barrier((values, list(args)))
        got = [self.swap(value, *way) for value, (_, way) in zip(values, moves)]
        outs = work(*args) if work is not None else ()
        return lax.optimization_barrier((got, outs))


def add_up(value, got):
    return (value.astype(F32) + got.astype(F32)).astype(BF16)


def in_order(value, got, axis, bit, dim):
    first = (lax.axis_index(axis) & bit) == 0
    return jnp.concatenate([jnp.where(first, value, got), jnp.where(first, got, value)], axis=dim)


class Flow:
    def __init__(self, value, steps):
        self.value = value
        self.steps = list(steps)

    def move(self):
        value = self.value
        if self.steps[0][0] == "halve":
            value = value[value.shape[0] // 2 :]
        return value, self.steps[0][1]

    def take(self, got):
        kind, way = self.steps[0][:2]
        value = self.value
        if kind == "double":
            self.value = jnp.concatenate([value, got], axis=0)
        elif kind == "halve":
            self.value = add_up(value[: value.shape[0] // 2], got)
        elif kind == "sum":
            self.value = add_up(value, got)
        elif kind == "total":
            self.value = value + got
        elif kind == "swap":
            self.got = got
        else:
            self.value = in_order(value, got, *way, self.steps[0][2])
        self.steps = self.steps[1:]


def advance(net, flows, work=None, args=()):
    flows = [flow for flow in flows if flow.steps]
    got, outs = net.beside([flow.move() for flow in flows], work, args)
    for flow, value in zip(flows, got):
        flow.take(value)
    return outs


def finish(net, flows, left=0):
    while any(len(flow.steps) > left for flow in flows):
        advance(net, [flow for flow in flows if len(flow.steps) > left])


def places(stages, parts):
    rep = lax.axis_index("replica")
    shard = lax.axis_index("shard")
    shards = 1
    for axis, bit in stages:
        shards *= 2 if axis == "shard" else 1
    count = 1 << len(parts)
    part = jnp.arange(count, dtype=jnp.int32)[:, None]
    block = jnp.arange(shards, dtype=jnp.int32)[None, :]
    part_rep = jnp.zeros_like(part)
    for i, bit in enumerate(parts):
        part_rep = part_rep + ((part >> (len(parts) - 1 - i)) & 1) * bit
    rep_diff = part_rep ^ rep
    shard_diff = block ^ shard
    where = jnp.zeros((count, shards), jnp.int32)
    for axis, bit in stages:
        diff = rep_diff if axis == "replica" else shard_diff
        where = where * 2 + jnp.where((diff & bit) != 0, 1, 0)
    return where.reshape(-1)


def dot(left, right):
    return jnp.dot(left, right, preferred_element_type=F32)


def dot_nt(left, right):
    return lax.dot_general(left, right, (((1,), (1,)), ((), ())), preferred_element_type=F32)


def dot_tn(left, right):
    return lax.dot_general(left, right, (((0,), (0,)), ((), ())), preferred_element_type=F32)


def inv_rms(value):
    return lax.rsqrt(jnp.mean(value * value, axis=-1, keepdims=True) + EPSILON)


def norm_back(grad, unit, inv, gain):
    scaled = grad * gain
    return inv * (scaled - unit * jnp.mean(scaled * unit, axis=-1, keepdims=True))


def rows_of(index, size):
    return pl.ds(pl.multiple_of(index * size, size), size)


def start_all(copies):
    for copy in copies:
        copy.start()


def wait_all(copies):
    for copy in copies:
        copy.wait()


def project_kernel(weight_qkv, heads, *refs):
    refs_qkv, refs = split(refs, len(weight_qkv.specs))
    (
        x_ref, cos_ref, sin_ref, gai_ref, gq_ref, gk_ref,
        normed_ref, qraw_ref, kraw_ref, v_ref, q_ref, k_ref,
        wqkv, sem_qkv,
    ) = refs
    length = x_ref.shape[0]
    hd = k_ref.shape[1]
    half = hd // 2
    factor = hd ** (-0.5)
    in_qkv = weight_qkv.copies(refs_qkv, wqkv, sem_qkv)
    start_all(in_qkv)
    gain = gai_ref[...]
    for i in range(length // QB):
        rows = slice(i * QB, (i + 1) * QB)
        x = x_ref[rows, :].astype(F32)
        normed_ref[rows, :] = (x * inv_rms(x) * gain).astype(BF16)
    wait_all(in_qkv)

    def turn(value, cos, sin):
        first, second = value[:, :half], value[:, half:]
        return jnp.concatenate([first * cos - second * sin, second * cos + first * sin], axis=1)

    def project(i, carry):
        rows = rows_of(i, QB)
        cos, sin = cos_ref[rows, :], sin_ref[rows, :]
        normed = normed_ref[rows, :]
        for h in range(heads):
            raw = dot(normed, wqkv[:, h * hd : (h + 1) * hd])
            qraw_ref[rows, h * hd : (h + 1) * hd] = raw.astype(BF16)
            turned = turn(raw * inv_rms(raw) * gq_ref[...], cos, sin)
            q_ref[h, rows, :] = (turned * factor).astype(BF16)
        raw = dot(normed, wqkv[:, heads * hd : (heads + 1) * hd])
        kraw_ref[rows, :] = raw.astype(BF16)
        k_ref[rows, :] = turn(raw * inv_rms(raw) * gk_ref[...], cos, sin).astype(BF16)
        v_ref[rows, :] = dot(normed, wqkv[:, (heads + 1) * hd :]).astype(BF16)
        return carry

    lax.fori_loop(0, length // QB, project, 0)


def attend_kernel(
    segr_ref, segc_ref, q_ref, k_ref, v_ref, probs_hbm, mixed_ref, probs_all, sem_probs
):
    heads, length, hd = q_ref.shape
    out_probs = probs_copies(probs_hbm, probs_all, sem_probs, True)
    for b in range(length // QB):
        low, high = key_range(b)
        width = high - low
        rows = slice(b * QB, high)
        seg_q, seg_k = segr_ref[rows, :], segc_ref[:, low:high]
        offset = (
            lax.broadcasted_iota(jnp.int32, (QB, width), 0)
            - lax.broadcasted_iota(jnp.int32, (QB, width), 1)
            + (b * QB - low)
        )
        allowed = (seg_q == seg_k) & (seg_q >= 0) & (offset >= 0) & (offset < WINDOW)
        allowed = allowed | (offset == 0)
        keys, vals = k_ref[low:high, :], v_ref[low:high, :]
        for h in range(heads):
            scores = jnp.where(allowed, dot_nt(q_ref[h, rows, :], keys), NEG)
            expo = jnp.exp(scores - jnp.max(scores, axis=1, keepdims=True))
            probs = (expo * (1.0 / jnp.sum(expo, axis=1, keepdims=True))).astype(BF16)
            probs_all[h, rows, 0:width] = probs
            mixed_ref[rows, h * hd : (h + 1) * hd] = dot(probs, vals).astype(BF16)
        out_probs[b].start()
    wait_all(out_probs)


def block_copies(cuts, place, hbm, mat, sem, outward):
    made = []
    for n, cut in enumerate(cuts):
        far, near = hbm.at[place[n]], mat.at[cut]
        src, dst = (near, far) if outward else (far, near)
        made.append(pltpu.make_async_copy(src, dst, sem.at[n]))
    return made


class Weight:
    def __init__(self, shape, matrix=None, core=None, pieces=()):
        self.shape = shape
        self.cuts = [cuts for _, cuts, _, _ in pieces]
        if matrix is not None:
            self.operands, self.specs, count = [matrix], [ANY], 1
        else:
            self.operands, self.specs, count = [core], [SMEM], 0
            for place, cuts, own, got in pieces:
                self.operands += [place, own, got]
                self.specs += [SMEM, ANY, ANY]
                count += 2 * len(cuts)
        self.scratch = [pltpu.VMEM(shape, BF16), pltpu.SemaphoreType.DMA((count,))]

    def copies(self, refs, mat, sem):
        if not self.cuts:
            return [pltpu.make_async_copy(refs[0], mat, sem.at[0])]
        core, made = refs[0][0], []
        for piece, cuts in enumerate(self.cuts):
            place, own, got = refs[3 * piece + 1 : 3 * piece + 4]
            for n, (rows, cols, step) in enumerate(cuts):
                for hbm, which in ((own, core), (got, 1 - core)):
                    first = pl.multiple_of(cols[0] + which * step, 128)
                    at = (pl.ds(*rows), pl.ds(first, cols[1]))
                    made.append(
                        pltpu.make_async_copy(hbm.at[place[n]], mat.at[at], sem.at[len(made)])
                    )
        return made


def split(refs, *counts):
    parts, at = [], 0
    for count in counts:
        parts.append(refs[at : at + count])
        at += count
    return parts + [refs[at:]]


def gate_kernel(weight_out, weight_gate, *refs):
    refs_out, refs_gate, refs = split(refs, len(weight_out.specs), len(weight_gate.specs))
    (
        mixed_ref, x_ref, gao_ref, gmi_ref,
        branch_ref, middle_ref, inner_ref, hidden_hbm, act_hbm, slope_hbm,
        wout, sem_out, wgu, sem_gate, hidden, act_all, slope_all, sem,
    ) = refs
    length = inner_ref.shape[0]
    ff = hidden.shape[1]
    in_out = weight_out.copies(refs_out, wout, sem_out)
    in_gate = weight_gate.copies(refs_gate, wgu, sem_gate)
    start_all(in_out)
    start_all(in_gate)
    wait_all(in_out)

    def attn_out(i, carry):
        rows = rows_of(i, QB)
        branch = dot(mixed_ref[rows, :], wout[...])
        branch_ref[rows, :] = branch.astype(BF16)
        middle = x_ref[rows, :].astype(F32) + branch * inv_rms(branch) * gao_ref[...]
        middle_ref[rows, :] = middle
        inner_ref[rows, :] = (middle * inv_rms(middle) * gmi_ref[...]).astype(BF16)
        return carry

    lax.fori_loop(0, length // QB, attn_out, 0)
    wait_all(in_gate)

    def forward(i, carry):
        rows = rows_of(i, RB)
        inner = inner_ref[rows, :]
        for c in range(ff // CB):
            cols = slice(c * CB, (c + 1) * CB)
            gate = dot(inner, wgu[:, cols])
            up = dot(inner, wgu[:, ff + c * CB : ff + (c + 1) * CB])
            square = gate * gate
            tanh = jnp.tanh(gate * (GELU_C + (GELU_C * 0.044715) * square))
            base = 0.5 + 0.5 * tanh
            act = gate * base
            slope = base + (0.5 * gate) * (1.0 - tanh * tanh) * (
                GELU_C + (3.0 * GELU_C * 0.044715) * square
            )
            hidden[rows, cols] = (act * up).astype(BF16)
            act_all[rows, cols] = act.astype(BF16)
            slope_all[rows, cols] = (slope * up).astype(BF16)
        return carry

    outs = []
    for i in range(length // RB):
        forward(i, 0)
        rows = slice(i * RB, (i + 1) * RB)
        for n, (near, far) in enumerate(
            ((hidden, hidden_hbm), (act_all, act_hbm), (slope_all, slope_hbm))
        ):
            copy = pltpu.make_async_copy(near.at[rows, :], far.at[rows, :], sem.at[3 * i + n])
            copy.start()
            outs.append(copy)
    wait_all(outs)


def mlp_kernel(weight_down, weight_gate, cuts_gdown, cuts_ggate, *refs):
    refs_down, refs_gate, refs = split(refs, len(weight_down.specs), len(weight_gate.specs))
    (
        place_gdown, place_ggate,
        middle_ref, branch_ref, inner_ref, top_ref, gmo_ref, gmi_ref, gao_ref,
        hidden_hbm, act_hbm, slope_hbm,
        output_ref, dmiddle_ref, dbranch_ref, ggain_ref, gdown_hbm, ggate_hbm,
        wdown, sem_down, wgu, sem_gate, hidden, dgu, ddown, gdown, ggate, sem, sem_gd, sem_gg,
    ) = refs
    length, ff = hidden.shape
    in_hidden = [pltpu.make_async_copy(hidden_hbm, hidden, sem.at[0])]
    in_down = weight_down.copies(refs_down, wdown, sem_down)
    in_slope = [
        pltpu.make_async_copy(slope_hbm, dgu.at[:, 0:ff], sem.at[1]),
        pltpu.make_async_copy(act_hbm, dgu.at[:, ff : 2 * ff], sem.at[2]),
    ]
    in_gate = weight_gate.copies(refs_gate, wgu, sem_gate)
    start_all(in_hidden)
    start_all(in_down)
    start_all(in_slope)
    start_all(in_gate)
    ggain_ref[...] = jnp.zeros_like(ggain_ref)
    wait_all(in_hidden)
    wait_all(in_down)

    def down_row(i, carry):
        rows = rows_of(i, QB)
        down = dot(hidden[rows, :], wdown[...])
        inv = inv_rms(down)
        unit = down * inv
        output_ref[rows, :] = (middle_ref[rows, :] + unit * gmo_ref[...]).astype(BF16)
        top = top_ref[rows, :].astype(F32)
        ddown[rows, :] = norm_back(top, unit, inv, gmo_ref[...]).astype(BF16)
        ggain_ref[0:1, :] += jnp.sum(top * unit, axis=0, keepdims=True)
        return carry

    lax.fori_loop(0, length // QB, down_row, 0)

    def down_grad(i, carry):
        cols = rows_of(i, CB)
        gdown[cols, :] = dot_tn(hidden[:, cols], ddown[...]).astype(BF16)
        return carry

    lax.fori_loop(0, ff // CB, down_grad, 0)
    out_down = block_copies(cuts_gdown, place_gdown, gdown_hbm, gdown, sem_gd, True)
    start_all(out_down)
    wait_all(in_slope)

    def hidden_back(i, carry):
        rows = rows_of(i, RB)
        grad = ddown[rows, :]
        for c in range(ff // CB):
            cols = slice(c * CB, (c + 1) * CB)
            more = slice(ff + c * CB, ff + (c + 1) * CB)
            dhid = dot_nt(grad, wdown[cols, :])
            dgu[rows, cols] = (dhid * dgu[rows, cols].astype(F32)).astype(BF16)
            dgu[rows, more] = (dhid * dgu[rows, more].astype(F32)).astype(BF16)
        return carry

    lax.fori_loop(0, length // RB, hidden_back, 0)

    def gate_grad(i, carry):
        cols = rows_of(i, CB)
        ggate[:, cols] = dot_tn(inner_ref[...], dgu[:, cols]).astype(BF16)
        return carry

    lax.fori_loop(0, 2 * ff // CB, gate_grad, 0)
    out_gate = block_copies(cuts_ggate, place_ggate, ggate_hbm, ggate, sem_gg, True)
    start_all(out_gate)
    wait_all(in_gate)

    def inner_back(i, carry):
        rows = rows_of(i, QB)
        dinner = dot_nt(dgu[rows, :], wgu[...])
        middle = middle_ref[rows, :]
        inv = inv_rms(middle)
        unit = middle * inv
        dmid = top_ref[rows, :].astype(F32) + norm_back(dinner, unit, inv, gmi_ref[...])
        dmiddle_ref[rows, :] = dmid
        ggain_ref[1:2, :] += jnp.sum(dinner * unit, axis=0, keepdims=True)
        branch = branch_ref[rows, :].astype(F32)
        inv = inv_rms(branch)
        unit = branch * inv
        dbranch_ref[rows, :] = norm_back(dmid, unit, inv, gao_ref[...]).astype(BF16)
        ggain_ref[2:3, :] += jnp.sum(dmid * unit, axis=0, keepdims=True)
        return carry

    lax.fori_loop(0, length // QB, inner_back, 0)
    wait_all(out_down)
    wait_all(out_gate)


def out_bwd_kernel(weight_out, cuts_gout, heads, *refs):
    refs_out, refs = split(refs, len(weight_out.specs))
    (
        place_gout, dbranch_ref, mixed_ref, dmixed_ref, gout_hbm, wout, sem_out, gout, sem_gout
    ) = refs
    length = mixed_ref.shape[0]
    hd = dmixed_ref.shape[2]
    in_out = weight_out.copies(refs_out, wout, sem_out)
    start_all(in_out)

    def weights_out(i, carry):
        cols = rows_of(i, QB)
        gout[cols, :] = dot_tn(mixed_ref[:, cols], dbranch_ref[...]).astype(BF16)
        return carry

    lax.fori_loop(0, heads * hd // QB, weights_out, 0)
    out_out = block_copies(cuts_gout, place_gout, gout_hbm, gout, sem_gout, True)
    start_all(out_out)
    wait_all(in_out)

    def mixed_back(i, carry):
        rows = rows_of(i, QB)
        for h in range(heads):
            cols = slice(h * hd, (h + 1) * hd)
            dmixed_ref[h, rows, :] = dot_nt(dbranch_ref[rows, :], wout[cols, :]).astype(BF16)
        return carry

    lax.fori_loop(0, length // QB, mixed_back, 0)
    wait_all(out_out)


def turn_back(value, cos, sin):
    half = value.shape[1] // 2
    first, second = value[:, :half], value[:, half:]
    return jnp.concatenate([first * cos + second * sin, second * cos - first * sin], axis=1)


def key_range(b):
    return max(0, b - WINDOW // QB) * QB, (b + 1) * QB


def probs_copies(probs_hbm, probs, sem, outward):
    made = []
    for b in range(probs.shape[1] // QB):
        low, high = key_range(b)
        at = (slice(None), slice(b * QB, high), slice(0, high - low))
        far, near = probs_hbm.at[at], probs.at[at]
        src, dst = (near, far) if outward else (far, near)
        made.append(pltpu.make_async_copy(src, dst, sem.at[b]))
    return made


def attn_bwd_kernel(cuts_gqkv, *refs):
    (
        place_gqkv, dmixed_ref, q_ref, k_ref, v_ref, qraw_ref, kraw_ref, normed_ref,
        cos_ref, sin_ref, gq_ref, gk_ref, probs_hbm,
        draw_ref, ggain_ref, gqkv_hbm,
        probs_all, sem_probs, ds, dq, dk, dv, gqkv, sem_gqkv,
    ) = refs
    heads, length, hd = q_ref.shape
    factor = hd ** (-0.5)
    in_probs = probs_copies(probs_hbm, probs_all, sem_probs, False)
    start_all(in_probs)
    dk[...] = jnp.zeros_like(dk)
    dv[...] = jnp.zeros_like(dv)
    for b in range(length // QB):
        low, high = key_range(b)
        width = high - low
        rows = slice(b * QB, high)
        in_probs[b].wait()
        keys, vals = k_ref[low:high, :], v_ref[low:high, :]
        for h in range(heads):
            probs = probs_all[h, rows, 0:width].astype(F32)
            dprobs = dot_nt(dmixed_ref[h, rows, :], vals)
            inner = jnp.sum(probs * dprobs, axis=1, keepdims=True)
            dscores = (probs * (dprobs - inner)).astype(BF16)
            ds[h, :, 0:width] = dscores
            dq[rows, h * hd : (h + 1) * hd] = dot(dscores, keys) * factor
        dk_add = jnp.zeros((width, hd), F32)
        dv_add = jnp.zeros((width, hd), F32)
        for h in range(heads):
            dk_add += dot_tn(ds[h, :, 0:width], q_ref[h, rows, :])
            dv_add += dot_tn(probs_all[h, rows, 0:width], dmixed_ref[h, rows, :])
        dk[low:high, :] += dk_add
        dv[low:high, :] += dv_add

    ggain_ref[...] = jnp.zeros_like(ggain_ref)

    def raw_back(i, carry):
        rows = rows_of(i, QB)
        cos, sin = cos_ref[rows, :], sin_ref[rows, :]
        total = jnp.zeros((1, hd), F32)
        for h in range(heads):
            cols = slice(h * hd, (h + 1) * hd)
            grad = turn_back(dq[rows, cols], cos, sin)
            raw = qraw_ref[rows, cols].astype(F32)
            inv = inv_rms(raw)
            unit = raw * inv
            draw_ref[rows, cols] = norm_back(grad, unit, inv, gq_ref[...]).astype(BF16)
            total += jnp.sum(grad * unit, axis=0, keepdims=True)
        ggain_ref[0:1, :] += total
        grad = turn_back(dk[rows, :], cos, sin)
        raw = kraw_ref[rows, :].astype(F32)
        inv = inv_rms(raw)
        unit = raw * inv
        draw_ref[rows, heads * hd : (heads + 1) * hd] = norm_back(
            grad, unit, inv, gk_ref[...]
        ).astype(BF16)
        ggain_ref[1:2, :] += jnp.sum(grad * unit, axis=0, keepdims=True)
        draw_ref[rows, (heads + 1) * hd :] = dv[rows, :].astype(BF16)
        return carry

    lax.fori_loop(0, length // QB, raw_back, 0)

    def weights(i, carry):
        cols = rows_of(i, QB)
        gqkv[:, cols] = dot_tn(normed_ref[...], draw_ref[:, cols]).astype(BF16)
        return carry

    lax.fori_loop(0, gqkv.shape[1] // QB, weights, 0)
    out_qkv = block_copies(cuts_gqkv, place_gqkv, gqkv_hbm, gqkv, sem_gqkv, True)
    start_all(out_qkv)
    wait_all(out_qkv)


def input_bwd_kernel(weight_qkv, *refs):
    refs_qkv, refs = split(refs, len(weight_qkv.specs))
    draw_ref, dmiddle_ref, x_ref, gai_ref, dx_ref, ggain_ref, wqkv, sem_qkv = refs
    in_qkv = weight_qkv.copies(refs_qkv, wqkv, sem_qkv)
    start_all(in_qkv)
    wait_all(in_qkv)
    ggain_ref[...] = jnp.zeros_like(ggain_ref)

    def finish(i, carry):
        rows = rows_of(i, QB)
        dnormed = dot_nt(draw_ref[rows, :], wqkv[...])
        x = x_ref[rows, :].astype(F32)
        inv = inv_rms(x)
        unit = x * inv
        dx_ref[rows, :] = dmiddle_ref[rows, :] + norm_back(dnormed, unit, inv, gai_ref[...])
        ggain_ref[...] += jnp.sum(dnormed * unit, axis=0, keepdims=True)
        return carry

    lax.fori_loop(0, x_ref.shape[0] // QB, finish, 0)


VMEM = pl.BlockSpec(memory_space=pltpu.VMEM)
SMEM = pl.BlockSpec(memory_space=pltpu.SMEM)
ANY = pl.BlockSpec(memory_space=pl.ANY)


def kernel_of(body, name, in_specs, outs, scratch, flops, **more):
    def run(*operands):
        total = 0
        for value in list(operands) + [value for value, _ in outs]:
            total += math.prod(value.shape) * value.dtype.itemsize
        return pl.pallas_call(
            body,
            name=name,
            out_shape=[value for value, _ in outs],
            in_specs=in_specs,
            out_specs=[spec for _, spec in outs],
            scratch_shapes=scratch,
            compiler_params=pltpu.CompilerParams(vmem_limit_bytes=56 << 20),
            cost_estimate=pl.CostEstimate(flops=flops, bytes_accessed=total, transcendentals=0),
            **more,
        )(*operands)

    return run


def typed(shape, dtype):
    return jax.ShapeDtypeStruct(shape, dtype)


def positions(seg):
    length = seg.shape[0]
    index = jnp.arange(length, dtype=jnp.int32)
    previous = jnp.concatenate([jnp.full((1,), -3, jnp.int32), seg[:-1]])
    starts = jnp.where(seg != previous, index, jnp.zeros_like(index))
    return index - lax.cummax(starts, axis=0)


def rope_angles(position, head_dim):
    half = head_dim // 2
    freqs = 10000.0 ** (-2.0 * jnp.arange(half, dtype=F32) / head_dim)
    return position.astype(F32)[:, None] * freqs[None, :]


def layer(
    net,
    inputs,
    segment_ids,
    out_grad,
    w_query,
    w_key,
    w_value,
    w_out,
    w_gate,
    w_up,
    w_down,
    scale_attn_in,
    scale_query,
    scale_key,
    scale_attn_out,
    scale_mlp_in,
    scale_mlp_out,
):
    length, width = inputs.shape
    hd = w_key.shape[1]
    heads = w_query.shape[1] // hd
    qkv = (heads + 2) * hd
    ff = w_gate.shape[1]
    shards = net.shards
    rep = lax.axis_index("replica")
    core = rep & 1
    side = (rep >> 1) & 1

    along = [("shard", bit) for bit in reversed(net.shard_bits)]
    over_core, over_side = ("replica", 1), ("replica", 2)
    doubles = lambda ways: [("double", way) for way in ways]

    def half_rows(value, index, parts):
        size = value.shape[0] // parts
        return lax.dynamic_slice_in_dim(value, index * size, size, 0)

    def half_cols(value, index, parts):
        size = value.shape[1] // parts
        return lax.dynamic_slice_in_dim(value, index * size, size, 1)

    path_left = along + [over_side]
    path_right = along[:-1] + [over_side, along[-1]]
    scales = (scale_attn_in, scale_attn_out, scale_mlp_in, scale_mlp_out, scale_query, scale_key)
    shape_qkv, shape_out = (width, qkv), (heads * hd, width)
    shape_gate, shape_down = (width, 2 * ff), (ff, width)
    last = [("swap", over_core)]

    flow_qkv = Flow(
        half_cols(jnp.concatenate([w_query, w_key, w_value], axis=1), core, 2)[None],
        doubles(along) + last,
    )
    angles = rope_angles(positions(segment_ids), hd)

    def prepare(w_gate, w_up, angles, *scales):
        own = half_cols(jnp.where(core == 0, w_gate, w_up), side, 2)[None]
        lanes = [jnp.pad(scale, (0, -scale.shape[0] % 128)).reshape(1, -1) for scale in scales]
        return own, jnp.concatenate(lanes, axis=1)[None], jnp.cos(angles), jnp.sin(angles)

    own_gate, own_gains, cos, sin = advance(
        net, [flow_qkv], prepare, [w_gate, w_up, angles, *scales]
    )
    flow_gate = Flow(own_gate, doubles(along[:-1]))
    flow_gains = Flow(own_gains, doubles(along))
    full_out = lax.all_gather(w_out, "shard", axis=0, tiled=True)
    full_down = lax.all_gather(w_down, "shard", axis=0, tiled=True)
    advance(net, [flow_qkv, flow_gains])
    advance(net, [flow_qkv, flow_gains, flow_gate])
    finish(net, [flow_qkv, flow_gains], 1)
    advance(net, [flow_qkv, flow_gains, flow_gate])
    finish(net, [flow_gate, flow_gains])
    half = flow_gate.value.shape[2] // 2
    flow_left = Flow(
        flow_gate.value[:, :, :half], doubles(path_left[len(along) - 1 :]) + last
    )
    flow_right = Flow(
        flow_gate.value[:, :, half:], doubles(path_right[len(along) - 1 :]) + last
    )
    place = places(along[::-1], [])
    place_left = places(path_left[::-1], [2])
    place_right = places(path_right[::-1], [2])

    packed = jnp.take(flow_gains.value[:, 0], place, axis=0)
    gains, at = [], 0
    for scale in scales:
        size = scale.shape[0]
        gains.append(packed[:, at : at + size].astype(F32).reshape(1, size * shards))
        at += -(-size // 128) * 128
    gai, gao, gmi, gmo, gq, gk = gains

    def is_direct(rows):
        return rows % 16 == 0

    def weight(shape, flows):
        parts = max(1, flows[0][0].value.shape[0] // shards)
        rows = shape[0] // shards
        count = shape[1] // 2 // parts
        if is_direct(rows):
            pieces, first = [], 0
            for flow, at in flows:
                size = flow.value.shape[2]
                cuts = [
                    ((t * rows, rows), (p * count + first, size), shape[1] // 2)
                    for p in range(parts)
                    for t in range(shards)
                ]
                pieces.append((at, cuts, flow.value, flow.got))
                first += size
            return Weight(shape, None, core.reshape(1), pieces)
        halves = []
        for which in ("value", "got"):
            laid = [
                jnp.take(getattr(flow, which), at, axis=0).reshape(parts, shards, rows, -1)
                for flow, at in flows
            ]
            laid = jnp.concatenate(laid, axis=3).transpose(1, 2, 0, 3)
            halves.append(laid.reshape(shape[0], shape[1] // 2))
        first = core == 0
        matrix = jnp.concatenate(
            [jnp.where(first, *halves), jnp.where(first, *halves[::-1])], axis=1
        )
        return Weight(shape, matrix)

    def cut_cols(rows, cols, parts):
        r, c = rows // shards, cols // parts
        return [
            (pl.ds(t * r, r), pl.ds(p * c, c)) for p in range(parts) for t in range(shards)
        ]

    def cut_rows(rows, parts):
        r = rows // shards // parts
        return [pl.ds((t * parts + p) * r, r) for p in range(parts) for t in range(shards)]

    class Grad:
        def __init__(self, ways, parts, cuts, by_cols, shape):
            self.ways, self.shape, self.by_cols = ways, shape, by_cols
            self.parts = 1 << len(parts)
            self.where = places(ways, parts)
            count = len(cuts)
            rows = shape[0] // shards if by_cols else shape[0] // count
            cols = shape[1] * shards // count if by_cols else shape[1]
            self.block = (rows, cols)
            self.direct = is_direct(rows)
            if self.direct:
                self.place, self.cuts, self.out = self.where, cuts, (count, rows, cols)
            else:
                self.place = jnp.zeros((1,), jnp.int32)
                self.cuts = [(slice(0, shape[0]), slice(0, shape[1]))]
                self.out = (1,) + shape
            self.out = (typed(self.out, BF16), ANY)
            self.scratch = [
                pltpu.VMEM(shape, BF16), pltpu.SemaphoreType.DMA((len(self.cuts),))
            ]

        def flow(self, buf, after):
            if not self.direct:
                if self.by_cols:
                    buf = buf.reshape(shards, self.block[0], self.parts, self.block[1])
                    buf = buf.transpose(2, 0, 1, 3)
                else:
                    buf = buf.reshape(shards, self.parts, self.block[0], self.block[1])
                    buf = buf.transpose(1, 0, 2, 3)
                buf = buf.reshape((self.parts * shards,) + self.block)
                order = jnp.zeros_like(self.where).at[self.where].set(
                    jnp.arange(self.where.shape[0], dtype=jnp.int32)
                )
                buf = jnp.take(buf, order, axis=0)
            return Flow(buf, [("halve", way) for way in self.ways] + after)

    up_along = [("shard", bit) for bit in net.shard_bits]
    by_half = [over_core] + up_along
    by_quarter = [over_core, over_side] + up_along
    grad_down = Grad(by_half, [1], cut_rows(ff, 2), False, shape_down)
    grad_gate = Grad(by_quarter, [1, 2], cut_cols(width, 2 * ff, 4), True, shape_gate)
    grad_out = Grad(by_half, [1], cut_rows(heads * hd, 2), False, shape_out)
    grad_qkv = Grad(by_quarter, [1, 2], cut_cols(width, qkv, 4), True, shape_qkv)

    in_v = lambda count: [VMEM] * count
    in_s = lambda count: [SMEM] * count
    out_v = lambda *types: [(typed(*one), VMEM) for one in types]
    sems = lambda count: pltpu.SemaphoreType.DMA((count,))
    reach = min(length, WINDOW + QB)
    bf = lambda *shape: (shape, BF16)
    f32 = lambda *shape: (shape, F32)

    seg_rows = segment_ids.reshape(length, 1)
    seg_cols = segment_ids.reshape(1, length)
    weight_qkv = weight(shape_qkv, [(flow_qkv, place)])
    weight_out, weight_down = Weight(shape_out, full_out), Weight(shape_down, full_down)
    normed, qraw, kraw, values, queries, keys = advance(
        net,
        [flow_left, flow_right],
        kernel_of(
            functools.partial(project_kernel, weight_qkv, heads),
            "project",
            weight_qkv.specs + in_v(6),
            out_v(
                bf(length, width),
                bf(length, heads * hd),
                bf(length, hd),
                bf(length, hd),
                bf(heads, length, hd),
                bf(length, hd),
            ),
            weight_qkv.scratch,
            2 * length * width * qkv,
        ),
        [*weight_qkv.operands, inputs, cos, sin, gai, gq, gk],
    )
    probs, mixed = advance(
        net,
        [flow_left, flow_right],
        kernel_of(
            attend_kernel,
            "attend",
            in_v(5),
            [(typed((heads, length, reach), BF16), ANY)] + out_v(bf(length, heads * hd)),
            [pltpu.VMEM((heads, length, reach), BF16), sems(length // QB)],
            4 * length * heads * hd * reach,
        ),
        [seg_rows, seg_cols, queries, keys, values],
    )

    finish(net, [flow_left, flow_right])
    weight_gate = weight(shape_gate, [(flow_left, place_left), (flow_right, place_right)])
    branch, middle, inner, hidden, act, slope = kernel_of(
        functools.partial(gate_kernel, weight_out, weight_gate),
        "gate",
        weight_out.specs + weight_gate.specs + in_v(4),
        out_v(bf(length, width), f32(length, width), bf(length, width))
        + [(typed((length, ff), BF16), ANY)] * 3,
        weight_out.scratch
        + weight_gate.scratch
        + [pltpu.VMEM((length, ff), BF16)] * 3
        + [sems(3 * (length // RB))],
        2 * length * width * (2 * ff + heads * hd),
    )(*weight_out.operands, *weight_gate.operands, mixed, inputs, gao, gmi)
    output, dmiddle, dbranch, ggain_mlp, buf_down, buf_gate = kernel_of(
        functools.partial(
            mlp_kernel, weight_down, weight_gate, grad_down.cuts, grad_gate.cuts
        ),
        "mlp",
        weight_down.specs + weight_gate.specs + in_s(2) + in_v(7) + [ANY] * 3,
        out_v(bf(length, width), f32(length, width), bf(length, width), f32(3, width))
        + [grad_down.out, grad_gate.out],
        weight_down.scratch
        + weight_gate.scratch
        + [
            pltpu.VMEM((length, ff), BF16),
            pltpu.VMEM((length, 2 * ff), BF16),
            pltpu.VMEM((length, width), BF16),
            grad_down.scratch[0],
            grad_gate.scratch[0],
            sems(3),
            grad_down.scratch[1],
            grad_gate.scratch[1],
        ],
        14 * length * width * ff,
    )(
        *weight_down.operands, *weight_gate.operands, grad_down.place, grad_gate.place,
        middle, branch, inner, out_grad, gmo, gmi, gao, hidden, act, slope,
    )
    back_down = grad_down.flow(buf_down, [("sum", over_side), ("join", over_core, 1)])
    back_gate = grad_gate.flow(buf_gate, [("join", over_side, 2)])

    dmixed, buf_out = advance(
        net,
        [back_gate, back_down],
        kernel_of(
            functools.partial(out_bwd_kernel, weight_out, grad_out.cuts, heads),
            "out_bwd",
            weight_out.specs + in_s(1) + in_v(2),
            out_v(bf(heads, length, hd)) + [grad_out.out],
            weight_out.scratch + grad_out.scratch,
            4 * length * heads * hd * width,
        ),
        [*weight_out.operands, grad_out.place, dbranch, mixed],
    )
    back_out = grad_out.flow(buf_out, [("sum", over_side), ("join", over_core, 1)])
    draw, ggain_qk, buf_qkv = advance(
        net,
        [back_gate, back_down, back_out],
        kernel_of(
            functools.partial(attn_bwd_kernel, grad_qkv.cuts),
            "attn_bwd",
            in_s(1) + in_v(11) + [ANY],
            out_v(bf(length, qkv), f32(2, hd)) + [grad_qkv.out],
            [
                pltpu.VMEM((heads, length, reach), BF16),
                sems(length // QB),
                pltpu.VMEM((heads, QB, reach), BF16),
                pltpu.VMEM((length, heads * hd), F32),
                pltpu.VMEM((length, hd), F32),
                pltpu.VMEM((length, hd), F32),
            ]
            + grad_qkv.scratch,
            2 * length * (width * qkv + 4 * heads * hd * reach),
        ),
        [
            grad_qkv.place, dmixed, queries, keys, values, qraw, kraw, normed, cos, sin, gq, gk,
            probs,
        ],
    )
    back_qkv = grad_qkv.flow(buf_qkv, [("join", over_side, 2), ("join", over_core, 2)])
    input_grad, ggain_in = advance(
        net,
        [back_gate, back_down, back_out, back_qkv],
        kernel_of(
            functools.partial(input_bwd_kernel, weight_qkv),
            "input_bwd",
            weight_qkv.specs + in_v(4),
            out_v(f32(length, width), f32(1, width)),
            weight_qkv.scratch,
            2 * length * width * qkv,
        ),
        [*weight_qkv.operands, draw, dmiddle, inputs, gai],
    )

    sums = jnp.concatenate(
        [ggain_in, ggain_mlp[2:3], ggain_mlp[1:2], ggain_mlp[0:1], ggain_qk[0:1], ggain_qk[1:2]],
        axis=1,
    )
    sums = Flow(sums.reshape(-1, 128), [("total", way) for way in [over_core, over_side] + along])
    finish(net, [back_down, back_gate, back_out, back_qkv, sums])
    share_gate = back_gate.value[0]
    other = net.swap(share_gate, *over_core)
    full_gate = jnp.where(core == 0, share_gate, other).astype(F32)
    full_up = jnp.where(core == 0, other, share_gate).astype(F32)
    full_qkv = back_qkv.value[0].astype(F32)
    full_out = back_out.value[0].astype(F32)
    full_down = back_down.value[0].astype(F32)
    sums = sums.value.reshape(-1)

    shard = lax.axis_index("shard")
    grads, at = [], 0
    for scale in scales:
        size = scale.shape[0]
        grads.append(lax.dynamic_slice_in_dim(sums, at + shard * size, size, 0))
        at += size * shards
    return (
        output,
        input_grad,
        full_qkv[:, : heads * hd],
        full_qkv[:, heads * hd : (heads + 1) * hd],
        full_qkv[:, (heads + 1) * hd :],
        full_out,
        full_gate,
        full_up,
        full_down,
        grads[0],
        grads[4],
        grads[5],
        grads[1],
        grads[2],
        grads[3],
    )


def solution(mesh):
    rows, vector = P("shard", None), P("shard")
    tokens = P(AXES, None)
    return jax.shard_map(
        functools.partial(layer, Net(mesh)),
        mesh=mesh,
        in_specs=(tokens, P(AXES), tokens) + (rows,) * 7 + (vector,) * 6,
        out_specs=(tokens, tokens) + (rows,) * 7 + (vector,) * 6,
        check_vma=False,
    )
```

```python
import functools
import math

import jax
import jax.numpy as jnp
from jax import lax
from jax.experimental import pallas as pl
from jax.experimental.pallas import tpu as pltpu
from jax.sharding import PartitionSpec as P

WINDOW = 512
EPSILON = 1e-06
NEG = -1e30
QB = 256
RB = 512
CB = 512
GB = 1024
AXES = ("replica", "shard")
F32 = jnp.float32
BF16 = jnp.bfloat16
GELU_C = math.sqrt(2.0 / math.pi)


def flip_pairs(reps, shards, axis, bit):
    pairs = []
    for rep in range(reps):
        for shard in range(shards):
            rep_to = rep ^ bit if axis == "replica" else rep
            shard_to = shard ^ bit if axis == "shard" else shard
            pairs.append((rep * shards + shard, rep_to * shards + shard_to))
    return pairs


class Net:
    def __init__(self, mesh):
        self.reps = mesh.shape["replica"]
        self.shards = mesh.shape["shard"]
        self.shard_bits = [1 << i for i in range(self.shards.bit_length() - 1)]
        self.rep_bits = [1 << i for i in range(self.reps.bit_length() - 1)]
        assert 1 << len(self.shard_bits) == self.shards
        assert self.reps == 4

    def swap(self, value, axis, bit):
        return lax.ppermute(value, AXES, flip_pairs(self.reps, self.shards, axis, bit))

    def launch(self, flows, args=()):
        moves = [flow.move() for flow in flows]
        values, args = lax.optimization_barrier(([value for value, _ in moves], list(args)))
        return [self.swap(value, *way) for value, (_, way) in zip(values, moves)], args


def add_up(value, got):
    return (value.astype(F32) + got.astype(F32)).astype(BF16)


def in_order(value, got, axis, bit, dim):
    first = (lax.axis_index(axis) & bit) == 0
    return jnp.concatenate([jnp.where(first, value, got), jnp.where(first, got, value)], axis=dim)


class Flow:
    def __init__(self, value, steps):
        self.value = value
        self.steps = list(steps)

    def move(self):
        if self.steps[0][0] == "halve":
            return self.value[1], self.steps[0][1]
        return self.value, self.steps[0][1]

    def take(self, got):
        kind, way = self.steps[0][:2]
        value = self.value
        if kind == "double":
            self.value = jnp.concatenate([value, got], axis=0)
        elif kind == "swap":
            self.got = got
        elif kind == "halve":
            near = value[0]
            if len(self.steps) > 1 and self.steps[1][0] == "halve":
                half = near.shape[0] // 2
                self.value = (add_up(near[:half], got[:half]), add_up(near[half:], got[half:]))
            else:
                self.value = add_up(near, got)
        elif kind == "total":
            self.value = value + got
        else:
            self.value = in_order(value[None], got[None], *way, 0)
        self.steps = self.steps[1:]


def land(flows, got, outs=()):
    got, outs = lax.optimization_barrier((got, outs))
    for flow, value in zip(flows, got):
        flow.take(value)
    return outs


def advance(net, flows, work=None, args=()):
    flows = [flow for flow in flows if flow.steps]
    got, args = net.launch(flows, args)
    return land(flows, got, work(*args) if work is not None else ())


def finish(net, flows, left=0):
    while any(len(flow.steps) > left for flow in flows):
        advance(net, [flow for flow in flows if len(flow.steps) > left])


def places(stages, parts):
    rep = lax.axis_index("replica")
    shard = lax.axis_index("shard")
    shards = 1
    for axis, bit in stages:
        shards *= 2 if axis == "shard" else 1
    count = 1 << len(parts)
    part = jnp.arange(count, dtype=jnp.int32)[:, None]
    block = jnp.arange(shards, dtype=jnp.int32)[None, :]
    part_rep = jnp.zeros_like(part)
    for i, bit in enumerate(parts):
        part_rep = part_rep + ((part >> (len(parts) - 1 - i)) & 1) * bit
    rep_diff = part_rep ^ rep
    shard_diff = block ^ shard
    where = jnp.zeros((count, shards), jnp.int32)
    for axis, bit in stages:
        diff = rep_diff if axis == "replica" else shard_diff
        where = where * 2 + jnp.where((diff & bit) != 0, 1, 0)
    return where.reshape(-1)


def dot(left, right):
    return jnp.dot(left, right, preferred_element_type=F32)


def dot_nt(left, right):
    return lax.dot_general(left, right, (((1,), (1,)), ((), ())), preferred_element_type=F32)


def dot_tn(left, right):
    return lax.dot_general(left, right, (((0,), (0,)), ((), ())), preferred_element_type=F32)


def inv_rms(value):
    return lax.rsqrt(jnp.mean(value * value, axis=-1, keepdims=True) + EPSILON)


def norm_back(grad, unit, inv, gain):
    scaled = grad * gain
    return inv * (scaled - unit * jnp.mean(scaled * unit, axis=-1, keepdims=True))


def rows_of(index, size):
    return pl.ds(pl.multiple_of(index * size, size), size)


def start_all(copies):
    for copy in copies:
        copy.start()


def wait_all(copies):
    for copy in copies:
        copy.wait()


def on_first(copies):
    @pl.when(pl.program_id(0) == 0)
    def _():
        start_all(copies)
        wait_all(copies)


def project_kernel(weight_qkv, heads, *refs):
    refs_qkv, refs = split(refs, len(weight_qkv.specs))
    (
        x_ref, cos_ref, sin_ref, gai_ref, gq_ref, gk_ref,
        normed_ref, qraw_ref, kraw_ref, v_ref, q_ref, k_ref,
        wqkv, sem_qkv,
    ) = refs
    hd = k_ref.shape[1]
    half = hd // 2
    factor = hd ** (-0.5)
    on_first(weight_qkv.copies(refs_qkv, wqkv, sem_qkv))
    x = x_ref[...].astype(F32)
    normed = (x * inv_rms(x) * gai_ref[...]).astype(BF16)
    normed_ref[...] = normed
    cos, sin = cos_ref[...], sin_ref[...]

    def turn(value):
        first, second = value[:, :half], value[:, half:]
        return jnp.concatenate([first * cos - second * sin, second * cos + first * sin], axis=1)

    for h in range(heads):
        raw = dot(normed, wqkv[:, h * hd : (h + 1) * hd])
        qraw_ref[:, h * hd : (h + 1) * hd] = raw.astype(BF16)
        q_ref[h, :, :] = (turn(raw * inv_rms(raw) * gq_ref[...]) * factor).astype(BF16)
    raw = dot(normed, wqkv[:, heads * hd : (heads + 1) * hd])
    kraw_ref[...] = raw.astype(BF16)
    k_ref[...] = turn(raw * inv_rms(raw) * gk_ref[...]).astype(BF16)
    v_ref[...] = dot(normed, wqkv[:, (heads + 1) * hd :]).astype(BF16)


def attend_kernel(
    segr_ref, segc_ref, q_ref, k_ref, v_ref, probs_hbm, mixed_ref, probs_all, sem_probs
):
    heads, length, hd = q_ref.shape
    out_probs = probs_copies(probs_hbm, probs_all, sem_probs, True)
    for b in range(length // QB):
        low, high = key_range(b)
        width = high - low
        rows = slice(b * QB, high)
        seg_q, seg_k = segr_ref[rows, :], segc_ref[:, low:high]
        offset = (
            lax.broadcasted_iota(jnp.int32, (QB, width), 0)
            - lax.broadcasted_iota(jnp.int32, (QB, width), 1)
            + (b * QB - low)
        )
        allowed = (seg_q == seg_k) & (seg_q >= 0) & (offset >= 0) & (offset < WINDOW)
        allowed = allowed | (offset == 0)
        keys, vals = k_ref[low:high, :], v_ref[low:high, :]
        for h in range(heads):
            scores = jnp.where(allowed, dot_nt(q_ref[h, rows, :], keys), NEG)
            expo = jnp.exp(scores - jnp.max(scores, axis=1, keepdims=True))
            probs = (expo * (1.0 / jnp.sum(expo, axis=1, keepdims=True))).astype(BF16)
            probs_all[h, rows, 0:width] = probs
            mixed_ref[rows, h * hd : (h + 1) * hd] = dot(probs, vals).astype(BF16)
        out_probs[b].start()
    wait_all(out_probs)


def cut_at(cut, which):
    (row, rows, row_step), (col, cols, col_step) = cut
    if row_step:
        row = pl.multiple_of(row + which * row_step, 16)
    if col_step:
        col = pl.multiple_of(col + which * col_step, 128)
    return pl.ds(row, rows), pl.ds(col, cols)


class Weight:
    def __init__(self, shape, matrix=None, rows=(), core=None, pieces=(), source=0):
        self.shape, self.rows, self.source = shape, rows, source
        self.cuts = [cuts for _, cuts, _, _ in pieces]
        if matrix is not None:
            self.operands, self.specs, count = [matrix], [ANY], len(rows)
        else:
            self.operands, self.specs, count = [core], [SMEM], 0
            for place, cuts, own, got in pieces:
                self.operands += [place, own, got]
                self.specs += [SMEM, ANY, ANY]
                count += 2 * len(cuts)
        self.scratch = [pltpu.VMEM(shape, BF16), pltpu.SemaphoreType.DMA((count,))]

    def copies(self, refs, mat, sem):
        made = []
        for source, to, count in self.rows:
            src, dst = refs[0].at[pl.ds(source, count), :], mat.at[pl.ds(to, count), :]
            made.append(pltpu.make_async_copy(src, dst, sem.at[len(made)]))
        for piece, cuts in enumerate(self.cuts):
            core = refs[0][0]
            place, own, got = refs[3 * piece + 1 : 3 * piece + 4]
            for n, cut in enumerate(cuts):
                for hbm, which in ((own, core), (got, 1 - core)):
                    src = hbm.at[place[n], pl.ds(self.source, cut[0][1]), :]
                    dst = mat.at[cut_at(cut, which)]
                    made.append(pltpu.make_async_copy(src, dst, sem.at[len(made)]))
        return made


def grad_copies(cuts, refs, mats, sem):
    core_ref, places_ref, near, far = refs
    if not cuts:
        return [pltpu.make_async_copy(m, o, sem.at[i]) for i, (m, o) in enumerate(zip(mats, (near, far)))]
    core, made = core_ref[0], []
    for mat, cut, which_place, n, col in cuts:
        for hbm, which in ((far, 1 - core), (near, core)):
            src = mats[mat].at[cut_at(cut, which)]
            dst = hbm.at[places_ref[which_place, n], :, pl.ds(col, cut[1][1])]
            made.append(pltpu.make_async_copy(src, dst, sem.at[len(made)]))
    return made


def split(refs, *counts):
    parts, at = [], 0
    for count in counts:
        parts.append(refs[at : at + count])
        at += count
    return parts + [refs[at:]]


def mlp_kernel(weight_out, weight_down, weight_gate, cuts_grad, *refs):
    refs_out, refs_down, refs_gate, to_grad, refs = split(
        refs, len(weight_out.specs), len(weight_down.specs), len(weight_gate.specs), 2
    )
    (
        mixed_ref, x_ref, gao_ref, gmi_ref, gmo_ref, top_hbm,
        output_hbm, dmiddle_hbm, dbranch_ref, ggain_ref, near, far,
        wout, sem_out, wdown, sem_down, wgu, sem_gate,
        top_ref, branch_ref, inner_ref, hidden, dgu, ddown, gdown, ggate, middle_ref, output_ref,
        sem, sem_grad,
    ) = refs
    length, ff = hidden.shape
    in_out = weight_out.copies(refs_out, wout, sem_out)
    in_gate = weight_gate.copies(refs_gate, wgu, sem_gate)
    in_down = weight_down.copies(refs_down, wdown, sem_down)
    in_top = pltpu.make_async_copy(top_hbm, top_ref, sem.at[0])
    start_all(in_out)
    start_all(in_gate)
    start_all(in_down)
    in_top.start()
    ggain_ref[...] = jnp.zeros_like(ggain_ref)
    wait_all(in_out)

    def attn_out(i, carry):
        rows = rows_of(i, QB)
        branch = dot(mixed_ref[rows, :], wout[...])
        branch_ref[rows, :] = branch.astype(BF16)
        middle = x_ref[rows, :].astype(F32) + branch * inv_rms(branch) * gao_ref[...]
        middle_ref[rows, :] = middle
        inner_ref[rows, :] = (middle * inv_rms(middle) * gmi_ref[...]).astype(BF16)
        return carry

    lax.fori_loop(0, length // QB, attn_out, 0)
    wait_all(in_gate)

    def forward(i, carry):
        rows = rows_of(i, RB)
        inner = inner_ref[rows, :]
        for c in range(ff // CB):
            cols = slice(c * CB, (c + 1) * CB)
            more = slice(ff + c * CB, ff + (c + 1) * CB)
            gate = dot(inner, wgu[:, cols])
            up = dot(inner, wgu[:, more])
            square = gate * gate
            tanh = jnp.tanh(gate * (GELU_C + (GELU_C * 0.044715) * square))
            base = 0.5 + 0.5 * tanh
            act = gate * base
            slope = base + (0.5 * gate) * (1.0 - tanh * tanh) * (
                GELU_C + (3.0 * GELU_C * 0.044715) * square
            )
            hidden[rows, cols] = (act * up).astype(BF16)
            dgu[rows, cols] = (slope * up).astype(BF16)
            dgu[rows, more] = act.astype(BF16)
        return carry

    lax.fori_loop(0, length // RB, forward, 0)
    wait_all(in_down)
    in_top.wait()

    def down_row(i, carry):
        rows = rows_of(i, RB)
        down = dot(hidden[rows, :], wdown[...])
        inv = inv_rms(down)
        unit = down * inv
        output_ref[rows, :] = (middle_ref[rows, :] + unit * gmo_ref[...]).astype(BF16)
        top = top_ref[rows, :].astype(F32)
        ddown[rows, :] = norm_back(top, unit, inv, gmo_ref[...]).astype(BF16)
        ggain_ref[0:1, :] += jnp.sum(top * unit, axis=0, keepdims=True)
        return carry

    lax.fori_loop(0, length // RB, down_row, 0)
    out_output = pltpu.make_async_copy(output_ref, output_hbm, sem.at[1])
    out_output.start()

    def down_grad(i, carry):
        cols = rows_of(i, GB)
        gdown[:, cols] = dot_tn(ddown[...], hidden[:, cols]).astype(BF16)
        return carry

    lax.fori_loop(0, ff // GB, down_grad, 0)

    def hidden_back(i, carry):
        rows = rows_of(i, RB)
        grad = ddown[rows, :]
        for c in range(ff // CB):
            cols = slice(c * CB, (c + 1) * CB)
            more = slice(ff + c * CB, ff + (c + 1) * CB)
            dhid = dot_nt(grad, wdown[cols, :])
            dgu[rows, cols] = (dhid * dgu[rows, cols].astype(F32)).astype(BF16)
            dgu[rows, more] = (dhid * dgu[rows, more].astype(F32)).astype(BF16)
        return carry

    lax.fori_loop(0, length // RB, hidden_back, 0)

    def gate_grad(i, carry):
        cols = rows_of(i, GB)
        ggate[:, cols] = dot_tn(inner_ref[...], dgu[:, cols]).astype(BF16)
        return carry

    lax.fori_loop(0, 2 * ff // GB, gate_grad, 0)
    out_grad = grad_copies(cuts_grad, (*to_grad, near, far), (ggate, gdown), sem_grad)
    start_all(out_grad)

    def inner_back(i, carry):
        rows = rows_of(i, RB)
        dinner = dot_nt(dgu[rows, :], wgu[...])
        middle = middle_ref[rows, :]
        inv = inv_rms(middle)
        unit = middle * inv
        dmid = top_ref[rows, :].astype(F32) + norm_back(dinner, unit, inv, gmi_ref[...])
        middle_ref[rows, :] = dmid
        ggain_ref[1:2, :] += jnp.sum(dinner * unit, axis=0, keepdims=True)
        branch = branch_ref[rows, :].astype(F32)
        inv = inv_rms(branch)
        unit = branch * inv
        dbranch_ref[rows, :] = norm_back(dmid, unit, inv, gao_ref[...]).astype(BF16)
        ggain_ref[2:3, :] += jnp.sum(dmid * unit, axis=0, keepdims=True)
        return carry

    lax.fori_loop(0, length // RB, inner_back, 0)
    out_middle = pltpu.make_async_copy(middle_ref, dmiddle_hbm, sem.at[2])
    out_middle.start()
    out_output.wait()
    wait_all(out_grad)
    out_middle.wait()


def out_bwd_kernel(weight_out, heads, *refs):
    refs_out, refs = split(refs, len(weight_out.specs))
    dbranch_ref, mixed_ref, dmixed_ref, gout_ref, wout, sem_out = refs
    length = mixed_ref.shape[0]
    hd = dmixed_ref.shape[2]
    in_out = weight_out.copies(refs_out, wout, sem_out)
    start_all(in_out)

    def weights_out(i, carry):
        cols = rows_of(i, CB)
        gout_ref[:, cols] = dot_tn(dbranch_ref[...], mixed_ref[:, cols]).astype(BF16)
        return carry

    lax.fori_loop(0, heads * hd // CB, weights_out, 0)
    wait_all(in_out)

    def mixed_back(i, carry):
        rows = rows_of(i, QB)
        for h in range(heads):
            cols = slice(h * hd, (h + 1) * hd)
            dmixed_ref[h, rows, :] = dot_nt(dbranch_ref[rows, :], wout[cols, :]).astype(BF16)
        return carry

    lax.fori_loop(0, length // QB, mixed_back, 0)


def turn_back(value, cos, sin):
    half = value.shape[1] // 2
    first, second = value[:, :half], value[:, half:]
    return jnp.concatenate([first * cos + second * sin, second * cos - first * sin], axis=1)


def key_range(b):
    return max(0, b - WINDOW // QB) * QB, (b + 1) * QB


def probs_copies(probs_hbm, probs, sem, outward):
    made = []
    for b in range(probs.shape[1] // QB):
        low, high = key_range(b)
        at = (slice(None), slice(b * QB, high), slice(0, high - low))
        far, near = probs_hbm.at[at], probs.at[at]
        src, dst = (near, far) if outward else (far, near)
        made.append(pltpu.make_async_copy(src, dst, sem.at[b]))
    return made


def attn_bwd_kernel(cuts_grad, *refs):
    (
        core_ref, places_ref, dmixed_ref, q_ref, k_ref, v_ref, qraw_ref, kraw_ref, normed_ref,
        cos_ref, sin_ref, gq_ref, gk_ref, gout_ref, probs_hbm,
        draw_ref, ggain_ref, near, far,
        probs_all, sem_probs, ds, dq, dk, dv, gqkv, sem_grad,
    ) = refs
    heads, length, hd = q_ref.shape
    factor = hd ** (-0.5)
    in_probs = probs_copies(probs_hbm, probs_all, sem_probs, False)
    start_all(in_probs)
    dk[...] = jnp.zeros_like(dk)
    dv[...] = jnp.zeros_like(dv)
    for b in range(length // QB):
        low, high = key_range(b)
        width = high - low
        rows = slice(b * QB, high)
        in_probs[b].wait()
        keys, vals = k_ref[low:high, :], v_ref[low:high, :]
        for h in range(heads):
            probs = probs_all[h, rows, 0:width].astype(F32)
            dprobs = dot_nt(dmixed_ref[h, rows, :], vals)
            inner = jnp.sum(probs * dprobs, axis=1, keepdims=True)
            dscores = (probs * (dprobs - inner)).astype(BF16)
            ds[h, :, 0:width] = dscores
            dq[rows, h * hd : (h + 1) * hd] = dot(dscores, keys) * factor
        stack = lambda value: value.reshape(heads * QB, value.shape[2])
        dk[:, low:high] += dot_tn(stack(q_ref[:, rows, :]), stack(ds[:, :, 0:width]))
        dv[:, low:high] += dot_tn(
            stack(dmixed_ref[:, rows, :]), stack(probs_all[:, rows, 0:width])
        )

    ggain_ref[...] = jnp.zeros_like(ggain_ref)

    def raw_back(i, carry):
        rows = rows_of(i, QB)
        cos, sin = cos_ref[rows, :], sin_ref[rows, :]
        total = jnp.zeros((1, hd), F32)
        for h in range(heads):
            cols = slice(h * hd, (h + 1) * hd)
            grad = turn_back(dq[rows, cols], cos, sin)
            raw = qraw_ref[rows, cols].astype(F32)
            inv = inv_rms(raw)
            unit = raw * inv
            draw_ref[rows, cols] = norm_back(grad, unit, inv, gq_ref[...]).astype(BF16)
            total += jnp.sum(grad * unit, axis=0, keepdims=True)
        ggain_ref[0:1, :] += total
        grad = turn_back(dk[:, rows].T, cos, sin)
        raw = kraw_ref[rows, :].astype(F32)
        inv = inv_rms(raw)
        unit = raw * inv
        draw_ref[rows, heads * hd : (heads + 1) * hd] = norm_back(
            grad, unit, inv, gk_ref[...]
        ).astype(BF16)
        ggain_ref[1:2, :] += jnp.sum(grad * unit, axis=0, keepdims=True)
        draw_ref[rows, (heads + 1) * hd :] = dv[:, rows].T.astype(BF16)
        return carry

    lax.fori_loop(0, length // QB, raw_back, 0)

    def weights(i, carry):
        cols = rows_of(i, CB)
        gqkv[:, cols] = dot_tn(normed_ref[...], draw_ref[:, cols]).astype(BF16)
        return carry

    lax.fori_loop(0, gqkv.shape[1] // CB, weights, 0)
    out_grad = grad_copies(cuts_grad, (core_ref, places_ref, near, far), (gqkv, gout_ref), sem_grad)
    start_all(out_grad)
    wait_all(out_grad)


def input_bwd_kernel(weight_qkv, *refs):
    refs_qkv, refs = split(refs, len(weight_qkv.specs))
    draw_ref, dmiddle_ref, x_ref, gai_ref, dx_ref, ggain_ref, wqkv, sem_qkv = refs
    on_first(weight_qkv.copies(refs_qkv, wqkv, sem_qkv))

    @pl.when(pl.program_id(0) == 0)
    def _():
        ggain_ref[...] = jnp.zeros_like(ggain_ref)

    dnormed = dot_nt(draw_ref[...], wqkv[...])
    x = x_ref[...].astype(F32)
    inv = inv_rms(x)
    unit = x * inv
    dx_ref[...] = dmiddle_ref[...] + norm_back(dnormed, unit, inv, gai_ref[...])
    ggain_ref[...] += jnp.sum(dnormed * unit, axis=0, keepdims=True)


def shares_kernel(widths, ca, me_ref, value_ref, got_ref, *refs):
    *a_refs, b_ref, turned = refs
    core, side = me_ref[0], me_ref[1]
    rows, size = value_ref.shape[1], turned.shape[1]
    pieces = (value_ref.shape[2] - ca) // size
    for c in range(2):
        for s in range(2):
            n = 2 * c + s
            at = jnp.bitwise_xor(side, s)
            own, got = value_ref[at].astype(F32), got_ref[at].astype(F32)
            block = jnp.where(core == c, own, got)
            low = 0
            for ref, count in zip(a_refs, widths):
                first, last = max(low, n * ca), min(low + count, (n + 1) * ca)
                if first < last:
                    ref[:, first - low : last - low] = block[:, first - n * ca : last - n * ca]
                low += count
            for j in range(pieces):
                row = (n * pieces + j) * rows
                turned[row : row + rows, :] = block[:, ca + j * size : ca + (j + 1) * size]
    b_ref[...] = turned[...].T


VMEM = pl.BlockSpec(memory_space=pltpu.VMEM)
SMEM = pl.BlockSpec(memory_space=pltpu.SMEM)
ANY = pl.BlockSpec(memory_space=pl.ANY)


def by_rows(width):
    return pl.BlockSpec((QB, width), lambda i: (i, 0))


def all_of(*shape):
    return pl.BlockSpec(shape, lambda i: (0,) * len(shape))


def kernel_of(body, name, in_specs, outs, scratch, flops, **more):
    def run(*operands):
        total = 0
        for value in list(operands) + [value for value, _ in outs]:
            total += math.prod(value.shape) * value.dtype.itemsize
        return pl.pallas_call(
            body,
            name=name,
            out_shape=[value for value, _ in outs],
            in_specs=in_specs,
            out_specs=[spec for _, spec in outs],
            scratch_shapes=scratch,
            compiler_params=pltpu.CompilerParams(vmem_limit_bytes=56 << 20),
            cost_estimate=pl.CostEstimate(flops=flops, bytes_accessed=total, transcendentals=0),
            **more,
        )(*operands)

    return run


def typed(shape, dtype):
    return jax.ShapeDtypeStruct(shape, dtype)


def positions(seg):
    length = seg.shape[0]
    index = jnp.arange(length, dtype=jnp.int32)
    previous = jnp.concatenate([jnp.full((1,), -3, jnp.int32), seg[:-1]])
    starts = jnp.where(seg != previous, index, jnp.zeros_like(index))
    return index - lax.cummax(starts, axis=0)


def rope_angles(position, head_dim):
    half = head_dim // 2
    freqs = 10000.0 ** (-2.0 * jnp.arange(half, dtype=F32) / head_dim)
    return position.astype(F32)[:, None] * freqs[None, :]


def layer(
    net,
    inputs,
    segment_ids,
    out_grad,
    w_query,
    w_key,
    w_value,
    w_out,
    w_gate,
    w_up,
    w_down,
    scale_attn_in,
    scale_query,
    scale_key,
    scale_attn_out,
    scale_mlp_in,
    scale_mlp_out,
):
    length, width = inputs.shape
    hd = w_key.shape[1]
    heads = w_query.shape[1] // hd
    qkv = (heads + 2) * hd
    ff = w_gate.shape[1]
    shards = net.shards
    rep = lax.axis_index("replica")
    core = rep & 1
    side = (rep >> 1) & 1

    along = [("shard", bit) for bit in reversed(net.shard_bits)]
    over_core, over_side = ("replica", 1), ("replica", 2)
    doubles = lambda ways: [("double", way) for way in ways]

    def half_rows(value, index, parts):
        size = value.shape[0] // parts
        return lax.dynamic_slice_in_dim(value, index * size, size, 0)

    def half_cols(value, index, parts):
        size = value.shape[1] // parts
        return lax.dynamic_slice_in_dim(value, index * size, size, 1)

    path_left = along + [over_side]
    path_right = along[:-1] + [over_side, along[-1]]
    scales = (scale_attn_in, scale_attn_out, scale_mlp_in, scale_mlp_out, scale_query, scale_key)
    shape_qkv, shape_out = (width, qkv), (heads * hd, width)
    shape_gate, shape_down = (width, 2 * ff), (ff, width)
    last = [("swap", over_core)]

    angles = rope_angles(positions(segment_ids), hd)
    half = qkv // 2
    rows_qkv = w_query.shape[0]
    key_at, value_at = heads * hd - half, heads * hd + hd - half
    second = jnp.pad(w_query[:, half:], ((0, 0), (0, qkv - heads * hd)))
    second += jnp.pad(w_key, ((0, 0), (key_at, half - key_at - hd)))
    second += jnp.pad(w_value, ((0, 0), (value_at, half - value_at - hd)))
    own_qkv = jnp.where(core == 0, w_query[:, :half], second)
    own_qkv = jnp.pad(own_qkv, ((0, 16), (0, 0)))
    at = 0
    for scale in scales:
        size = scale.shape[0]
        own_qkv += jnp.pad(scale[None, :], ((rows_qkv, 15), (at, half - at - size)))
        at += -(-size // 128) * 128
    flow_qkv = Flow(own_qkv[None], doubles(along) + last)
    own_gate = half_cols(jnp.where(core == 0, w_gate, w_up), side, 2)[None]
    flow_gate = Flow(own_gate, doubles(along[:-1]))
    own_rows = jnp.concatenate([half_rows(w_out, core, 2), half_rows(w_down, core, 2)], axis=0)
    cos, sin = advance(net, [flow_qkv], lambda a: (jnp.cos(a), jnp.sin(a)), [angles])
    finish(net, [flow_qkv], 3)
    advance(net, [flow_qkv, flow_gate])
    flow_rows = Flow(lax.all_gather(own_rows[None], "shard", axis=0, tiled=True), last)
    finish(net, [flow_qkv, flow_gate], 2)
    finish(net, [flow_gate], 1)
    flows = [flow_qkv, flow_gate]
    got, _ = net.launch(flows)
    land(flows[:1], got[:1])
    core_got, _ = net.launch(flows[:1])
    land(flows[1:], got[1:])
    half = flow_gate.value.shape[2] // 2
    flow_left = Flow(
        flow_gate.value[:, :, :half], doubles(path_left[len(along) - 1 :]) + last
    )
    flow_right = Flow(
        flow_gate.value[:, :, half:], doubles(path_right[len(along) - 1 :]) + last
    )
    place = places(along[::-1], [])
    place_left = places(path_left[::-1], [2])
    place_right = places(path_right[::-1], [2])

    packed = jnp.take(flow_qkv.value[:, rows_qkv], place, axis=0)
    gains, at = [], 0
    for scale in scales:
        size = scale.shape[0]
        gains.append(packed[:, at : at + size].astype(F32).reshape(1, size * shards))
        at += -(-size // 128) * 128
    gai, gao, gmi, gmo, gq, gk = gains

    def is_direct(rows):
        return rows % 16 == 0

    first_core = core.reshape(1)

    def weight(shape, flows):
        parts = max(1, flows[0][0].value.shape[0] // shards)
        rows = shape[0] // shards
        count = shape[1] // 2 // parts
        if is_direct(rows):
            pieces, first = [], 0
            for flow, at in flows:
                size = flow.value.shape[2]
                cuts = [
                    ((t * rows, rows, 0), (p * count + first, size, shape[1] // 2))
                    for p in range(parts)
                    for t in range(shards)
                ]
                pieces.append((at, cuts, flow.value, flow.got))
                first += size
            return Weight(shape, core=first_core, pieces=pieces)
        halves = []
        for which in ("value", "got"):
            laid = [
                jnp.take(getattr(flow, which)[:, :rows], at, axis=0).reshape(
                    parts, shards, rows, -1
                )
                for flow, at in flows
            ]
            laid = jnp.concatenate(laid, axis=3).transpose(1, 2, 0, 3)
            halves.append(laid.reshape(shape[0], shape[1] // 2))
        first = core == 0
        matrix = jnp.concatenate(
            [jnp.where(first, *halves), jnp.where(first, *halves[::-1])], axis=1
        )
        return Weight(shape, matrix, [(0, 0, shape[0])])

    def weight_rows(shape, flow, first, rows):
        if is_direct(first) and is_direct(rows):
            cuts = [((2 * t * rows, rows, rows), (0, shape[1], 0)) for t in range(shards)]
            order = jnp.arange(shards, dtype=jnp.int32)
            return Weight(
                shape,
                core=first_core,
                pieces=[(order, cuts, flow.value, flow.got)],
                source=first,
            )
        both = [value[:, first : first + rows] for value in (flow.value, flow.got)]
        matrix = jnp.stack(
            [jnp.where(core == 0, *both), jnp.where(core == 0, *both[::-1])], axis=1
        )
        return Weight(shape, matrix.reshape(shape), [(0, 0, shape[0])])

    class Grad:
        def __init__(self, shape_a, shape_b, left):
            self.shapes = shape_a, shape_b
            self.rows = rows = width // shards
            self.cols = ca, cb = shape_a[1] // 4, shape_b[1] // 4
            self.size = size = shape_b[1] // shards
            self.left = left
            first, second, others = up_along[0], up_along[1], up_along[2:]
            self.others = others
            self.ways = [[first, over_side, second] + others]
            if left < ca + cb:
                self.ways.insert(0, [over_side, second, first] + others)
            self.places = jnp.stack([places(ways, [2]) for ways in self.ways])
            self.direct = is_direct(rows)
            self.cuts = []
            if self.direct:
                for p in range(2):
                    for t in range(shards):
                        n = p * shards + t
                        edges = (0, left, ca) if left < ca else (0, ca)
                        for which, (low, high) in enumerate(zip(edges, edges[1:])):
                            cut = (t * rows, rows, 0), (p * ca + low, high - low, shape_a[1] // 2)
                            self.cuts.append((0, cut, which, n, low))
                        for j in range(cb // size):
                            high = (p * cb // size + j) * rows
                            cut = (high, rows, width // 2), (t * size, size, 0)
                            self.cuts.append((1, cut, len(self.ways) - 1, n, ca + j * size))
                self.outs = [(typed((2 * shards, rows, ca + cb), BF16), ANY)] * 2
            else:
                self.outs = [(typed(shape, BF16), ANY) for shape in self.shapes]
            self.operands = [first_core, self.places]
            self.sems = pltpu.SemaphoreType.DMA((max(2, 2 * len(self.cuts)),))

        def flow(self, near, far):
            if not self.direct:
                a, b = near, far
                a = a.reshape(shards, self.rows, 2, 2, self.cols[0]).transpose(2, 3, 0, 1, 4)
                b = b.reshape(2, 2, shards // 4, self.rows, shards, self.size)
                b = b.transpose(0, 1, 4, 3, 2, 5).reshape(a.shape[:4] + (self.cols[1],))
                both = jnp.concatenate([a, b], axis=4)
                both = jnp.where(core == 0, both, both[::-1])
                both = both.reshape((2, 2 * shards) + both.shape[3:])
                sides = []
                for n, ways in enumerate(self.ways):
                    order = jnp.zeros_like(self.places[n]).at[self.places[n]].set(
                        jnp.arange(2 * shards, dtype=jnp.int32)
                    )
                    sides.append(jnp.take(both, order, axis=1))
                if len(sides) == 2:
                    sides = [sides[0][..., : self.left], sides[1][..., self.left :]]
                near, far = jnp.concatenate(sides, axis=3)
            steps = [("halve", over_core)]
            if len(self.ways) == 1:
                steps += [("halve", way) for way in self.ways[0]] + self.ends()
            return Flow((near, far), steps)

        def ends(self):
            if self.direct:
                return [("double", over_side), ("swap", over_core)]
            return [("stack", over_side), ("stack", over_core)]

        def parts(self, flow):
            made, edges = [], [0, self.left, sum(self.cols)]
            for n, ways in enumerate(self.ways):
                value = flow.value[:, :, edges[n] : edges[n + 1]]
                half = value.shape[0] // 2
                made.append(
                    Flow((value[:half], value[half:]), [("halve", way) for way in ways[:3]])
                )
            return made

        def rest(self, made):
            value = jnp.concatenate([flow.value for flow in made], axis=2)
            half = value.shape[0] // 2
            steps = [("halve", way) for way in self.others] + self.ends()
            return Flow((value[:half], value[half:]), steps)

        def shares(self, widths, value, got=None):
            ca, cb = self.cols
            if not self.direct:
                value = value[:, :, 0].astype(F32)
                a = value[..., :ca].transpose(2, 0, 1, 3).reshape(self.rows, 4 * ca)
                b = value[..., ca:].reshape(2, 2, self.rows, cb // self.size, self.size)
                b = b.transpose(0, 1, 3, 2, 4).reshape(width, self.size)
                edges = [sum(widths[:n]) for n in range(len(widths) + 1)]
                return [a[:, low:high] for low, high in zip(edges, edges[1:])] + [b.T]
            outs = [(typed((self.rows, count), F32), VMEM) for count in widths]
            outs.append((typed((self.size, width), F32), VMEM))
            return kernel_of(
                functools.partial(shares_kernel, widths, ca),
                "shares",
                [SMEM] + [VMEM] * 2,
                outs,
                [pltpu.VMEM((width, self.size), F32)],
                0,
            )(jnp.stack([core, side]), value, got)

    up_along = [("shard", bit) for bit in net.shard_bits]
    grad_mlp = Grad(shape_gate, (width, ff), (2 * ff + ff) // 8)
    grad_attn = Grad(shape_qkv, (width, heads * hd), (qkv + heads * hd) // 4)

    in_v = lambda count: [VMEM] * count
    in_s = lambda count: [SMEM] * count
    out_v = lambda *types: [(typed(*one), VMEM) for one in types]
    sems = lambda count: pltpu.SemaphoreType.DMA((count,))
    reach = min(length, WINDOW + QB)
    bf = lambda *shape: (shape, BF16)
    f32 = lambda *shape: (shape, F32)

    seg_rows = segment_ids.reshape(length, 1)
    seg_cols = segment_ids.reshape(1, length)
    flows = [flow_left, flow_right]
    got, _ = net.launch(flows)
    land([flow_qkv], core_got)
    weight_qkv = weight(shape_qkv, [(flow_qkv, place)])
    steps = (length // QB,)
    outs = land(
        flows,
        got,
        kernel_of(
            functools.partial(project_kernel, weight_qkv, heads),
            "project",
            weight_qkv.specs
            + [by_rows(width), by_rows(hd // 2), by_rows(hd // 2)]
            + [all_of(1, width), all_of(1, hd), all_of(1, hd)],
            [
                (typed((length, width), BF16), by_rows(width)),
                (typed((length, heads * hd), BF16), by_rows(heads * hd)),
                (typed((length, hd), BF16), by_rows(hd)),
                (typed((length, hd), BF16), by_rows(hd)),
                (
                    typed((heads, length, hd), BF16),
                    pl.BlockSpec((heads, QB, hd), lambda i: (0, i, 0)),
                ),
                (typed((length, hd), BF16), by_rows(hd)),
            ],
            weight_qkv.scratch,
            2 * length * width * qkv,
            grid=steps,
        )(*weight_qkv.operands, inputs, cos, sin, gai, gq, gk),
    )
    normed, qraw, kraw, values, queries, keys = outs
    probs, mixed = advance(
        net,
        [flow_left, flow_right],
        kernel_of(
            attend_kernel,
            "attend",
            in_v(5),
            [(typed((heads, length, reach), BF16), ANY)] + out_v(bf(length, heads * hd)),
            [pltpu.VMEM((heads, length, reach), BF16), sems(length // QB)],
            4 * length * heads * hd * reach,
        ),
        [seg_rows, seg_cols, queries, keys, values],
    )

    finish(net, [flow_left, flow_right, flow_rows])
    high, low = w_out.shape[0] // 2, w_down.shape[0] // 2
    weight_out = weight_rows(shape_out, flow_rows, 0, high)
    weight_down = weight_rows(shape_down, flow_rows, high, low)
    weight_gate = weight(shape_gate, [(flow_left, place_left), (flow_right, place_right)])
    output, dmiddle, dbranch, ggain_mlp, *ends = kernel_of(
        functools.partial(mlp_kernel, weight_out, weight_down, weight_gate, grad_mlp.cuts),
        "mlp",
        weight_out.specs + weight_down.specs + weight_gate.specs + in_s(2) + in_v(5) + [ANY],
        [
            (typed((length, width), BF16), ANY),
            (typed((length, width), F32), ANY),
            (typed((length, width), BF16), VMEM),
            (typed((3, width), F32), VMEM),
        ]
        + grad_mlp.outs,
        weight_out.scratch
        + weight_down.scratch
        + weight_gate.scratch
        + [
            pltpu.VMEM((length, width), BF16),
            pltpu.VMEM((length, width), BF16),
            pltpu.VMEM((length, width), BF16),
            pltpu.VMEM((length, ff), BF16),
            pltpu.VMEM((length, 2 * ff), BF16),
            pltpu.VMEM((length, width), BF16),
            pltpu.VMEM((width, ff), BF16),
            pltpu.VMEM(shape_gate, BF16),
            pltpu.VMEM((length, width), F32),
            pltpu.VMEM((length, width), BF16),
            sems(3),
            grad_mlp.sems,
        ],
        2 * length * width * (9 * ff + heads * hd),
    )(
        *weight_out.operands, *weight_down.operands, *weight_gate.operands, *grad_mlp.operands,
        mixed, inputs, gao, gmi, gmo, out_grad,
    )
    back_mlp = grad_mlp.flow(*ends)
    dmixed, gout = advance(
        net,
        [back_mlp],
        kernel_of(
            functools.partial(out_bwd_kernel, weight_out, heads),
            "out_bwd",
            weight_out.specs + in_v(2),
            out_v(bf(heads, length, hd), bf(width, heads * hd)),
            weight_out.scratch,
            4 * length * heads * hd * width,
        ),
        [*weight_out.operands, dbranch, mixed],
    )
    back_mlp = grad_mlp.parts(back_mlp)
    draw, ggain_qk, *ends = advance(
        net,
        back_mlp,
        kernel_of(
            functools.partial(attn_bwd_kernel, grad_attn.cuts),
            "attn_bwd",
            in_s(2) + in_v(12) + [ANY],
            out_v(bf(length, qkv), f32(2, hd)) + grad_attn.outs,
            [
                pltpu.VMEM((heads, length, reach), BF16),
                sems(length // QB),
                pltpu.VMEM((heads, QB, reach), BF16),
                pltpu.VMEM((length, heads * hd), F32),
                pltpu.VMEM((hd, length), F32),
                pltpu.VMEM((hd, length), F32),
                pltpu.VMEM(shape_qkv, BF16),
                grad_attn.sems,
            ],
            2 * length * (width * qkv + 4 * heads * hd * reach),
        ),
        [
            *grad_attn.operands, dmixed, queries, keys, values, qraw, kraw, normed, cos, sin, gq,
            gk, gout, probs,
        ],
    )
    back_attn = grad_attn.flow(*ends)
    flows = [back_attn, *back_mlp]
    got, (draw,) = net.launch(flows, [draw])
    land(flows[:1], got[:1])
    more, (draw,) = net.launch([back_attn], [draw])
    input_grad, ggain_in = land(
        [*back_mlp, back_attn],
        got[1:] + more,
        kernel_of(
            functools.partial(input_bwd_kernel, weight_qkv),
            "input_bwd",
            weight_qkv.specs + [by_rows(qkv), by_rows(width), by_rows(width), all_of(1, width)],
            [
                (typed((length, width), F32), by_rows(width)),
                (typed((1, width), F32), all_of(1, width)),
            ],
            weight_qkv.scratch,
            2 * length * width * qkv,
            grid=steps,
        )(*weight_qkv.operands, draw, dmiddle, inputs, gai),
    )
    sums = jnp.concatenate(
        [ggain_in, ggain_mlp[2:3], ggain_mlp[1:2], ggain_mlp[0:1], ggain_qk[0:1], ggain_qk[1:2]],
        axis=1,
    )
    sums = Flow(sums.reshape(-1, 128), [("total", way) for way in [over_core, over_side] + along])
    advance(net, [*back_mlp, back_attn, sums])
    back_mlp = grad_mlp.rest(back_mlp)
    while back_mlp.steps:
        advance(net, [back_mlp, back_attn, sums])
    finish(net, [back_attn, sums], 1)
    full_gate, full_up, full_down = advance(
        net,
        [back_attn, sums],
        functools.partial(grad_mlp.shares, (ff, ff)),
        [back_mlp.value] + ([back_mlp.got] if grad_mlp.direct else []),
    )
    full_query, full_key, full_value, full_out = grad_attn.shares(
        (heads * hd, hd, hd), back_attn.value, getattr(back_attn, "got", None)
    )
    sums = sums.value.reshape(-1)

    shard = lax.axis_index("shard")
    grads, at = [], 0
    for scale in scales:
        size = scale.shape[0]
        grads.append(lax.dynamic_slice_in_dim(sums, at + shard * size, size, 0))
        at += size * shards
    return (
        output,
        input_grad,
        full_query,
        full_key,
        full_value,
        full_out,
        full_gate,
        full_up,
        full_down,
        grads[0],
        grads[4],
        grads[5],
        grads[1],
        grads[2],
        grads[3],
    )


def solution(mesh):
    rows, vector = P("shard", None), P("shard")
    tokens = P(AXES, None)
    return jax.shard_map(
        functools.partial(layer, Net(mesh)),
        mesh=mesh,
        in_specs=(tokens, P(AXES), tokens) + (rows,) * 7 + (vector,) * 6,
        out_specs=(tokens, tokens) + (rows,) * 7 + (vector,) * 6,
        check_vma=False,
    )
```

```python
import functools
import math

import jax
import jax.numpy as jnp
from jax import lax
from jax.experimental import pallas as pl
from jax.experimental.pallas import tpu as pltpu
from jax.sharding import PartitionSpec as P

WINDOW = 512
EPSILON = 1e-06
NEG = -1e30
QB = 256
RB = 512
CB = 512
GB = 1024
AXES = ("replica", "shard")
F32 = jnp.float32
BF16 = jnp.bfloat16
GELU_C = math.sqrt(2.0 / math.pi)


def flip_pairs(reps, shards, axis, bit):
    pairs = []
    for rep in range(reps):
        for shard in range(shards):
            rep_to = rep ^ bit if axis == "replica" else rep
            shard_to = shard ^ bit if axis == "shard" else shard
            pairs.append((rep * shards + shard, rep_to * shards + shard_to))
    return pairs


class Net:
    def __init__(self, mesh):
        self.reps = mesh.shape["replica"]
        self.shards = mesh.shape["shard"]
        self.shard_bits = [1 << i for i in range(self.shards.bit_length() - 1)]
        self.rep_bits = [1 << i for i in range(self.reps.bit_length() - 1)]
        assert 1 << len(self.shard_bits) == self.shards
        assert self.reps == 4

    def swap(self, value, axis, bit):
        return lax.ppermute(value, AXES, flip_pairs(self.reps, self.shards, axis, bit))

    def launch(self, flows, args=()):
        moves = [flow.move() for flow in flows]
        values, args = lax.optimization_barrier(([value for value, _ in moves], list(args)))
        return [self.swap(value, *way) for value, (_, way) in zip(values, moves)], args


def add_up(value, got):
    return (value.astype(F32) + got.astype(F32)).astype(BF16)


def in_order(value, got, axis, bit, dim):
    first = (lax.axis_index(axis) & bit) == 0
    return jnp.concatenate([jnp.where(first, value, got), jnp.where(first, got, value)], axis=dim)


class Flow:
    def __init__(self, value, steps):
        self.value = value
        self.steps = list(steps)

    def move(self):
        if self.steps[0][0] == "halve":
            return self.value[1], self.steps[0][1]
        return self.value, self.steps[0][1]

    def take(self, got):
        kind, way = self.steps[0][:2]
        value = self.value
        if kind == "double":
            self.value = jnp.concatenate([value, got], axis=0)
        elif kind == "swap":
            self.got = got
        elif kind == "halve":
            near = value[0]
            if len(self.steps) > 1 and self.steps[1][0] == "halve":
                half = near.shape[0] // 2
                self.value = (add_up(near[:half], got[:half]), add_up(near[half:], got[half:]))
            else:
                self.value = add_up(near, got)
        elif kind == "total":
            self.value = value + got
        else:
            self.value = in_order(value[None], got[None], *way, 0)
        self.steps = self.steps[1:]


def land(flows, got, outs=()):
    got, outs = lax.optimization_barrier((got, outs))
    for flow, value in zip(flows, got):
        flow.take(value)
    return outs


def advance(net, flows, work=None, args=()):
    flows = [flow for flow in flows if flow.steps]
    got, args = net.launch(flows, args)
    return land(flows, got, work(*args) if work is not None else ())


def finish(net, flows, left=0):
    while any(len(flow.steps) > left for flow in flows):
        advance(net, [flow for flow in flows if len(flow.steps) > left])


def places(stages, parts):
    rep = lax.axis_index("replica")
    shard = lax.axis_index("shard")
    shards = 1
    for axis, bit in stages:
        shards *= 2 if axis == "shard" else 1
    count = 1 << len(parts)
    part = jnp.arange(count, dtype=jnp.int32)[:, None]
    block = jnp.arange(shards, dtype=jnp.int32)[None, :]
    part_rep = jnp.zeros_like(part)
    for i, bit in enumerate(parts):
        part_rep = part_rep + ((part >> (len(parts) - 1 - i)) & 1) * bit
    rep_diff = part_rep ^ rep
    shard_diff = block ^ shard
    where = jnp.zeros((count, shards), jnp.int32)
    for axis, bit in stages:
        diff = rep_diff if axis == "replica" else shard_diff
        where = where * 2 + jnp.where((diff & bit) != 0, 1, 0)
    return where.reshape(-1)


def dot(left, right):
    return jnp.dot(left, right, preferred_element_type=F32)


def dot_nt(left, right):
    return lax.dot_general(left, right, (((1,), (1,)), ((), ())), preferred_element_type=F32)


def dot_tn(left, right):
    return lax.dot_general(left, right, (((0,), (0,)), ((), ())), preferred_element_type=F32)


def inv_rms(value):
    return lax.rsqrt(jnp.mean(value * value, axis=-1, keepdims=True) + EPSILON)


def norm_back(grad, unit, inv, gain):
    scaled = grad * gain
    return inv * (scaled - unit * jnp.mean(scaled * unit, axis=-1, keepdims=True))


def rows_of(index, size):
    return pl.ds(pl.multiple_of(index * size, size), size)


def start_all(copies):
    for copy in copies:
        copy.start()


def wait_all(copies):
    for copy in copies:
        copy.wait()


def on_first(copies):
    @pl.when(pl.program_id(0) == 0)
    def _():
        start_all(copies)
        wait_all(copies)


def project_kernel(weight_qkv, heads, *refs):
    refs_qkv, refs = split(refs, len(weight_qkv.specs))
    (
        x_ref, cos_ref, sin_ref, gai_ref, gq_ref, gk_ref,
        normed_ref, qraw_ref, kraw_ref, v_ref, q_ref, k_ref,
        wqkv, sem_qkv,
    ) = refs
    hd = k_ref.shape[1]
    half = hd // 2
    factor = hd ** (-0.5)
    on_first(weight_qkv.copies(refs_qkv, wqkv, sem_qkv))
    x = x_ref[...].astype(F32)
    normed = (x * inv_rms(x) * gai_ref[...]).astype(BF16)
    normed_ref[...] = normed
    cos, sin = cos_ref[...], sin_ref[...]

    def turn(value):
        first, second = value[:, :half], value[:, half:]
        return jnp.concatenate([first * cos - second * sin, second * cos + first * sin], axis=1)

    for h in range(heads):
        raw = dot(normed, wqkv[:, h * hd : (h + 1) * hd])
        qraw_ref[:, h * hd : (h + 1) * hd] = raw.astype(BF16)
        q_ref[h, :, :] = (turn(raw * inv_rms(raw) * gq_ref[...]) * factor).astype(BF16)
    raw = dot(normed, wqkv[:, heads * hd : (heads + 1) * hd])
    kraw_ref[...] = raw.astype(BF16)
    k_ref[...] = turn(raw * inv_rms(raw) * gk_ref[...]).astype(BF16)
    v_ref[...] = dot(normed, wqkv[:, (heads + 1) * hd :]).astype(BF16)


def attend_kernel(
    segr_ref, segc_ref, q_ref, k_ref, v_ref, probs_hbm, mixed_ref, probs_all, sem_probs
):
    heads, length, hd = q_ref.shape
    out_probs = probs_copies(probs_hbm, probs_all, sem_probs, True)
    for b in range(length // QB):
        low, high = key_range(b)
        width = high - low
        rows = slice(b * QB, high)
        seg_q, seg_k = segr_ref[rows, :], segc_ref[:, low:high]
        offset = (
            lax.broadcasted_iota(jnp.int32, (QB, width), 0)
            - lax.broadcasted_iota(jnp.int32, (QB, width), 1)
            + (b * QB - low)
        )
        allowed = (seg_q == seg_k) & (seg_q >= 0) & (offset >= 0) & (offset < WINDOW)
        allowed = allowed | (offset == 0)
        keys, vals = k_ref[low:high, :], v_ref[low:high, :]
        for h in range(heads):
            scores = jnp.where(allowed, dot_nt(q_ref[h, rows, :], keys), NEG)
            expo = jnp.exp(scores - jnp.max(scores, axis=1, keepdims=True))
            probs = (expo * (1.0 / jnp.sum(expo, axis=1, keepdims=True))).astype(BF16)
            probs_all[h, rows, 0:width] = probs
            mixed_ref[rows, h * hd : (h + 1) * hd] = dot(probs, vals).astype(BF16)
        out_probs[b].start()
    wait_all(out_probs)


def cut_at(cut, which):
    (row, rows, row_step), (col, cols, col_step) = cut
    if row_step:
        row = pl.multiple_of(row + which * row_step, 16)
    if col_step:
        col = pl.multiple_of(col + which * col_step, 128)
    return pl.ds(row, rows), pl.ds(col, cols)


class Weight:
    def __init__(self, shape, matrix=None, rows=(), core=None, pieces=(), source=0):
        self.shape, self.rows, self.source = shape, rows, source
        self.cuts = [cuts for _, cuts, _, _ in pieces]
        if matrix is not None:
            self.operands, self.specs, count = [matrix], [ANY], len(rows)
        else:
            self.operands, self.specs, count = [core], [SMEM], 0
            for place, cuts, own, got in pieces:
                self.operands += [place, own, got]
                self.specs += [SMEM, ANY, ANY]
                count += 2 * len(cuts)
        self.scratch = [pltpu.VMEM(shape, BF16), pltpu.SemaphoreType.DMA((count,))]

    def copies(self, refs, mat, sem):
        made = []
        for source, to, count in self.rows:
            src, dst = refs[0].at[pl.ds(source, count), :], mat.at[pl.ds(to, count), :]
            made.append(pltpu.make_async_copy(src, dst, sem.at[len(made)]))
        for piece, cuts in enumerate(self.cuts):
            core = refs[0][0]
            place, own, got = refs[3 * piece + 1 : 3 * piece + 4]
            for n, cut in enumerate(cuts):
                for hbm, which in ((own, core), (got, 1 - core)):
                    src = hbm.at[place[n], pl.ds(self.source, cut[0][1]), :]
                    dst = mat.at[cut_at(cut, which)]
                    made.append(pltpu.make_async_copy(src, dst, sem.at[len(made)]))
        return made


def grad_copies(cuts, refs, mats, sem):
    core_ref, places_ref, near, far = refs
    if not cuts:
        return [pltpu.make_async_copy(m, o, sem.at[i]) for i, (m, o) in enumerate(zip(mats, (near, far)))]
    core, made = core_ref[0], []
    for mat, cut, which_place, n, col in cuts:
        for hbm, which in ((far, 1 - core), (near, core)):
            src = mats[mat].at[cut_at(cut, which)]
            dst = hbm.at[places_ref[which_place, n], :, pl.ds(col, cut[1][1])]
            made.append(pltpu.make_async_copy(src, dst, sem.at[len(made)]))
    return made


def split(refs, *counts):
    parts, at = [], 0
    for count in counts:
        parts.append(refs[at : at + count])
        at += count
    return parts + [refs[at:]]


def mlp_kernel(weight_out, weight_down, weight_gate, cuts_grad, *refs):
    refs_out, refs_down, refs_gate, to_grad, refs = split(
        refs, len(weight_out.specs), len(weight_down.specs), len(weight_gate.specs), 2
    )
    (
        mixed_ref, x_ref, gao_ref, gmi_ref, gmo_ref, top_hbm,
        output_hbm, dmiddle_hbm, dbranch_ref, ggain_ref, near, far,
        wout, sem_out, wdown, sem_down, wgu, sem_gate,
        top_ref, branch_ref, inner_ref, hidden, dgu, ddown, gdown, ggate, middle_ref, output_ref,
        sem, sem_grad,
    ) = refs
    length, ff = hidden.shape
    in_out = weight_out.copies(refs_out, wout, sem_out)
    in_gate = weight_gate.copies(refs_gate, wgu, sem_gate)
    in_down = weight_down.copies(refs_down, wdown, sem_down)
    in_top = pltpu.make_async_copy(top_hbm, top_ref, sem.at[0])
    start_all(in_out)
    start_all(in_gate)
    start_all(in_down)
    in_top.start()
    ggain_ref[...] = jnp.zeros_like(ggain_ref)
    wait_all(in_out)

    def attn_out(i, carry):
        rows = rows_of(i, QB)
        branch = dot(mixed_ref[rows, :], wout[...])
        branch_ref[rows, :] = branch.astype(BF16)
        middle = x_ref[rows, :].astype(F32) + branch * inv_rms(branch) * gao_ref[...]
        middle_ref[rows, :] = middle
        inner_ref[rows, :] = (middle * inv_rms(middle) * gmi_ref[...]).astype(BF16)
        return carry

    lax.fori_loop(0, length // QB, attn_out, 0)
    wait_all(in_gate)

    def forward(i, carry):
        rows = rows_of(i, RB)
        inner = inner_ref[rows, :]
        for c in range(ff // CB):
            cols = slice(c * CB, (c + 1) * CB)
            more = slice(ff + c * CB, ff + (c + 1) * CB)
            gate = dot(inner, wgu[:, cols])
            up = dot(inner, wgu[:, more])
            square = gate * gate
            tanh = jnp.tanh(gate * (GELU_C + (GELU_C * 0.044715) * square))
            base = 0.5 + 0.5 * tanh
            act = gate * base
            slope = base + (0.5 * gate) * (1.0 - tanh * tanh) * (
                GELU_C + (3.0 * GELU_C * 0.044715) * square
            )
            hidden[rows, cols] = (act * up).astype(BF16)
            dgu[rows, cols] = (slope * up).astype(BF16)
            dgu[rows, more] = act.astype(BF16)
        return carry

    lax.fori_loop(0, length // RB, forward, 0)
    wait_all(in_down)
    in_top.wait()

    def down_row(i, carry):
        rows = rows_of(i, RB)
        down = dot(hidden[rows, :], wdown[...])
        inv = inv_rms(down)
        unit = down * inv
        output_ref[rows, :] = (middle_ref[rows, :] + unit * gmo_ref[...]).astype(BF16)
        top = top_ref[rows, :].astype(F32)
        ddown[rows, :] = norm_back(top, unit, inv, gmo_ref[...]).astype(BF16)
        ggain_ref[0:1, :] += jnp.sum(top * unit, axis=0, keepdims=True)
        return carry

    lax.fori_loop(0, length // RB, down_row, 0)
    out_output = pltpu.make_async_copy(output_ref, output_hbm, sem.at[1])
    out_output.start()

    def down_grad(i, carry):
        cols = rows_of(i, GB)
        gdown[:, cols] = dot_tn(ddown[...], hidden[:, cols]).astype(BF16)
        return carry

    lax.fori_loop(0, ff // GB, down_grad, 0)

    def hidden_back(i, carry):
        rows = rows_of(i, RB)
        grad = ddown[rows, :]
        for c in range(ff // CB):
            cols = slice(c * CB, (c + 1) * CB)
            more = slice(ff + c * CB, ff + (c + 1) * CB)
            dhid = dot_nt(grad, wdown[cols, :])
            dgu[rows, cols] = (dhid * dgu[rows, cols].astype(F32)).astype(BF16)
            dgu[rows, more] = (dhid * dgu[rows, more].astype(F32)).astype(BF16)
        return carry

    lax.fori_loop(0, length // RB, hidden_back, 0)

    def gate_grad(i, carry):
        cols = rows_of(i, GB)
        ggate[:, cols] = dot_tn(inner_ref[...], dgu[:, cols]).astype(BF16)
        return carry

    lax.fori_loop(0, 2 * ff // GB, gate_grad, 0)
    out_grad = grad_copies(cuts_grad, (*to_grad, near, far), (ggate, gdown), sem_grad)
    start_all(out_grad)

    def inner_back(i, carry):
        rows = rows_of(i, RB)
        dinner = dot_nt(dgu[rows, :], wgu[...])
        middle = middle_ref[rows, :]
        inv = inv_rms(middle)
        unit = middle * inv
        dmid = top_ref[rows, :].astype(F32) + norm_back(dinner, unit, inv, gmi_ref[...])
        middle_ref[rows, :] = dmid
        ggain_ref[1:2, :] += jnp.sum(dinner * unit, axis=0, keepdims=True)
        branch = branch_ref[rows, :].astype(F32)
        inv = inv_rms(branch)
        unit = branch * inv
        dbranch_ref[rows, :] = norm_back(dmid, unit, inv, gao_ref[...]).astype(BF16)
        ggain_ref[2:3, :] += jnp.sum(dmid * unit, axis=0, keepdims=True)
        return carry

    lax.fori_loop(0, length // RB, inner_back, 0)
    out_middle = pltpu.make_async_copy(middle_ref, dmiddle_hbm, sem.at[2])
    out_middle.start()
    out_output.wait()
    wait_all(out_grad)
    out_middle.wait()


def out_bwd_kernel(weight_out, heads, *refs):
    refs_out, refs = split(refs, len(weight_out.specs))
    dbranch_ref, mixed_ref, dmixed_ref, gout_ref, wout, sem_out = refs
    length = mixed_ref.shape[0]
    hd = dmixed_ref.shape[2]
    in_out = weight_out.copies(refs_out, wout, sem_out)
    start_all(in_out)

    def weights_out(i, carry):
        cols = rows_of(i, CB)
        gout_ref[:, cols] = dot_tn(dbranch_ref[...], mixed_ref[:, cols]).astype(BF16)
        return carry

    lax.fori_loop(0, heads * hd // CB, weights_out, 0)
    wait_all(in_out)

    def mixed_back(i, carry):
        rows = rows_of(i, QB)
        for h in range(heads):
            cols = slice(h * hd, (h + 1) * hd)
            dmixed_ref[h, rows, :] = dot_nt(dbranch_ref[rows, :], wout[cols, :]).astype(BF16)
        return carry

    lax.fori_loop(0, length // QB, mixed_back, 0)


def turn_back(value, cos, sin):
    half = value.shape[1] // 2
    first, second = value[:, :half], value[:, half:]
    return jnp.concatenate([first * cos + second * sin, second * cos - first * sin], axis=1)


def key_range(b):
    return max(0, b - WINDOW // QB) * QB, (b + 1) * QB


def probs_copies(probs_hbm, probs, sem, outward):
    made = []
    for b in range(probs.shape[1] // QB):
        low, high = key_range(b)
        at = (slice(None), slice(b * QB, high), slice(0, high - low))
        far, near = probs_hbm.at[at], probs.at[at]
        src, dst = (near, far) if outward else (far, near)
        made.append(pltpu.make_async_copy(src, dst, sem.at[b]))
    return made


def attn_bwd_kernel(cuts_grad, *refs):
    (
        core_ref, places_ref, dmixed_ref, q_ref, k_ref, v_ref,
        cos_ref, sin_ref, gq_ref, gk_ref, qraw_hbm, kraw_hbm, normed_hbm, gout_hbm, probs_hbm,
        draw_ref, ggain_ref, near, far,
        probs_all, sem_probs, ds, dq, dk, dv, gqkv, sem_grad,
        qraw_ref, kraw_ref, normed_ref, gout, sem_late,
    ) = refs
    heads, length, hd = q_ref.shape
    factor = hd ** (-0.5)
    in_probs = probs_copies(probs_hbm, probs_all, sem_probs, False)
    start_all(in_probs)
    late = ((gout_hbm, gout), (qraw_hbm, qraw_ref), (kraw_hbm, kraw_ref), (normed_hbm, normed_ref))
    in_late = [pltpu.make_async_copy(*pair, sem_late.at[n]) for n, pair in enumerate(late)]
    start_all(in_late)
    out_grad = grad_copies(cuts_grad, (core_ref, places_ref, near, far), (gqkv, gout), sem_grad)
    early = [cut[0] == 1 for cut in cuts_grad for _ in range(2)] or [False, True]
    dk[...] = jnp.zeros_like(dk)
    dv[...] = jnp.zeros_like(dv)
    for b in range(length // QB):
        low, high = key_range(b)
        width = high - low
        rows = slice(b * QB, high)
        in_probs[b].wait()
        keys, vals = k_ref[low:high, :], v_ref[low:high, :]
        for h in range(heads):
            probs = probs_all[h, rows, 0:width].astype(F32)
            dprobs = dot_nt(dmixed_ref[h, rows, :], vals)
            inner = jnp.sum(probs * dprobs, axis=1, keepdims=True)
            dscores = (probs * (dprobs - inner)).astype(BF16)
            ds[h, :, 0:width] = dscores
            dq[rows, h * hd : (h + 1) * hd] = dot(dscores, keys) * factor
        stack = lambda value: value.reshape(heads * QB, value.shape[2])
        dk[:, low:high] += dot_tn(stack(q_ref[:, rows, :]), stack(ds[:, :, 0:width]))
        dv[:, low:high] += dot_tn(
            stack(dmixed_ref[:, rows, :]), stack(probs_all[:, rows, 0:width])
        )

    ggain_ref[...] = jnp.zeros_like(ggain_ref)
    wait_all(in_late)
    start_all([copy for copy, first in zip(out_grad, early) if first])

    def raw_back(i, carry):
        rows = rows_of(i, QB)
        cos, sin = cos_ref[rows, :], sin_ref[rows, :]
        total = jnp.zeros((1, hd), F32)
        for h in range(heads):
            cols = slice(h * hd, (h + 1) * hd)
            grad = turn_back(dq[rows, cols], cos, sin)
            raw = qraw_ref[rows, cols].astype(F32)
            inv = inv_rms(raw)
            unit = raw * inv
            draw_ref[rows, cols] = norm_back(grad, unit, inv, gq_ref[...]).astype(BF16)
            total += jnp.sum(grad * unit, axis=0, keepdims=True)
        ggain_ref[0:1, :] += total
        grad = turn_back(dk[:, rows].T, cos, sin)
        raw = kraw_ref[rows, :].astype(F32)
        inv = inv_rms(raw)
        unit = raw * inv
        draw_ref[rows, heads * hd : (heads + 1) * hd] = norm_back(
            grad, unit, inv, gk_ref[...]
        ).astype(BF16)
        ggain_ref[1:2, :] += jnp.sum(grad * unit, axis=0, keepdims=True)
        draw_ref[rows, (heads + 1) * hd :] = dv[:, rows].T.astype(BF16)
        return carry

    lax.fori_loop(0, length // QB, raw_back, 0)

    def weights(i, carry):
        cols = rows_of(i, CB)
        gqkv[:, cols] = dot_tn(normed_ref[...], draw_ref[:, cols]).astype(BF16)
        return carry

    lax.fori_loop(0, gqkv.shape[1] // CB, weights, 0)
    start_all([copy for copy, first in zip(out_grad, early) if not first])
    wait_all(out_grad)


def input_bwd_kernel(weight_qkv, *refs):
    refs_qkv, refs = split(refs, len(weight_qkv.specs))
    draw_ref, dmiddle_ref, x_ref, gai_ref, dx_ref, ggain_ref, wqkv, sem_qkv = refs
    on_first(weight_qkv.copies(refs_qkv, wqkv, sem_qkv))

    @pl.when(pl.program_id(0) == 0)
    def _():
        ggain_ref[...] = jnp.zeros_like(ggain_ref)

    dnormed = dot_nt(draw_ref[...], wqkv[...])
    x = x_ref[...].astype(F32)
    inv = inv_rms(x)
    unit = x * inv
    dx_ref[...] = dmiddle_ref[...] + norm_back(dnormed, unit, inv, gai_ref[...])
    ggain_ref[...] += jnp.sum(dnormed * unit, axis=0, keepdims=True)


def shares_kernel(widths, ca, me_ref, value_ref, got_ref, *refs):
    *a_refs, b_ref, turned = refs
    core, side = me_ref[0], me_ref[1]
    rows, size = value_ref.shape[1], turned.shape[1]
    pieces = (value_ref.shape[2] - ca) // size
    for c in range(2):
        for s in range(2):
            n = 2 * c + s
            at = jnp.bitwise_xor(side, s)
            own, got = value_ref[at].astype(F32), got_ref[at].astype(F32)
            block = jnp.where(core == c, own, got)
            low = 0
            for ref, count in zip(a_refs, widths):
                first, last = max(low, n * ca), min(low + count, (n + 1) * ca)
                if first < last:
                    ref[:, first - low : last - low] = block[:, first - n * ca : last - n * ca]
                low += count
            for j in range(pieces):
                row = (n * pieces + j) * rows
                turned[row : row + rows, :] = block[:, ca + j * size : ca + (j + 1) * size]
    b_ref[...] = turned[...].T


VMEM = pl.BlockSpec(memory_space=pltpu.VMEM)
SMEM = pl.BlockSpec(memory_space=pltpu.SMEM)
ANY = pl.BlockSpec(memory_space=pl.ANY)


def by_rows(width):
    return pl.BlockSpec((QB, width), lambda i: (i, 0))


def all_of(*shape):
    return pl.BlockSpec(shape, lambda i: (0,) * len(shape))


VMEM_MIB = {"out_bwd": 24, "attn_bwd": 44, "input_bwd": 24, "shares": 12}


def kernel_of(body, name, in_specs, outs, scratch, flops, **more):
    def run(*operands):
        total = 0
        for value in list(operands) + [value for value, _ in outs]:
            total += math.prod(value.shape) * value.dtype.itemsize
        return pl.pallas_call(
            body,
            name=name,
            out_shape=[value for value, _ in outs],
            in_specs=in_specs,
            out_specs=[spec for _, spec in outs],
            scratch_shapes=scratch,
            compiler_params=pltpu.CompilerParams(
                vmem_limit_bytes=VMEM_MIB.get(name, 56) << 20
            ),
            cost_estimate=pl.CostEstimate(flops=flops, bytes_accessed=total, transcendentals=0),
            **more,
        )(*operands)

    return run


def typed(shape, dtype):
    return jax.ShapeDtypeStruct(shape, dtype)


def positions(seg):
    length = seg.shape[0]
    index = jnp.arange(length, dtype=jnp.int32)
    previous = jnp.concatenate([jnp.full((1,), -3, jnp.int32), seg[:-1]])
    starts = jnp.where(seg != previous, index, jnp.zeros_like(index))
    return index - lax.cummax(starts, axis=0)


def rope_angles(position, head_dim):
    half = head_dim // 2
    freqs = 10000.0 ** (-2.0 * jnp.arange(half, dtype=F32) / head_dim)
    return position.astype(F32)[:, None] * freqs[None, :]


def layer(
    net,
    inputs,
    segment_ids,
    out_grad,
    w_query,
    w_key,
    w_value,
    w_out,
    w_gate,
    w_up,
    w_down,
    scale_attn_in,
    scale_query,
    scale_key,
    scale_attn_out,
    scale_mlp_in,
    scale_mlp_out,
):
    length, width = inputs.shape
    hd = w_key.shape[1]
    heads = w_query.shape[1] // hd
    qkv = (heads + 2) * hd
    ff = w_gate.shape[1]
    shards = net.shards
    rep = lax.axis_index("replica")
    core = rep & 1
    side = (rep >> 1) & 1

    along = [("shard", bit) for bit in reversed(net.shard_bits)]
    over_core, over_side = ("replica", 1), ("replica", 2)
    doubles = lambda ways: [("double", way) for way in ways]

    def half_rows(value, index, parts):
        size = value.shape[0] // parts
        return lax.dynamic_slice_in_dim(value, index * size, size, 0)

    def half_cols(value, index, parts):
        size = value.shape[1] // parts
        return lax.dynamic_slice_in_dim(value, index * size, size, 1)

    path_left = along + [over_side]
    path_right = along[:-1] + [over_side, along[-1]]
    scales = (scale_attn_in, scale_attn_out, scale_mlp_in, scale_mlp_out, scale_query, scale_key)
    shape_qkv, shape_out = (width, qkv), (heads * hd, width)
    shape_gate, shape_down = (width, 2 * ff), (ff, width)
    last = [("swap", over_core)]

    angles = rope_angles(positions(segment_ids), hd)
    half = qkv // 2
    rows_qkv = w_query.shape[0]
    key_at, value_at = heads * hd - half, heads * hd + hd - half
    second = jnp.pad(w_query[:, half:], ((0, 0), (0, qkv - heads * hd)))
    second += jnp.pad(w_key, ((0, 0), (key_at, half - key_at - hd)))
    second += jnp.pad(w_value, ((0, 0), (value_at, half - value_at - hd)))
    own_qkv = jnp.where(core == 0, w_query[:, :half], second)
    own_qkv = jnp.pad(own_qkv, ((0, 16), (0, 0)))
    at = 0
    for scale in scales:
        size = scale.shape[0]
        own_qkv += jnp.pad(scale[None, :], ((rows_qkv, 15), (at, half - at - size)))
        at += -(-size // 128) * 128
    flow_qkv = Flow(own_qkv[None], doubles(along) + last)
    own_gate = half_cols(jnp.where(core == 0, w_gate, w_up), side, 2)[None]
    flow_gate = Flow(own_gate, doubles(along[:-1]))
    own_rows = jnp.concatenate([half_rows(w_out, core, 2), half_rows(w_down, core, 2)], axis=0)
    cos, sin = advance(net, [flow_qkv], lambda a: (jnp.cos(a), jnp.sin(a)), [angles])
    finish(net, [flow_qkv], 3)
    advance(net, [flow_qkv, flow_gate])
    flow_rows = Flow(lax.all_gather(own_rows[None], "shard", axis=0, tiled=True), last)
    finish(net, [flow_qkv, flow_gate], 2)
    finish(net, [flow_gate], 1)
    flows = [flow_qkv, flow_gate]
    got, _ = net.launch(flows)
    land(flows[:1], got[:1])
    core_got, _ = net.launch(flows[:1])
    land(flows[1:], got[1:])
    half = flow_gate.value.shape[2] // 2
    flow_left = Flow(
        flow_gate.value[:, :, :half], doubles(path_left[len(along) - 1 :]) + last
    )
    flow_right = Flow(
        flow_gate.value[:, :, half:], doubles(path_right[len(along) - 1 :]) + last
    )
    place = places(along[::-1], [])
    place_left = places(path_left[::-1], [2])
    place_right = places(path_right[::-1], [2])

    packed = jnp.take(flow_qkv.value[:, rows_qkv], place, axis=0)
    gains, at = [], 0
    for scale in scales:
        size = scale.shape[0]
        gains.append(packed[:, at : at + size].astype(F32).reshape(1, size * shards))
        at += -(-size // 128) * 128
    gai, gao, gmi, gmo, gq, gk = gains

    def is_direct(rows):
        return rows % 16 == 0

    first_core = core.reshape(1)

    def weight(shape, flows):
        parts = max(1, flows[0][0].value.shape[0] // shards)
        rows = shape[0] // shards
        count = shape[1] // 2 // parts
        if is_direct(rows):
            pieces, first = [], 0
            for flow, at in flows:
                size = flow.value.shape[2]
                cuts = [
                    ((t * rows, rows, 0), (p * count + first, size, shape[1] // 2))
                    for p in range(parts)
                    for t in range(shards)
                ]
                pieces.append((at, cuts, flow.value, flow.got))
                first += size
            return Weight(shape, core=first_core, pieces=pieces)
        halves = []
        for which in ("value", "got"):
            laid = [
                jnp.take(getattr(flow, which)[:, :rows], at, axis=0).reshape(
                    parts, shards, rows, -1
                )
                for flow, at in flows
            ]
            laid = jnp.concatenate(laid, axis=3).transpose(1, 2, 0, 3)
            halves.append(laid.reshape(shape[0], shape[1] // 2))
        first = core == 0
        matrix = jnp.concatenate(
            [jnp.where(first, *halves), jnp.where(first, *halves[::-1])], axis=1
        )
        return Weight(shape, matrix, [(0, 0, shape[0])])

    def weight_rows(shape, flow, first, rows):
        if is_direct(first) and is_direct(rows):
            cuts = [((2 * t * rows, rows, rows), (0, shape[1], 0)) for t in range(shards)]
            order = jnp.arange(shards, dtype=jnp.int32)
            return Weight(
                shape,
                core=first_core,
                pieces=[(order, cuts, flow.value, flow.got)],
                source=first,
            )
        both = [value[:, first : first + rows] for value in (flow.value, flow.got)]
        matrix = jnp.stack(
            [jnp.where(core == 0, *both), jnp.where(core == 0, *both[::-1])], axis=1
        )
        return Weight(shape, matrix.reshape(shape), [(0, 0, shape[0])])

    class Grad:
        def __init__(self, shape_a, shape_b, left):
            self.shapes = shape_a, shape_b
            self.rows = rows = width // shards
            self.cols = ca, cb = shape_a[1] // 4, shape_b[1] // 4
            self.size = size = shape_b[1] // shards
            self.left = left
            first, second, others = up_along[0], up_along[1], up_along[2:]
            self.others = others
            self.ways = [[first, over_side, second] + others]
            if left < ca + cb:
                self.ways.insert(0, [over_side, second, first] + others)
            self.places = jnp.stack([places(ways, [2]) for ways in self.ways])
            self.direct = is_direct(rows)
            self.cuts = []
            if self.direct:
                for p in range(2):
                    for t in range(shards):
                        n = p * shards + t
                        edges = (0, left, ca) if left < ca else (0, ca)
                        for which, (low, high) in enumerate(zip(edges, edges[1:])):
                            cut = (t * rows, rows, 0), (p * ca + low, high - low, shape_a[1] // 2)
                            self.cuts.append((0, cut, which, n, low))
                        for j in range(cb // size):
                            high = (p * cb // size + j) * rows
                            cut = (high, rows, width // 2), (t * size, size, 0)
                            self.cuts.append((1, cut, len(self.ways) - 1, n, ca + j * size))
                self.outs = [(typed((2 * shards, rows, ca + cb), BF16), ANY)] * 2
            else:
                self.outs = [(typed(shape, BF16), ANY) for shape in self.shapes]
            self.sems = pltpu.SemaphoreType.DMA((max(2, 2 * len(self.cuts)),))

        def flow(self, near, far):
            if not self.direct:
                a, b = near, far
                a = a.reshape(shards, self.rows, 2, 2, self.cols[0]).transpose(2, 3, 0, 1, 4)
                b = b.reshape(2, 2, shards // 4, self.rows, shards, self.size)
                b = b.transpose(0, 1, 4, 3, 2, 5).reshape(a.shape[:4] + (self.cols[1],))
                both = jnp.concatenate([a, b], axis=4)
                both = jnp.where(core == 0, both, both[::-1])
                both = both.reshape((2, 2 * shards) + both.shape[3:])
                sides = []
                for n, ways in enumerate(self.ways):
                    order = jnp.zeros_like(self.places[n]).at[self.places[n]].set(
                        jnp.arange(2 * shards, dtype=jnp.int32)
                    )
                    sides.append(jnp.take(both, order, axis=1))
                if len(sides) == 2:
                    sides = [sides[0][..., : self.left], sides[1][..., self.left :]]
                near, far = jnp.concatenate(sides, axis=3)
            steps = [("halve", over_core)]
            if len(self.ways) == 1:
                steps += [("halve", way) for way in self.ways[0]] + self.ends()
            return Flow((near, far), steps)

        def ends(self):
            if self.direct:
                return [("double", over_side), ("swap", over_core)]
            return [("stack", over_side), ("stack", over_core)]

        def parts(self, flow):
            made, edges = [], [0, self.left, sum(self.cols)]
            for n, ways in enumerate(self.ways):
                value = flow.value[:, :, edges[n] : edges[n + 1]]
                half = value.shape[0] // 2
                made.append(
                    Flow((value[:half], value[half:]), [("halve", way) for way in ways[:3]])
                )
            return made

        def rest(self, made):
            value = jnp.concatenate([flow.value for flow in made], axis=2)
            half = value.shape[0] // 2
            steps = [("halve", way) for way in self.others] + self.ends()
            return Flow((value[:half], value[half:]), steps)

        def shares(self, widths, value, got=None):
            ca, cb = self.cols
            if not self.direct:
                value = value[:, :, 0].astype(F32)
                a = value[..., :ca].transpose(2, 0, 1, 3).reshape(self.rows, 4 * ca)
                b = value[..., ca:].reshape(2, 2, self.rows, cb // self.size, self.size)
                b = b.transpose(0, 1, 3, 2, 4).reshape(width, self.size)
                edges = [sum(widths[:n]) for n in range(len(widths) + 1)]
                return [a[:, low:high] for low, high in zip(edges, edges[1:])] + [b.T]
            outs = [(typed((self.rows, count), F32), VMEM) for count in widths]
            outs.append((typed((self.size, width), F32), VMEM))
            return kernel_of(
                functools.partial(shares_kernel, widths, ca),
                "shares",
                [SMEM] + [VMEM] * 2,
                outs,
                [pltpu.VMEM((width, self.size), F32)],
                0,
            )(jnp.stack([core, side]), value, got)

    up_along = [("shard", bit) for bit in net.shard_bits]
    grad_mlp = Grad(shape_gate, (width, ff), (2 * ff + ff) // 8)
    grad_attn = Grad(shape_qkv, (width, heads * hd), (qkv + heads * hd) // 4)

    in_v = lambda count: [VMEM] * count
    in_s = lambda count: [SMEM] * count
    out_v = lambda *types: [(typed(*one), VMEM) for one in types]
    sems = lambda count: pltpu.SemaphoreType.DMA((count,))
    reach = min(length, WINDOW + QB)
    bf = lambda *shape: (shape, BF16)
    f32 = lambda *shape: (shape, F32)

    seg_rows = segment_ids.reshape(length, 1)
    seg_cols = segment_ids.reshape(1, length)
    flows = [flow_left, flow_right]
    got, _ = net.launch(flows)
    land([flow_qkv], core_got)
    weight_qkv = weight(shape_qkv, [(flow_qkv, place)])
    steps = (length // QB,)
    outs = land(
        flows,
        got,
        kernel_of(
            functools.partial(project_kernel, weight_qkv, heads),
            "project",
            weight_qkv.specs
            + [by_rows(width), by_rows(hd // 2), by_rows(hd // 2)]
            + [all_of(1, width), all_of(1, hd), all_of(1, hd)],
            [
                (typed((length, width), BF16), by_rows(width)),
                (typed((length, heads * hd), BF16), by_rows(heads * hd)),
                (typed((length, hd), BF16), by_rows(hd)),
                (typed((length, hd), BF16), by_rows(hd)),
                (
                    typed((heads, length, hd), BF16),
                    pl.BlockSpec((heads, QB, hd), lambda i: (0, i, 0)),
                ),
                (typed((length, hd), BF16), by_rows(hd)),
            ],
            weight_qkv.scratch,
            2 * length * width * qkv,
            grid=steps,
        )(*weight_qkv.operands, inputs, cos, sin, gai, gq, gk),
    )
    normed, qraw, kraw, values, queries, keys = outs
    flows = [flow_left, flow_right]
    got, args = net.launch(flows, [seg_rows, seg_cols, queries, keys, values])
    small = [gao, gmi, gmo, place_left, place_right, grad_mlp.places]
    small, args = lax.optimization_barrier((small, args))
    gao, gmi, gmo, place_left, place_right, grad_mlp.places = small
    probs, mixed = land(
        flows,
        got,
        kernel_of(
            attend_kernel,
            "attend",
            in_v(5),
            [(typed((heads, length, reach), BF16), ANY)] + out_v(bf(length, heads * hd)),
            [pltpu.VMEM((heads, length, reach), BF16), sems(length // QB)],
            4 * length * heads * hd * reach,
        )(*args),
    )

    finish(net, [flow_left, flow_right, flow_rows])
    high, low = w_out.shape[0] // 2, w_down.shape[0] // 2
    weight_out = weight_rows(shape_out, flow_rows, 0, high)
    weight_down = weight_rows(shape_down, flow_rows, high, low)
    weight_gate = weight(shape_gate, [(flow_left, place_left), (flow_right, place_right)])
    output, dmiddle, dbranch, ggain_mlp, *ends = kernel_of(
        functools.partial(mlp_kernel, weight_out, weight_down, weight_gate, grad_mlp.cuts),
        "mlp",
        weight_out.specs + weight_down.specs + weight_gate.specs + in_s(2) + in_v(5) + [ANY],
        [
            (typed((length, width), BF16), ANY),
            (typed((length, width), F32), ANY),
            (typed((length, width), BF16), VMEM),
            (typed((3, width), F32), VMEM),
        ]
        + grad_mlp.outs,
        weight_out.scratch
        + weight_down.scratch
        + weight_gate.scratch
        + [
            pltpu.VMEM((length, width), BF16),
            pltpu.VMEM((length, width), BF16),
            pltpu.VMEM((length, width), BF16),
            pltpu.VMEM((length, ff), BF16),
            pltpu.VMEM((length, 2 * ff), BF16),
            pltpu.VMEM((length, width), BF16),
            pltpu.VMEM((width, ff), BF16),
            pltpu.VMEM(shape_gate, BF16),
            pltpu.VMEM((length, width), F32),
            pltpu.VMEM((length, width), BF16),
            sems(3),
            grad_mlp.sems,
        ],
        2 * length * width * (9 * ff + heads * hd),
    )(
        *weight_out.operands, *weight_down.operands, *weight_gate.operands, first_core, grad_mlp.places,
        mixed, inputs, gao, gmi, gmo, out_grad,
    )
    back_mlp = grad_mlp.flow(*ends)
    dmixed, gout = advance(
        net,
        [back_mlp],
        kernel_of(
            functools.partial(out_bwd_kernel, weight_out, heads),
            "out_bwd",
            weight_out.specs + in_v(2),
            out_v(bf(heads, length, hd), bf(width, heads * hd)),
            weight_out.scratch,
            4 * length * heads * hd * width,
        ),
        [*weight_out.operands, dbranch, mixed],
    )
    back_mlp = grad_mlp.parts(back_mlp)
    draw, ggain_qk, *ends = advance(
        net,
        back_mlp,
        kernel_of(
            functools.partial(attn_bwd_kernel, grad_attn.cuts),
            "attn_bwd",
            in_s(2) + in_v(8) + [ANY] * 5,
            out_v(bf(length, qkv), f32(2, hd)) + grad_attn.outs,
            [
                pltpu.VMEM((heads, length, reach), BF16),
                sems(length // QB),
                pltpu.VMEM((heads, QB, reach), BF16),
                pltpu.VMEM((length, heads * hd), F32),
                pltpu.VMEM((hd, length), F32),
                pltpu.VMEM((hd, length), F32),
                pltpu.VMEM(shape_qkv, BF16),
                grad_attn.sems,
                pltpu.VMEM((length, heads * hd), BF16),
                pltpu.VMEM((length, hd), BF16),
                pltpu.VMEM((length, width), BF16),
                pltpu.VMEM((width, heads * hd), BF16),
                sems(4),
            ],
            2 * length * (width * qkv + 4 * heads * hd * reach),
        ),
        [
            first_core, grad_attn.places, dmixed, queries, keys, values, cos, sin, gq, gk, qraw,
            kraw, normed, gout, probs,
        ],
    )
    back_attn = grad_attn.flow(*ends)
    flows = [back_attn, *back_mlp]
    got, (draw,) = net.launch(flows, [draw])
    land(flows[:1], got[:1])
    more, (draw,) = net.launch([back_attn], [draw])
    input_grad, ggain_in = land(
        [*back_mlp, back_attn],
        got[1:] + more,
        kernel_of(
            functools.partial(input_bwd_kernel, weight_qkv),
            "input_bwd",
            weight_qkv.specs + [by_rows(qkv), by_rows(width), by_rows(width), all_of(1, width)],
            [
                (typed((length, width), F32), by_rows(width)),
                (typed((1, width), F32), all_of(1, width)),
            ],
            weight_qkv.scratch,
            2 * length * width * qkv,
            grid=steps,
        )(*weight_qkv.operands, draw, dmiddle, inputs, gai),
    )
    sums = jnp.concatenate(
        [ggain_in, ggain_mlp[2:3], ggain_mlp[1:2], ggain_mlp[0:1], ggain_qk[0:1], ggain_qk[1:2]],
        axis=1,
    )
    sums = Flow(sums.reshape(-1, 128), [("total", way) for way in [over_core, over_side] + along])
    advance(net, [*back_mlp, back_attn, sums])
    back_mlp = grad_mlp.rest(back_mlp)
    while back_mlp.steps:
        advance(net, [back_mlp, back_attn, sums])
    finish(net, [back_attn, sums], 1)
    full_gate, full_up, full_down = advance(
        net,
        [back_attn, sums],
        functools.partial(grad_mlp.shares, (ff, ff)),
        [back_mlp.value] + ([back_mlp.got] if grad_mlp.direct else []),
    )
    full_query, full_key, full_value, full_out = grad_attn.shares(
        (heads * hd, hd, hd), back_attn.value, getattr(back_attn, "got", None)
    )
    sums = sums.value.reshape(-1)

    shard = lax.axis_index("shard")
    grads, at = [], 0
    for scale in scales:
        size = scale.shape[0]
        grads.append(lax.dynamic_slice_in_dim(sums, at + shard * size, size, 0))
        at += size * shards
    return (
        output,
        input_grad,
        full_query,
        full_key,
        full_value,
        full_out,
        full_gate,
        full_up,
        full_down,
        grads[0],
        grads[4],
        grads[5],
        grads[1],
        grads[2],
        grads[3],
    )


def solution(mesh):
    rows, vector = P("shard", None), P("shard")
    tokens = P(AXES, None)
    return jax.shard_map(
        functools.partial(layer, Net(mesh)),
        mesh=mesh,
        in_specs=(tokens, P(AXES), tokens) + (rows,) * 7 + (vector,) * 6,
        out_specs=(tokens, tokens) + (rows,) * 7 + (vector,) * 6,
        check_vma=False,
    )
```

```python
import functools
import math

import jax
import jax.numpy as jnp
from jax import lax
from jax.experimental import pallas as pl
from jax.experimental.pallas import tpu as pltpu
from jax.sharding import PartitionSpec as P

WINDOW = 512
EPSILON = 1e-06
NEG = -1e30
QB = 256
RB = 512
CB = 512
GB = 1024
AXES = ("replica", "shard")
F32 = jnp.float32
BF16 = jnp.bfloat16
GELU_C = math.sqrt(2.0 / math.pi)


def flip_pairs(reps, shards, axis, bit):
    pairs = []
    for rep in range(reps):
        for shard in range(shards):
            rep_to = rep ^ bit if axis == "replica" else rep
            shard_to = shard ^ bit if axis == "shard" else shard
            pairs.append((rep * shards + shard, rep_to * shards + shard_to))
    return pairs


class Net:
    def __init__(self, mesh):
        self.reps = mesh.shape["replica"]
        self.shards = mesh.shape["shard"]
        self.shard_bits = [1 << i for i in range(self.shards.bit_length() - 1)]
        self.rep_bits = [1 << i for i in range(self.reps.bit_length() - 1)]
        assert 1 << len(self.shard_bits) == self.shards
        assert self.reps == 4

    def swap(self, value, axis, bit):
        return lax.ppermute(value, AXES, flip_pairs(self.reps, self.shards, axis, bit))

    def launch(self, flows, args=()):
        moves = [flow.move() for flow in flows]
        values, args = lax.optimization_barrier(([value for value, _ in moves], list(args)))
        return [self.swap(value, *way) for value, (_, way) in zip(values, moves)], args


def add_up(value, got):
    return (value.astype(F32) + got.astype(F32)).astype(BF16)


def in_order(value, got, axis, bit, dim):
    first = (lax.axis_index(axis) & bit) == 0
    return jnp.concatenate([jnp.where(first, value, got), jnp.where(first, got, value)], axis=dim)


class Flow:
    def __init__(self, value, steps):
        self.value = value
        self.steps = list(steps)

    def move(self):
        if self.steps[0][0] == "halve":
            return self.value[1], self.steps[0][1]
        return self.value, self.steps[0][1]

    def take(self, got):
        kind, way = self.steps[0][:2]
        value = self.value
        if kind == "double":
            self.value = jnp.concatenate([value, got], axis=0)
        elif kind == "swap":
            self.got = got
        elif kind == "halve":
            near = value[0]
            if len(self.steps) > 1 and self.steps[1][0] == "halve":
                half = near.shape[0] // 2
                self.value = (add_up(near[:half], got[:half]), add_up(near[half:], got[half:]))
            else:
                self.value = add_up(near, got)
        elif kind == "total":
            self.value = value + got
        else:
            self.value = in_order(value[None], got[None], *way, 0)
        self.steps = self.steps[1:]


def land(flows, got, outs=()):
    got, outs = lax.optimization_barrier((got, outs))
    for flow, value in zip(flows, got):
        flow.take(value)
    return outs


def advance(net, flows, work=None, args=()):
    flows = [flow for flow in flows if flow.steps]
    got, args = net.launch(flows, args)
    return land(flows, got, work(*args) if work is not None else ())


def finish(net, flows, left=0):
    while any(len(flow.steps) > left for flow in flows):
        advance(net, [flow for flow in flows if len(flow.steps) > left])


def places(stages, parts):
    rep = lax.axis_index("replica")
    shard = lax.axis_index("shard")
    shards = 1
    for axis, bit in stages:
        shards *= 2 if axis == "shard" else 1
    count = 1 << len(parts)
    part = jnp.arange(count, dtype=jnp.int32)[:, None]
    block = jnp.arange(shards, dtype=jnp.int32)[None, :]
    part_rep = jnp.zeros_like(part)
    for i, bit in enumerate(parts):
        part_rep = part_rep + ((part >> (len(parts) - 1 - i)) & 1) * bit
    rep_diff = part_rep ^ rep
    shard_diff = block ^ shard
    where = jnp.zeros((count, shards), jnp.int32)
    for axis, bit in stages:
        diff = rep_diff if axis == "replica" else shard_diff
        where = where * 2 + jnp.where((diff & bit) != 0, 1, 0)
    return where.reshape(-1)


def dot(left, right):
    return jnp.dot(left, right, preferred_element_type=F32)


def dot_nt(left, right):
    return lax.dot_general(left, right, (((1,), (1,)), ((), ())), preferred_element_type=F32)


def dot_tn(left, right):
    return lax.dot_general(left, right, (((0,), (0,)), ((), ())), preferred_element_type=F32)


def inv_rms(value):
    return lax.rsqrt(jnp.mean(value * value, axis=-1, keepdims=True) + EPSILON)


def norm_back(grad, unit, inv, gain):
    scaled = grad * gain
    return inv * (scaled - unit * jnp.mean(scaled * unit, axis=-1, keepdims=True))


def rows_of(index, size):
    return pl.ds(pl.multiple_of(index * size, size), size)


def start_all(copies):
    for copy in copies:
        copy.start()


def wait_all(copies):
    for copy in copies:
        copy.wait()


def on_first(copies):
    @pl.when(pl.program_id(0) == 0)
    def _():
        start_all(copies)
        wait_all(copies)


def project_kernel(weight_qkv, heads, *refs):
    refs_qkv, refs = split(refs, len(weight_qkv.specs))
    (
        x_ref, cos_ref, sin_ref, gai_ref, gq_ref, gk_ref,
        normed_ref, qraw_ref, kraw_ref, v_ref, q_ref, k_ref,
        wqkv, sem_qkv,
    ) = refs
    hd = k_ref.shape[1]
    half = hd // 2
    factor = hd ** (-0.5)
    on_first(weight_qkv.copies(refs_qkv, wqkv, sem_qkv))
    x = x_ref[...].astype(F32)
    normed = (x * inv_rms(x) * gai_ref[...]).astype(BF16)
    normed_ref[...] = normed
    cos, sin = cos_ref[...], sin_ref[...]

    def turn(value):
        first, second = value[:, :half], value[:, half:]
        return jnp.concatenate([first * cos - second * sin, second * cos + first * sin], axis=1)

    for h in range(heads):
        raw = dot(normed, wqkv[:, h * hd : (h + 1) * hd])
        qraw_ref[:, h * hd : (h + 1) * hd] = raw.astype(BF16)
        q_ref[h, :, :] = (turn(raw * inv_rms(raw) * gq_ref[...]) * factor).astype(BF16)
    raw = dot(normed, wqkv[:, heads * hd : (heads + 1) * hd])
    kraw_ref[...] = raw.astype(BF16)
    k_ref[...] = turn(raw * inv_rms(raw) * gk_ref[...]).astype(BF16)
    v_ref[...] = dot(normed, wqkv[:, (heads + 1) * hd :]).astype(BF16)


def attend_kernel(
    segr_ref, segc_ref, q_ref, k_ref, v_ref, probs_hbm, mixed_ref, probs_all, sem_probs
):
    heads, length, hd = q_ref.shape
    out_probs = probs_copies(probs_hbm, probs_all, sem_probs, True)
    for b in range(length // QB):
        low, high = key_range(b)
        width = high - low
        rows = slice(b * QB, high)
        seg_q, seg_k = segr_ref[rows, :], segc_ref[:, low:high]
        offset = (
            lax.broadcasted_iota(jnp.int32, (QB, width), 0)
            - lax.broadcasted_iota(jnp.int32, (QB, width), 1)
            + (b * QB - low)
        )
        allowed = (seg_q == seg_k) & (seg_q >= 0) & (offset >= 0) & (offset < WINDOW)
        allowed = allowed | (offset == 0)
        keys, vals = k_ref[low:high, :], v_ref[low:high, :]
        for h in range(heads):
            scores = jnp.where(allowed, dot_nt(q_ref[h, rows, :], keys), NEG)
            expo = jnp.exp(scores - jnp.max(scores, axis=1, keepdims=True))
            probs = (expo * (1.0 / jnp.sum(expo, axis=1, keepdims=True))).astype(BF16)
            probs_all[h, rows, 0:width] = probs
            mixed_ref[rows, h * hd : (h + 1) * hd] = dot(probs, vals).astype(BF16)
        out_probs[b].start()
    wait_all(out_probs)


def cut_at(cut, which):
    (row, rows, row_step), (col, cols, col_step) = cut
    if row_step:
        row = pl.multiple_of(row + which * row_step, 16)
    if col_step:
        col = pl.multiple_of(col + which * col_step, 128)
    return pl.ds(row, rows), pl.ds(col, cols)


class Weight:
    def __init__(self, shape, matrix=None, rows=(), core=None, pieces=(), source=0):
        self.shape, self.rows, self.source = shape, rows, source
        self.cuts = [cuts for _, cuts, _, _ in pieces]
        if matrix is not None:
            self.operands, self.specs, count = [matrix], [ANY], len(rows)
        else:
            self.operands, self.specs, count = [core], [SMEM], 0
            for place, cuts, own, got in pieces:
                self.operands += [place, own, got]
                self.specs += [SMEM, ANY, ANY]
                count += 2 * len(cuts)
        self.scratch = [pltpu.VMEM(shape, BF16), pltpu.SemaphoreType.DMA((count,))]

    def copies(self, refs, mat, sem):
        made = []
        for source, to, count in self.rows:
            src, dst = refs[0].at[pl.ds(source, count), :], mat.at[pl.ds(to, count), :]
            made.append(pltpu.make_async_copy(src, dst, sem.at[len(made)]))
        for piece, cuts in enumerate(self.cuts):
            core = refs[0][0]
            place, own, got = refs[3 * piece + 1 : 3 * piece + 4]
            for n, cut in enumerate(cuts):
                for hbm, which in ((own, core), (got, 1 - core)):
                    src = hbm.at[place[n], pl.ds(self.source, cut[0][1]), :]
                    dst = mat.at[cut_at(cut, which)]
                    made.append(pltpu.make_async_copy(src, dst, sem.at[len(made)]))
        return made


def grad_copies(cuts, refs, mats, sem):
    core_ref, places_ref, near, far = refs
    if not cuts:
        return [pltpu.make_async_copy(m, o, sem.at[i]) for i, (m, o) in enumerate(zip(mats, (near, far)))]
    core, made = core_ref[0], []
    for mat, cut, which_place, n, col in cuts:
        for hbm, which in ((far, 1 - core), (near, core)):
            src = mats[mat].at[cut_at(cut, which)]
            dst = hbm.at[places_ref[which_place, n], :, pl.ds(col, cut[1][1])]
            made.append(pltpu.make_async_copy(src, dst, sem.at[len(made)]))
    return made


def split(refs, *counts):
    parts, at = [], 0
    for count in counts:
        parts.append(refs[at : at + count])
        at += count
    return parts + [refs[at:]]


def mlp_kernel(weight_out, weight_down, weight_gate, cuts_grad, *refs):
    refs_out, refs_down, refs_gate, to_grad, refs = split(
        refs, len(weight_out.specs), len(weight_down.specs), len(weight_gate.specs), 2
    )
    (
        mixed_ref, x_ref, gao_ref, gmi_ref, gmo_ref, top_hbm,
        output_hbm, dmiddle_hbm, dbranch_ref, ggain_ref, near, far,
        wout, sem_out, wdown, sem_down, wgu, sem_gate,
        top_ref, branch_ref, inner_ref, hidden, dgu, ddown, gdown, ggate, middle_ref, output_ref,
        sem, sem_grad,
    ) = refs
    length, ff = hidden.shape
    in_out = weight_out.copies(refs_out, wout, sem_out)
    in_gate = weight_gate.copies(refs_gate, wgu, sem_gate)
    in_down = weight_down.copies(refs_down, wdown, sem_down)
    in_top = pltpu.make_async_copy(top_hbm, top_ref, sem.at[0])
    start_all(in_out)
    start_all(in_gate)
    start_all(in_down)
    in_top.start()
    ggain_ref[...] = jnp.zeros_like(ggain_ref)
    wait_all(in_out)

    def attn_out(i, carry):
        rows = rows_of(i, QB)
        branch = dot(mixed_ref[rows, :], wout[...])
        branch_ref[rows, :] = branch.astype(BF16)
        middle = x_ref[rows, :].astype(F32) + branch * inv_rms(branch) * gao_ref[...]
        middle_ref[rows, :] = middle
        inner_ref[rows, :] = (middle * inv_rms(middle) * gmi_ref[...]).astype(BF16)
        return carry

    lax.fori_loop(0, length // QB, attn_out, 0, unroll=True)
    wait_all(in_gate)

    def forward(i, carry):
        rows = rows_of(i, RB)
        inner = inner_ref[rows, :]
        for c in range(ff // CB):
            cols = slice(c * CB, (c + 1) * CB)
            more = slice(ff + c * CB, ff + (c + 1) * CB)
            gate = dot(inner, wgu[:, cols])
            up = dot(inner, wgu[:, more])
            square = gate * gate
            tanh = jnp.tanh(gate * (GELU_C + (GELU_C * 0.044715) * square))
            base = 0.5 + 0.5 * tanh
            act = gate * base
            slope = base + (0.5 * gate) * (1.0 - tanh * tanh) * (
                GELU_C + (3.0 * GELU_C * 0.044715) * square
            )
            hidden[rows, cols] = (act * up).astype(BF16)
            dgu[rows, cols] = (slope * up).astype(BF16)
            dgu[rows, more] = act.astype(BF16)
        return carry

    lax.fori_loop(0, length // RB, forward, 0)
    wait_all(in_down)
    in_top.wait()

    def down_row(i, carry):
        rows = rows_of(i, RB)
        down = dot(hidden[rows, :], wdown[...])
        inv = inv_rms(down)
        unit = down * inv
        output_ref[rows, :] = (middle_ref[rows, :] + unit * gmo_ref[...]).astype(BF16)
        top = top_ref[rows, :].astype(F32)
        ddown[rows, :] = norm_back(top, unit, inv, gmo_ref[...]).astype(BF16)
        ggain_ref[0:1, :] += jnp.sum(top * unit, axis=0, keepdims=True)
        return carry

    lax.fori_loop(0, length // RB, down_row, 0, unroll=True)
    out_output = pltpu.make_async_copy(output_ref, output_hbm, sem.at[1])
    out_output.start()

    def down_grad(i, carry):
        cols = rows_of(i, GB)
        gdown[:, cols] = dot_tn(ddown[...], hidden[:, cols]).astype(BF16)
        return carry

    lax.fori_loop(0, ff // GB, down_grad, 0)

    def hidden_back(i, carry):
        rows = rows_of(i, RB)
        grad = ddown[rows, :]
        for c in range(ff // CB):
            cols = slice(c * CB, (c + 1) * CB)
            more = slice(ff + c * CB, ff + (c + 1) * CB)
            dhid = dot_nt(grad, wdown[cols, :])
            dgu[rows, cols] = (dhid * dgu[rows, cols].astype(F32)).astype(BF16)
            dgu[rows, more] = (dhid * dgu[rows, more].astype(F32)).astype(BF16)
        return carry

    lax.fori_loop(0, length // RB, hidden_back, 0)

    def gate_grad(i, carry):
        cols = rows_of(i, GB)
        ggate[:, cols] = dot_tn(inner_ref[...], dgu[:, cols]).astype(BF16)
        return carry

    lax.fori_loop(0, 2 * ff // GB, gate_grad, 0)
    out_grad = grad_copies(cuts_grad, (*to_grad, near, far), (ggate, gdown), sem_grad)
    start_all(out_grad)

    def inner_back(i, carry):
        rows = rows_of(i, RB)
        dinner = dot_nt(dgu[rows, :], wgu[...])
        middle = middle_ref[rows, :]
        inv = inv_rms(middle)
        unit = middle * inv
        dmid = top_ref[rows, :].astype(F32) + norm_back(dinner, unit, inv, gmi_ref[...])
        middle_ref[rows, :] = dmid
        ggain_ref[1:2, :] += jnp.sum(dinner * unit, axis=0, keepdims=True)
        branch = branch_ref[rows, :].astype(F32)
        inv = inv_rms(branch)
        unit = branch * inv
        dbranch_ref[rows, :] = norm_back(dmid, unit, inv, gao_ref[...]).astype(BF16)
        ggain_ref[2:3, :] += jnp.sum(dmid * unit, axis=0, keepdims=True)
        return carry

    lax.fori_loop(0, length // RB, inner_back, 0, unroll=True)
    out_middle = pltpu.make_async_copy(middle_ref, dmiddle_hbm, sem.at[2])
    out_middle.start()
    out_output.wait()
    wait_all(out_grad)
    out_middle.wait()


def out_bwd_kernel(weight_out, heads, *refs):
    refs_out, refs = split(refs, len(weight_out.specs))
    dbranch_ref, mixed_ref, dmixed_ref, gout_ref, wout, sem_out = refs
    length = mixed_ref.shape[0]
    hd = dmixed_ref.shape[2]
    in_out = weight_out.copies(refs_out, wout, sem_out)
    start_all(in_out)

    def weights_out(i, carry):
        cols = rows_of(i, CB)
        gout_ref[:, cols] = dot_tn(dbranch_ref[...], mixed_ref[:, cols]).astype(BF16)
        return carry

    lax.fori_loop(0, heads * hd // CB, weights_out, 0)
    wait_all(in_out)

    def mixed_back(i, carry):
        rows = rows_of(i, QB)
        for h in range(heads):
            cols = slice(h * hd, (h + 1) * hd)
            dmixed_ref[h, rows, :] = dot_nt(dbranch_ref[rows, :], wout[cols, :]).astype(BF16)
        return carry

    lax.fori_loop(0, length // QB, mixed_back, 0)


def turn_back(value, cos, sin):
    half = value.shape[1] // 2
    first, second = value[:, :half], value[:, half:]
    return jnp.concatenate([first * cos + second * sin, second * cos - first * sin], axis=1)


def key_range(b):
    return max(0, b - WINDOW // QB) * QB, (b + 1) * QB


def probs_copies(probs_hbm, probs, sem, outward):
    made = []
    for b in range(probs.shape[1] // QB):
        low, high = key_range(b)
        at = (slice(None), slice(b * QB, high), slice(0, high - low))
        far, near = probs_hbm.at[at], probs.at[at]
        src, dst = (near, far) if outward else (far, near)
        made.append(pltpu.make_async_copy(src, dst, sem.at[b]))
    return made


def attn_bwd_kernel(cuts_grad, *refs):
    (
        core_ref, places_ref, dmixed_ref, q_ref, k_ref, v_ref,
        cos_ref, sin_ref, gq_ref, gk_ref, qraw_hbm, kraw_hbm, normed_hbm, gout_hbm, probs_hbm,
        draw_ref, ggain_ref, near, far,
        probs_all, sem_probs, ds, dq, dk, dv, gqkv, sem_grad,
        qraw_ref, kraw_ref, normed_ref, gout, sem_late,
    ) = refs
    heads, length, hd = q_ref.shape
    factor = hd ** (-0.5)
    in_probs = probs_copies(probs_hbm, probs_all, sem_probs, False)
    start_all(in_probs)
    late = ((gout_hbm, gout), (qraw_hbm, qraw_ref), (kraw_hbm, kraw_ref), (normed_hbm, normed_ref))
    in_late = [pltpu.make_async_copy(*pair, sem_late.at[n]) for n, pair in enumerate(late)]
    start_all(in_late)
    out_grad = grad_copies(cuts_grad, (core_ref, places_ref, near, far), (gqkv, gout), sem_grad)
    early = [cut[0] == 1 for cut in cuts_grad for _ in range(2)] or [False, True]
    dk[...] = jnp.zeros_like(dk)
    dv[...] = jnp.zeros_like(dv)
    for b in range(length // QB):
        low, high = key_range(b)
        width = high - low
        rows = slice(b * QB, high)
        in_probs[b].wait()
        keys, vals = k_ref[low:high, :], v_ref[low:high, :]
        for h in range(heads):
            probs = probs_all[h, rows, 0:width].astype(F32)
            dprobs = dot_nt(dmixed_ref[h, rows, :], vals)
            inner = jnp.sum(probs * dprobs, axis=1, keepdims=True)
            dscores = (probs * (dprobs - inner)).astype(BF16)
            ds[h, :, 0:width] = dscores
            dq[rows, h * hd : (h + 1) * hd] = dot(dscores, keys) * factor
        stack = lambda value: value.reshape(heads * QB, value.shape[2])
        dk[:, low:high] += dot_tn(stack(q_ref[:, rows, :]), stack(ds[:, :, 0:width]))
        dv[:, low:high] += dot_tn(
            stack(dmixed_ref[:, rows, :]), stack(probs_all[:, rows, 0:width])
        )

    ggain_ref[...] = jnp.zeros_like(ggain_ref)
    wait_all(in_late)
    start_all([copy for copy, first in zip(out_grad, early) if first])

    def raw_back(i, carry):
        rows = rows_of(i, QB)
        cos, sin = cos_ref[rows, :], sin_ref[rows, :]
        total = jnp.zeros((1, hd), F32)
        for h in range(heads):
            cols = slice(h * hd, (h + 1) * hd)
            grad = turn_back(dq[rows, cols], cos, sin)
            raw = qraw_ref[rows, cols].astype(F32)
            inv = inv_rms(raw)
            unit = raw * inv
            draw_ref[rows, cols] = norm_back(grad, unit, inv, gq_ref[...]).astype(BF16)
            total += jnp.sum(grad * unit, axis=0, keepdims=True)
        ggain_ref[0:1, :] += total
        grad = turn_back(dk[:, rows].T, cos, sin)
        raw = kraw_ref[rows, :].astype(F32)
        inv = inv_rms(raw)
        unit = raw * inv
        draw_ref[rows, heads * hd : (heads + 1) * hd] = norm_back(
            grad, unit, inv, gk_ref[...]
        ).astype(BF16)
        ggain_ref[1:2, :] += jnp.sum(grad * unit, axis=0, keepdims=True)
        draw_ref[rows, (heads + 1) * hd :] = dv[:, rows].T.astype(BF16)
        return carry

    lax.fori_loop(0, length // QB, raw_back, 0)

    def weights(i, carry):
        cols = rows_of(i, CB)
        gqkv[:, cols] = dot_tn(normed_ref[...], draw_ref[:, cols]).astype(BF16)
        return carry

    lax.fori_loop(0, gqkv.shape[1] // CB, weights, 0)
    start_all([copy for copy, first in zip(out_grad, early) if not first])
    wait_all(out_grad)


def input_bwd_kernel(weight_qkv, *refs):
    refs_qkv, refs = split(refs, len(weight_qkv.specs))
    draw_ref, dmiddle_ref, x_ref, gai_ref, dx_ref, ggain_ref, wqkv, sem_qkv = refs
    on_first(weight_qkv.copies(refs_qkv, wqkv, sem_qkv))

    @pl.when(pl.program_id(0) == 0)
    def _():
        ggain_ref[...] = jnp.zeros_like(ggain_ref)

    dnormed = dot_nt(draw_ref[...], wqkv[...])
    x = x_ref[...].astype(F32)
    inv = inv_rms(x)
    unit = x * inv
    dx_ref[...] = dmiddle_ref[...] + norm_back(dnormed, unit, inv, gai_ref[...])
    ggain_ref[...] += jnp.sum(dnormed * unit, axis=0, keepdims=True)


def shares_kernel(widths, ca, me_ref, value_ref, got_ref, *refs):
    *a_refs, b_ref, turned = refs
    core, side = me_ref[0], me_ref[1]
    rows, size = value_ref.shape[1], turned.shape[1]
    pieces = (value_ref.shape[2] - ca) // size
    for c in range(2):
        for s in range(2):
            n = 2 * c + s
            at = jnp.bitwise_xor(side, s)
            own, got = value_ref[at].astype(F32), got_ref[at].astype(F32)
            block = jnp.where(core == c, own, got)
            low = 0
            for ref, count in zip(a_refs, widths):
                first, last = max(low, n * ca), min(low + count, (n + 1) * ca)
                if first < last:
                    ref[:, first - low : last - low] = block[:, first - n * ca : last - n * ca]
                low += count
            for j in range(pieces):
                row = (n * pieces + j) * rows
                turned[row : row + rows, :] = block[:, ca + j * size : ca + (j + 1) * size]
    b_ref[...] = turned[...].T


VMEM = pl.BlockSpec(memory_space=pltpu.VMEM)
SMEM = pl.BlockSpec(memory_space=pltpu.SMEM)
ANY = pl.BlockSpec(memory_space=pl.ANY)


def by_rows(width):
    return pl.BlockSpec((QB, width), lambda i: (i, 0))


def all_of(*shape):
    return pl.BlockSpec(shape, lambda i: (0,) * len(shape))


VMEM_MIB = {"out_bwd": 24, "attn_bwd": 44, "input_bwd": 24, "shares": 12}


def kernel_of(body, name, in_specs, outs, scratch, flops, **more):
    def run(*operands):
        total = 0
        for value in list(operands) + [value for value, _ in outs]:
            total += math.prod(value.shape) * value.dtype.itemsize
        return pl.pallas_call(
            body,
            name=name,
            out_shape=[value for value, _ in outs],
            in_specs=in_specs,
            out_specs=[spec for _, spec in outs],
            scratch_shapes=scratch,
            compiler_params=pltpu.CompilerParams(
                vmem_limit_bytes=VMEM_MIB.get(name, 56) << 20
            ),
            cost_estimate=pl.CostEstimate(flops=flops, bytes_accessed=total, transcendentals=0),
            **more,
        )(*operands)

    return run


def typed(shape, dtype):
    return jax.ShapeDtypeStruct(shape, dtype)


def positions(seg):
    length = seg.shape[0]
    index = jnp.arange(length, dtype=jnp.int32)
    previous = jnp.concatenate([jnp.full((1,), -3, jnp.int32), seg[:-1]])
    starts = jnp.where(seg != previous, index, jnp.zeros_like(index))
    return index - lax.cummax(starts, axis=0)


def rope_angles(position, head_dim):
    half = head_dim // 2
    freqs = 10000.0 ** (-2.0 * jnp.arange(half, dtype=F32) / head_dim)
    return position.astype(F32)[:, None] * freqs[None, :]


def layer(
    net,
    inputs,
    segment_ids,
    out_grad,
    w_query,
    w_key,
    w_value,
    w_out,
    w_gate,
    w_up,
    w_down,
    scale_attn_in,
    scale_query,
    scale_key,
    scale_attn_out,
    scale_mlp_in,
    scale_mlp_out,
):
    length, width = inputs.shape
    hd = w_key.shape[1]
    heads = w_query.shape[1] // hd
    qkv = (heads + 2) * hd
    ff = w_gate.shape[1]
    shards = net.shards
    rep = lax.axis_index("replica")
    core = rep & 1
    side = (rep >> 1) & 1

    along = [("shard", bit) for bit in reversed(net.shard_bits)]
    over_core, over_side = ("replica", 1), ("replica", 2)
    doubles = lambda ways: [("double", way) for way in ways]

    def half_rows(value, index, parts):
        size = value.shape[0] // parts
        return lax.dynamic_slice_in_dim(value, index * size, size, 0)

    def half_cols(value, index, parts):
        size = value.shape[1] // parts
        return lax.dynamic_slice_in_dim(value, index * size, size, 1)

    path_left = along + [over_side]
    path_right = along[:-1] + [over_side, along[-1]]
    scales = (scale_attn_in, scale_attn_out, scale_mlp_in, scale_mlp_out, scale_query, scale_key)
    shape_qkv, shape_out = (width, qkv), (heads * hd, width)
    shape_gate, shape_down = (width, 2 * ff), (ff, width)
    last = [("swap", over_core)]

    angles = rope_angles(positions(segment_ids), hd)
    half = qkv // 2
    rows_qkv = w_query.shape[0]
    key_at, value_at = heads * hd - half, heads * hd + hd - half
    second = jnp.pad(w_query[:, half:], ((0, 0), (0, qkv - heads * hd)))
    second += jnp.pad(w_key, ((0, 0), (key_at, half - key_at - hd)))
    second += jnp.pad(w_value, ((0, 0), (value_at, half - value_at - hd)))
    own_qkv = jnp.where(core == 0, w_query[:, :half], second)
    own_qkv = jnp.pad(own_qkv, ((0, 16), (0, 0)))
    at = 0
    for scale in scales:
        size = scale.shape[0]
        own_qkv += jnp.pad(scale[None, :], ((rows_qkv, 15), (at, half - at - size)))
        at += -(-size // 128) * 128
    flow_qkv = Flow(own_qkv[None], doubles(along) + last)
    own_gate = half_cols(jnp.where(core == 0, w_gate, w_up), side, 2)[None]
    flow_gate = Flow(own_gate, doubles(along[:-1]))
    own_rows = jnp.concatenate([half_rows(w_out, core, 2), half_rows(w_down, core, 2)], axis=0)
    cos, sin = advance(net, [flow_qkv], lambda a: (jnp.cos(a), jnp.sin(a)), [angles])
    finish(net, [flow_qkv], 3)
    advance(net, [flow_qkv, flow_gate])
    flow_rows = Flow(lax.all_gather(own_rows[None], "shard", axis=0, tiled=True), last)
    finish(net, [flow_qkv, flow_gate], 2)
    finish(net, [flow_gate], 1)
    flows = [flow_qkv, flow_gate]
    got, _ = net.launch(flows)
    land(flows[:1], got[:1])
    core_got, _ = net.launch(flows[:1])
    land(flows[1:], got[1:])
    half = flow_gate.value.shape[2] // 2
    flow_left = Flow(
        flow_gate.value[:, :, :half], doubles(path_left[len(along) - 1 :]) + last
    )
    flow_right = Flow(
        flow_gate.value[:, :, half:], doubles(path_right[len(along) - 1 :]) + last
    )
    place = places(along[::-1], [])
    place_left = places(path_left[::-1], [2])
    place_right = places(path_right[::-1], [2])

    packed = jnp.take(flow_qkv.value[:, rows_qkv], place, axis=0)
    gains, at = [], 0
    for scale in scales:
        size = scale.shape[0]
        gains.append(packed[:, at : at + size].astype(F32).reshape(1, size * shards))
        at += -(-size // 128) * 128
    gai, gao, gmi, gmo, gq, gk = gains

    def is_direct(rows):
        return rows % 16 == 0

    first_core = core.reshape(1)

    def weight(shape, flows):
        parts = max(1, flows[0][0].value.shape[0] // shards)
        rows = shape[0] // shards
        count = shape[1] // 2 // parts
        if is_direct(rows):
            pieces, first = [], 0
            for flow, at in flows:
                size = flow.value.shape[2]
                cuts = [
                    ((t * rows, rows, 0), (p * count + first, size, shape[1] // 2))
                    for p in range(parts)
                    for t in range(shards)
                ]
                pieces.append((at, cuts, flow.value, flow.got))
                first += size
            return Weight(shape, core=first_core, pieces=pieces)
        halves = []
        for which in ("value", "got"):
            laid = [
                jnp.take(getattr(flow, which)[:, :rows], at, axis=0).reshape(
                    parts, shards, rows, -1
                )
                for flow, at in flows
            ]
            laid = jnp.concatenate(laid, axis=3).transpose(1, 2, 0, 3)
            halves.append(laid.reshape(shape[0], shape[1] // 2))
        first = core == 0
        matrix = jnp.concatenate(
            [jnp.where(first, *halves), jnp.where(first, *halves[::-1])], axis=1
        )
        return Weight(shape, matrix, [(0, 0, shape[0])])

    def weight_rows(shape, flow, first, rows):
        if is_direct(first) and is_direct(rows):
            cuts = [((2 * t * rows, rows, rows), (0, shape[1], 0)) for t in range(shards)]
            order = jnp.arange(shards, dtype=jnp.int32)
            return Weight(
                shape,
                core=first_core,
                pieces=[(order, cuts, flow.value, flow.got)],
                source=first,
            )
        both = [value[:, first : first + rows] for value in (flow.value, flow.got)]
        matrix = jnp.stack(
            [jnp.where(core == 0, *both), jnp.where(core == 0, *both[::-1])], axis=1
        )
        return Weight(shape, matrix.reshape(shape), [(0, 0, shape[0])])

    class Grad:
        def __init__(self, shape_a, shape_b, left):
            self.shapes = shape_a, shape_b
            self.rows = rows = width // shards
            self.cols = ca, cb = shape_a[1] // 4, shape_b[1] // 4
            self.size = size = shape_b[1] // shards
            self.left = left
            first, second, others = up_along[0], up_along[1], up_along[2:]
            self.others = others
            self.ways = [[first, over_side, second] + others]
            if left < ca + cb:
                self.ways.insert(0, [over_side, second, first] + others)
            self.places = jnp.stack([places(ways, [2]) for ways in self.ways])
            self.direct = is_direct(rows)
            self.cuts = []
            if self.direct:
                for p in range(2):
                    for t in range(shards):
                        n = p * shards + t
                        edges = (0, left, ca) if left < ca else (0, ca)
                        for which, (low, high) in enumerate(zip(edges, edges[1:])):
                            cut = (t * rows, rows, 0), (p * ca + low, high - low, shape_a[1] // 2)
                            self.cuts.append((0, cut, which, n, low))
                        for j in range(cb // size):
                            high = (p * cb // size + j) * rows
                            cut = (high, rows, width // 2), (t * size, size, 0)
                            self.cuts.append((1, cut, len(self.ways) - 1, n, ca + j * size))
                self.outs = [(typed((2 * shards, rows, ca + cb), BF16), ANY)] * 2
            else:
                self.outs = [(typed(shape, BF16), ANY) for shape in self.shapes]
            self.sems = pltpu.SemaphoreType.DMA((max(2, 2 * len(self.cuts)),))

        def flow(self, near, far):
            if not self.direct:
                a, b = near, far
                a = a.reshape(shards, self.rows, 2, 2, self.cols[0]).transpose(2, 3, 0, 1, 4)
                b = b.reshape(2, 2, shards // 4, self.rows, shards, self.size)
                b = b.transpose(0, 1, 4, 3, 2, 5).reshape(a.shape[:4] + (self.cols[1],))
                both = jnp.concatenate([a, b], axis=4)
                both = jnp.where(core == 0, both, both[::-1])
                both = both.reshape((2, 2 * shards) + both.shape[3:])
                sides = []
                for n, ways in enumerate(self.ways):
                    order = jnp.zeros_like(self.places[n]).at[self.places[n]].set(
                        jnp.arange(2 * shards, dtype=jnp.int32)
                    )
                    sides.append(jnp.take(both, order, axis=1))
                if len(sides) == 2:
                    sides = [sides[0][..., : self.left], sides[1][..., self.left :]]
                near, far = jnp.concatenate(sides, axis=3)
            steps = [("halve", over_core)]
            if len(self.ways) == 1:
                steps += [("halve", way) for way in self.ways[0]] + self.ends()
            return Flow((near, far), steps)

        def ends(self):
            if self.direct:
                return [("double", over_side), ("swap", over_core)]
            return [("stack", over_side), ("stack", over_core)]

        def parts(self, flow):
            made, edges = [], [0, self.left, sum(self.cols)]
            for n, ways in enumerate(self.ways):
                value = flow.value[:, :, edges[n] : edges[n + 1]]
                half = value.shape[0] // 2
                made.append(
                    Flow((value[:half], value[half:]), [("halve", way) for way in ways[:3]])
                )
            return made

        def rest(self, made):
            value = jnp.concatenate([flow.value for flow in made], axis=2)
            half = value.shape[0] // 2
            steps = [("halve", way) for way in self.others] + self.ends()
            return Flow((value[:half], value[half:]), steps)

        def shares(self, widths, value, got=None):
            ca, cb = self.cols
            if not self.direct:
                value = value[:, :, 0].astype(F32)
                a = value[..., :ca].transpose(2, 0, 1, 3).reshape(self.rows, 4 * ca)
                b = value[..., ca:].reshape(2, 2, self.rows, cb // self.size, self.size)
                b = b.transpose(0, 1, 3, 2, 4).reshape(width, self.size)
                edges = [sum(widths[:n]) for n in range(len(widths) + 1)]
                return [a[:, low:high] for low, high in zip(edges, edges[1:])] + [b.T]
            outs = [(typed((self.rows, count), F32), VMEM) for count in widths]
            outs.append((typed((self.size, width), F32), VMEM))
            return kernel_of(
                functools.partial(shares_kernel, widths, ca),
                "shares",
                [SMEM] + [VMEM] * 2,
                outs,
                [pltpu.VMEM((width, self.size), F32)],
                0,
            )(jnp.stack([core, side]), value, got)

    up_along = [("shard", bit) for bit in net.shard_bits]
    grad_mlp = Grad(shape_gate, (width, ff), (2 * ff + ff) // 8)
    grad_attn = Grad(shape_qkv, (width, heads * hd), (qkv + heads * hd) // 4)

    in_v = lambda count: [VMEM] * count
    in_s = lambda count: [SMEM] * count
    out_v = lambda *types: [(typed(*one), VMEM) for one in types]
    sems = lambda count: pltpu.SemaphoreType.DMA((count,))
    reach = min(length, WINDOW + QB)
    bf = lambda *shape: (shape, BF16)
    f32 = lambda *shape: (shape, F32)

    seg_rows = segment_ids.reshape(length, 1)
    seg_cols = segment_ids.reshape(1, length)
    flows = [flow_left, flow_right]
    got, _ = net.launch(flows)
    land([flow_qkv], core_got)
    weight_qkv = weight(shape_qkv, [(flow_qkv, place)])
    steps = (length // QB,)
    outs = land(
        flows,
        got,
        kernel_of(
            functools.partial(project_kernel, weight_qkv, heads),
            "project",
            weight_qkv.specs
            + [by_rows(width), by_rows(hd // 2), by_rows(hd // 2)]
            + [all_of(1, width), all_of(1, hd), all_of(1, hd)],
            [
                (typed((length, width), BF16), by_rows(width)),
                (typed((length, heads * hd), BF16), by_rows(heads * hd)),
                (typed((length, hd), BF16), by_rows(hd)),
                (typed((length, hd), BF16), by_rows(hd)),
                (
                    typed((heads, length, hd), BF16),
                    pl.BlockSpec((heads, QB, hd), lambda i: (0, i, 0)),
                ),
                (typed((length, hd), BF16), by_rows(hd)),
            ],
            weight_qkv.scratch,
            2 * length * width * qkv,
            grid=steps,
        )(*weight_qkv.operands, inputs, cos, sin, gai, gq, gk),
    )
    normed, qraw, kraw, values, queries, keys = outs
    flows = [flow_left, flow_right]
    got, args = net.launch(flows, [seg_rows, seg_cols, queries, keys, values])
    small = [gao, gmi, gmo, place_left, place_right, grad_mlp.places]
    small, args = lax.optimization_barrier((small, args))
    gao, gmi, gmo, place_left, place_right, grad_mlp.places = small
    probs, mixed = land(
        flows,
        got,
        kernel_of(
            attend_kernel,
            "attend",
            in_v(5),
            [(typed((heads, length, reach), BF16), ANY)] + out_v(bf(length, heads * hd)),
            [pltpu.VMEM((heads, length, reach), BF16), sems(length // QB)],
            4 * length * heads * hd * reach,
        )(*args),
    )

    finish(net, [flow_left, flow_right, flow_rows])
    high, low = w_out.shape[0] // 2, w_down.shape[0] // 2
    weight_out = weight_rows(shape_out, flow_rows, 0, high)
    weight_down = weight_rows(shape_down, flow_rows, high, low)
    weight_gate = weight(shape_gate, [(flow_left, place_left), (flow_right, place_right)])
    output, dmiddle, dbranch, ggain_mlp, *ends = kernel_of(
        functools.partial(mlp_kernel, weight_out, weight_down, weight_gate, grad_mlp.cuts),
        "mlp",
        weight_out.specs + weight_down.specs + weight_gate.specs + in_s(2) + in_v(5) + [ANY],
        [
            (typed((length, width), BF16), ANY),
            (typed((length, width), F32), ANY),
            (typed((length, width), BF16), VMEM),
            (typed((3, width), F32), VMEM),
        ]
        + grad_mlp.outs,
        weight_out.scratch
        + weight_down.scratch
        + weight_gate.scratch
        + [
            pltpu.VMEM((length, width), BF16),
            pltpu.VMEM((length, width), BF16),
            pltpu.VMEM((length, width), BF16),
            pltpu.VMEM((length, ff), BF16),
            pltpu.VMEM((length, 2 * ff), BF16),
            pltpu.VMEM((length, width), BF16),
            pltpu.VMEM((width, ff), BF16),
            pltpu.VMEM(shape_gate, BF16),
            pltpu.VMEM((length, width), F32),
            pltpu.VMEM((length, width), BF16),
            sems(3),
            grad_mlp.sems,
        ],
        2 * length * width * (9 * ff + heads * hd),
    )(
        *weight_out.operands, *weight_down.operands, *weight_gate.operands, first_core, grad_mlp.places,
        mixed, inputs, gao, gmi, gmo, out_grad,
    )
    back_mlp = grad_mlp.flow(*ends)
    dmixed, gout = advance(
        net,
        [back_mlp],
        kernel_of(
            functools.partial(out_bwd_kernel, weight_out, heads),
            "out_bwd",
            weight_out.specs + in_v(2),
            out_v(bf(heads, length, hd), bf(width, heads * hd)),
            weight_out.scratch,
            4 * length * heads * hd * width,
        ),
        [*weight_out.operands, dbranch, mixed],
    )
    back_mlp = grad_mlp.parts(back_mlp)
    draw, ggain_qk, *ends = advance(
        net,
        back_mlp,
        kernel_of(
            functools.partial(attn_bwd_kernel, grad_attn.cuts),
            "attn_bwd",
            in_s(2) + in_v(8) + [ANY] * 5,
            out_v(bf(length, qkv), f32(2, hd)) + grad_attn.outs,
            [
                pltpu.VMEM((heads, length, reach), BF16),
                sems(length // QB),
                pltpu.VMEM((heads, QB, reach), BF16),
                pltpu.VMEM((length, heads * hd), F32),
                pltpu.VMEM((hd, length), F32),
                pltpu.VMEM((hd, length), F32),
                pltpu.VMEM(shape_qkv, BF16),
                grad_attn.sems,
                pltpu.VMEM((length, heads * hd), BF16),
                pltpu.VMEM((length, hd), BF16),
                pltpu.VMEM((length, width), BF16),
                pltpu.VMEM((width, heads * hd), BF16),
                sems(4),
            ],
            2 * length * (width * qkv + 4 * heads * hd * reach),
        ),
        [
            first_core, grad_attn.places, dmixed, queries, keys, values, cos, sin, gq, gk, qraw,
            kraw, normed, gout, probs,
        ],
    )
    back_attn = grad_attn.flow(*ends)
    flows = [back_attn, *back_mlp]
    got, (draw,) = net.launch(flows, [draw])
    land(flows[:1], got[:1])
    more, (draw,) = net.launch([back_attn], [draw])
    input_grad, ggain_in = land(
        [*back_mlp, back_attn],
        got[1:] + more,
        kernel_of(
            functools.partial(input_bwd_kernel, weight_qkv),
            "input_bwd",
            weight_qkv.specs + [by_rows(qkv), by_rows(width), by_rows(width), all_of(1, width)],
            [
                (typed((length, width), F32), by_rows(width)),
                (typed((1, width), F32), all_of(1, width)),
            ],
            weight_qkv.scratch,
            2 * length * width * qkv,
            grid=steps,
        )(*weight_qkv.operands, draw, dmiddle, inputs, gai),
    )
    sums = jnp.concatenate(
        [ggain_in, ggain_mlp[2:3], ggain_mlp[1:2], ggain_mlp[0:1], ggain_qk[0:1], ggain_qk[1:2]],
        axis=1,
    )
    sums = Flow(sums.reshape(-1, 128), [("total", way) for way in [over_core, over_side] + along])
    advance(net, [*back_mlp, back_attn, sums])
    back_mlp = grad_mlp.rest(back_mlp)
    while back_mlp.steps:
        advance(net, [back_mlp, back_attn, sums])
    finish(net, [back_attn, sums], 1)
    full_gate, full_up, full_down = advance(
        net,
        [back_attn, sums],
        functools.partial(grad_mlp.shares, (ff, ff)),
        [back_mlp.value] + ([back_mlp.got] if grad_mlp.direct else []),
    )
    full_query, full_key, full_value, full_out = grad_attn.shares(
        (heads * hd, hd, hd), back_attn.value, getattr(back_attn, "got", None)
    )
    sums = sums.value.reshape(-1)

    shard = lax.axis_index("shard")
    grads, at = [], 0
    for scale in scales:
        size = scale.shape[0]
        grads.append(lax.dynamic_slice_in_dim(sums, at + shard * size, size, 0))
        at += size * shards
    return (
        output,
        input_grad,
        full_query,
        full_key,
        full_value,
        full_out,
        full_gate,
        full_up,
        full_down,
        grads[0],
        grads[4],
        grads[5],
        grads[1],
        grads[2],
        grads[3],
    )


def solution(mesh):
    rows, vector = P("shard", None), P("shard")
    tokens = P(AXES, None)
    return jax.shard_map(
        functools.partial(layer, Net(mesh)),
        mesh=mesh,
        in_specs=(tokens, P(AXES), tokens) + (rows,) * 7 + (vector,) * 6,
        out_specs=(tokens, tokens) + (rows,) * 7 + (vector,) * 6,
        check_vma=False,
    )
```
